32 devices in a mesh: dp: 8 (over y, x, core), seq: 4 (over z).
Axes of the slice: x: 2, y: 2, z: 4, core: 2. Of those that a mesh axis runs over, the one named last changes fastest.
Arguments:
- tokens: bfloat16 [16, 1024, 1024], P('dp', 'seq'), may hold values from -6 to 6
- cotangent: bfloat16 [16, 1024, 1024], P('dp', 'seq'), may hold values from -6 to 6
- lengths: int32 [16, 4], P('dp'), may hold values from 1 to 1021, as said below
- owners: int32 [192], replicated, may hold values from 0 to 7, as said below
- masters: float32 [256, 131072], P('dp', 'seq'), may hold values from -0.75 to 0.75
- first_moment: float32 [256, 131072], P('dp', 'seq'), may hold values from -320 to 320
- second_moment: float32 [256, 131072], P('dp', 'seq'), may hold values from 204.8 to 819.2
- small_params: float32 [14336], P(('dp', 'seq')), may hold values from -0.8 to 1.4
- small_first: float32 [14336], P(('dp', 'seq')), may hold values from -640 to 640
- small_second: float32 [14336], P(('dp', 'seq')), may hold values from 819.2 to 3276.8
Outputs:
- outputs: bfloat16 [16, 1024, 1024], P('dp', 'seq')
- grad_in: bfloat16 [16, 1024, 1024], P('dp', 'seq')
- new_masters: float32 [256, 131072], P('dp', 'seq')
- new_first: float32 [256, 131072], P('dp', 'seq')
- new_second: float32 [256, 131072], P('dp', 'seq')
- new_low: bfloat16 [256, 131072], P('dp', 'seq')
- small_new: float32 [14336], P(('dp', 'seq'))
- small_first_new: float32 [14336], P(('dp', 'seq'))
- small_second_new: float32 [14336], P(('dp', 'seq'))
The draws below stay inside these ranges and needn't reach their ends.
Inputs may be any that keep to these rules, and one draw needn't show every extreme that they name: Each row's 4 lengths sum to 1024; all but one, at a place drawn per row, are at most 64; in some row all those others are 1. `owners`: no index owns more than 32 blocks, and some index owns exactly 32.
All inputs are finite; a program needn't handle non-finite values.
Results may differ from the reference program's by a relative error of at most 0.018.
Values may be sent and summed in bfloat16 or wider, within the bound.
No kernel may reach another device: no remote copies, remote signals or barrier semaphores. Data moves between devices by JAX's collectives and lax.ppermute only.
A program may use at most 512 MiB of HBM per device.

```python
import math
import jax
import jax.numpy as jnp
from jax import lax

D = 1024
HEADS = 16
HD = 64
ROT = 32
FF = 4096
LAYERS = 2
LEN = 1024
NPROT = 4
STEP = 10
UNIT = 131072
ROWS = 16
SHORT = 64
NU = 192
CAP = 32
SMALLP = 14336
N_DP = 8


def owner_draw(key):
    key = jax.random.fold_in(key, 11)
    first_key, second_key, third_key = jax.random.split(key, 3)
    slot_count = N_DP * CAP
    slot_ids = jnp.arange(slot_count, dtype=jnp.int32)
    score = jax.random.permutation(first_key, slot_count).astype(jnp.int32)
    favored = jax.random.randint(second_key, (), 0, N_DP, dtype=jnp.int32)
    score = score + jnp.where(slot_ids // CAP == favored, slot_count, 0).astype(jnp.int32)
    chosen = lax.top_k(score, NU)[1].astype(jnp.int32)
    chosen = jax.random.permutation(third_key, chosen)
    return (chosen // CAP).astype(jnp.int32)


def draw_owners(key, part):
    return owner_draw(key)


def draw_masters(key, part):
    owners = owner_draw(key)
    key = jax.random.fold_in(key, 5)
    block_index = jnp.arange(NU, dtype=jnp.int32)
    same_owner = owners[:, None] == owners[None, :]
    earlier = block_index[None, :] < block_index[:, None]
    slot_rank = jnp.sum((same_owner & earlier).astype(jnp.int32), axis=1)
    slot_of_block = owners * CAP + slot_rank
    hit = slot_of_block[None, :] == jnp.arange(N_DP * CAP, dtype=jnp.int32)[:, None]
    block_of_slot = jnp.sum(jnp.where(hit, block_index[None, :], 0), axis=1) + jnp.where(jnp.any(hit, axis=1), 0, NU)
    per_layer = (4 * D * D + 2 * D * FF) // UNIT
    inner_start = block_of_slot % per_layer * UNIT
    spread = jnp.where(inner_start < 3 * D * D, D ** (-0.5), jnp.where(inner_start < 4 * D * D, 6.0 * D ** (-0.5), jnp.where(inner_start < 4 * D * D + D * FF, D ** (-0.5), FF ** (-0.5))))
    noise = jax.random.truncated_normal(key, -4.0, 4.0, (N_DP * CAP, UNIT), jnp.float32)
    return (noise * spread[:, None]).astype(jnp.float32)


def draw_lengths(key, part):
    key = jax.random.fold_in(key, 3)
    first_key, second_key, third_key = jax.random.split(key, 3)
    shorts = jax.random.randint(first_key, (ROWS, NPROT), 1, SHORT + 1, dtype=jnp.int32)
    longest = jax.random.randint(second_key, (ROWS, 1), 0, NPROT, dtype=jnp.int32)
    single_row = jax.random.randint(third_key, (), 0, ROWS, dtype=jnp.int32)
    row_ids = jnp.arange(ROWS, dtype=jnp.int32)[:, None]
    shorts = jnp.where(row_ids == single_row, 1, shorts).astype(jnp.int32)
    picked = jnp.arange(NPROT, dtype=jnp.int32)[None, :] == longest
    others = jnp.sum(jnp.where(picked, 0, shorts), axis=1, keepdims=True)
    return jnp.where(picked, LEN - others, shorts).astype(jnp.int32)


def draw_small_params(key, part):
    key = jax.random.fold_in(key, 9)
    within = jnp.arange(SMALLP, dtype=jnp.int32) % (3 * D + FF)
    noise = jax.random.truncated_normal(key, -4.0, 4.0, (SMALLP,), jnp.float32)
    return jnp.where(within < D, 1.0 + 0.1 * noise, 0.2 * noise).astype(jnp.float32)


def steps_of(own_key, shape, cuts, smallest, top_value):
    loudness = 1.0
    for position, blocks in cuts:
        draws = jax.random.uniform(jax.random.fold_in(jax.random.fold_in(own_key, 6), position), (blocks,), jnp.float32, smallest / len(cuts), top_value / len(cuts))
        loudness = loudness * jnp.repeat(jnp.exp(draws), shape[position] // blocks).reshape((-1,) + (1,) * (len(shape) - 1 - position))
    return loudness


def centred(own_key, extent, scale, most, shards=(), held_as=jnp.bfloat16):
    entries = jax.random.normal(own_key, extent, jnp.float32) * scale
    if len(shards) > 0:
        entries = steps_of(own_key, extent, shards, -0.22, 0.18) * entries
    return jnp.clip(entries, min=-most, max=most).astype(held_as)


def setup_inputs(seed: int = 0) -> dict:
    seeds = jax.random.split(jax.random.key(seed), 11)
    return {
        "tokens": centred(seeds[0], (ROWS, LEN, D), 1.0, 6.0, ((0, 8), (1, 4))),
        "cotangent": centred(seeds[1], (ROWS, LEN, D), 1.0, 6.0, ((0, 8), (1, 4))),
        "lengths": draw_lengths(jax.random.fold_in(seeds[10], 71), 0),
        "owners": draw_owners(jax.random.fold_in(seeds[10], 71), 0),
        "masters": draw_masters(jax.random.fold_in(seeds[10], 71), 0),
        "first_moment": centred(seeds[5], (N_DP * CAP, UNIT), (0.39 * (ROWS * LEN) ** 0.5), 320.0, ((0, 8), (1, 4)), jnp.float32),
        "second_moment": jnp.clip(jnp.exp(math.log(819.2) - 1.3862944 * jax.random.uniform(seeds[6], (N_DP * CAP, UNIT), jnp.float32) ** steps_of(seeds[6], (N_DP * CAP, UNIT), ((0, 8), (1, 4)), -0.2, 0.2)), 204.8, 819.2),
        "small_params": draw_small_params(jax.random.fold_in(seeds[10], 71), 0),
        "small_first": centred(seeds[8], (SMALLP,), (0.78 * (ROWS * LEN) ** 0.5), 640.0, ((0, 32),), jnp.float32),
        "small_second": jnp.clip(jnp.exp(math.log(3276.8) - 1.3862944 * jax.random.uniform(seeds[9], (SMALLP,), jnp.float32) ** steps_of(seeds[9], (SMALLP,), ((0, 32),), -0.2, 0.2)), 819.2, 3276.8),
    }


norm_epsilon = 1e-05
gelu_coeff = 0.7978845608
gelu_cubic = 0.044715
beta_first = 0.9
beta_second = 0.999
learn_rate = 0.05
small_rate = 0.3
decay_rate = 0.1
adam_epsilon = 1e-08
HIGHEST = lax.Precision.HIGHEST

@jax.custom_vjp
def low(v):
    return lax.optimization_barrier(v.astype(jnp.bfloat16)).astype(jnp.float32)

@jax.custom_vjp
def low_back(v):
    return v

def low_keep(v):
    return (low(v), None)

def low_pass(kept, grad):
    return (grad,)

def back_keep(v):
    return (v, None)

def back_low(kept, grad):
    return (low(grad),)
low.defvjp(low_keep, low_pass)
low_back.defvjp(back_keep, back_low)

def matmul(left, right):
    return jnp.dot(left, right, precision=HIGHEST, preferred_element_type=jnp.float32)

def gelu_tanh(values):
    return 0.5 * values * (1.0 + jnp.tanh(gelu_coeff * (values + gelu_cubic * values * values * values)))

def token_tables(lengths, length):
    ends = jnp.cumsum(lengths, axis=1)
    starts = ends - lengths
    places = jnp.arange(length, dtype=jnp.int32)
    segment = lax.optimization_barrier(jnp.sum((places[None, :, None] >= ends[:, None, :]).astype(jnp.int32), axis=2))
    owner_hit = segment[:, :, None] == jnp.arange(lengths.shape[1], dtype=jnp.int32)[None, None, :]
    first = lax.optimization_barrier(jnp.sum(jnp.where(owner_hit, starts[:, None, :], 0), axis=2))
    return (segment, places[None, :] - first)

def angle_tables(within):
    inverse = 1.0 / 10000.0 ** (jnp.arange(0, ROT, 2, dtype=jnp.float32) / ROT)
    angle = within.astype(jnp.float32)[..., None] * inverse
    return (jnp.cos(angle), jnp.sin(angle))

def rotate(projected, cosines, sines):
    half = ROT // 2
    pair = projected[:, :, :2]
    first = pair[..., :half]
    second = pair[..., half:ROT]
    cos_b = cosines[:, :, None, None, :]
    sin_b = sines[:, :, None, None, :]
    turned = jnp.concatenate([first * cos_b - second * sin_b, second * cos_b + first * sin_b, pair[..., ROT:]], axis=-1)
    return jnp.concatenate([turned, projected[:, :, 2:]], axis=2)

def layer_norm_parts(state):
    centered = state - lax.optimization_barrier(jnp.mean(state, axis=-1, keepdims=True))
    inv_std = lax.rsqrt(lax.optimization_barrier(jnp.mean(centered * centered, axis=-1, keepdims=True)) + norm_epsilon)
    return centered * inv_std

def row_attention(packed):
    queries, key_rows, value_rows, segment_row = packed
    scores = low_back(jnp.einsum('qhd,khd->hqk', queries, key_rows, precision=HIGHEST) * HD ** (-0.5))
    places = jnp.arange(segment_row.shape[0])
    allowed = (places[None, :] <= places[:, None]) & (segment_row[:, None] == segment_row[None, :])
    scores = jnp.where(allowed[None], scores, -1e+30)
    shifted = jnp.exp(scores - lax.optimization_barrier(jnp.max(scores, axis=-1, keepdims=True)))
    weights_p = low(shifted / lax.optimization_barrier(jnp.sum(shifted, axis=-1, keepdims=True)))
    context = jnp.einsum('hqk,khd->qhd', weights_p, value_rows, precision=HIGHEST)
    return context.reshape(segment_row.shape[0], D)

def unpack(flat, small, layer):
    per_layer = 4 * D * D + 2 * D * FF
    start = layer * per_layer
    w_qkv = flat[start:start + 3 * D * D].reshape(D, 3 * D)
    start = start + 3 * D * D
    w_out = flat[start:start + D * D].reshape(D, D)
    start = start + D * D
    w_in = flat[start:start + D * FF].reshape(D, FF)
    start = start + D * FF
    w_down = flat[start:start + D * FF].reshape(FF, D)
    base = layer * (3 * D + FF)
    gain = small[base:base + D]
    shift = small[base + D:base + 2 * D]
    bias_in = small[base + 2 * D:base + 2 * D + FF]
    bias_out = small[base + 2 * D + FF:base + 3 * D + FF]
    return (w_qkv, w_out, w_in, w_down, gain, shift, bias_in, bias_out)

def block_forward(state, weights, segment, cosines, sines):
    w_qkv, w_out, w_in, w_down, gain, shift, bias_in, bias_out = weights
    group = state.shape[0]
    hidden = low(layer_norm_parts(state) * gain + shift)
    projected = low_back(matmul(hidden, w_qkv)).reshape(group, LEN, 3, HEADS, HD)
    rotated = low_back(low(rotate(projected, cosines, sines)))
    context = lax.map(jax.checkpoint(row_attention), (rotated[:, :, 0], rotated[:, :, 1], rotated[:, :, 2], segment))
    context = low_back(low(context))
    attended = low_back(matmul(context, w_out))
    inner = low_back(matmul(hidden, w_in) + bias_in)
    activated = low(gelu_tanh(inner))
    branch = low_back(matmul(activated, w_down) + bias_out)
    return state + attended + branch

def forward(flat, small, state, segment, cosines, sines):
    for layer in range(LAYERS):
        state = block_forward(state, unpack(flat, small, layer), segment, cosines, sines)
    return state

def adam_update(weights, grads, moment_one, moment_two, rate, decay):
    new_one = beta_first * moment_one + (1.0 - beta_first) * grads
    new_two = beta_second * moment_two + (1.0 - beta_second) * grads * grads
    corrected_one = new_one / (1.0 - beta_first ** STEP)
    corrected_two = new_two / (1.0 - beta_second ** STEP)
    new_weights = weights - rate * (corrected_one / (jnp.sqrt(corrected_two) + adam_epsilon) + decay * weights)
    return (new_weights, new_one, new_two)

def reference(tokens, cotangent, lengths, owners, masters, first_moment, second_moment, small_params, small_first, small_second):
    block_index = jnp.arange(NU, dtype=jnp.int32)
    same_owner = owners[:, None] == owners[None, :]
    earlier = block_index[None, :] < block_index[:, None]
    slot_rank = lax.optimization_barrier(jnp.sum((same_owner & earlier).astype(jnp.int32), axis=1))
    slot_of_block = owners * CAP + slot_rank
    rounded = lax.optimization_barrier(masters.astype(jnp.bfloat16)).astype(jnp.float32)
    flat = rounded[slot_of_block].reshape(-1)
    small_round = lax.optimization_barrier(small_params.astype(jnp.bfloat16)).astype(jnp.float32)
    segment, within = token_tables(lengths, LEN)
    cosines, sines = angle_tables(within)
    groups = ROWS // 4
    inputs = (tokens.astype(jnp.float32).reshape(groups, 4, LEN, D), cotangent.astype(jnp.float32).reshape(groups, 4, LEN, D), segment.reshape(groups, 4, LEN), cosines.reshape(groups, 4, LEN, ROT // 2), sines.reshape(groups, 4, LEN, ROT // 2))

    def scan_step(carry, batch):
        x_group, cot_group, seg_group, cos_group, sin_group = batch

        def run(flat_in, small_in, x_in):
            return forward(flat_in, small_in, x_in, seg_group, cos_group, sin_group)
        result, pullback = jax.vjp(run, flat, small_round, x_group)
        grad_flat, grad_small, grad_x = pullback(cot_group)
        return ((carry[0] + grad_flat, carry[1] + grad_small), (result.astype(jnp.bfloat16), grad_x.astype(jnp.bfloat16)))
    start_carry = (jnp.zeros((NU * UNIT,), jnp.float32), jnp.zeros((SMALLP,), jnp.float32))
    (grad_flat, grad_small), (outputs, grad_in) = lax.scan(scan_step, start_carry, inputs)
    slot_ids = jnp.arange(N_DP * CAP, dtype=jnp.int32)
    hit = slot_of_block[None, :] == slot_ids[:, None]
    block_of_slot = lax.optimization_barrier(jnp.sum(jnp.where(hit, block_index[None, :], 0), axis=1)) + jnp.where(jnp.any(hit, axis=1), 0, NU)
    padded = jnp.concatenate([grad_flat.reshape(NU, UNIT), jnp.zeros((1, UNIT), jnp.float32)], axis=0)
    grad_rows = padded[block_of_slot]
    new_masters, new_first, new_second = adam_update(masters, grad_rows, first_moment, second_moment, learn_rate, decay_rate)
    small_new, small_first_new, small_second_new = adam_update(small_params, grad_small, small_first, small_second, small_rate, 0.0)
    return (outputs.reshape(ROWS, LEN, D), grad_in.reshape(ROWS, LEN, D), new_masters, new_first, new_second, new_masters.astype(jnp.bfloat16), small_new, small_first_new, small_second_new)
```

```python
import functools

import jax
import jax.numpy as jnp
import numpy as np
from jax import lax
from jax.experimental import pallas as pl
from jax.experimental.pallas import tpu as pltpu
from jax.sharding import PartitionSpec as P

HEADS = 16
HD = 64
ROT = 32
FF = 4096
LAYERS = 2
STEP = 10
TP = 4

norm_epsilon = 1e-05
gelu_coeff = 0.7978845608
gelu_cubic = 0.044715
beta_first = 0.9
beta_second = 0.999
learn_rate = 0.05
small_rate = 0.3
decay_rate = 0.1
adam_epsilon = 1e-08
BIG = 1e30
BF = jnp.bfloat16
F32 = jnp.float32


def gelu_tanh(values):
    return (
        0.5
        * values
        * (1.0 + jnp.tanh(gelu_coeff * (values + gelu_cubic * values * values * values)))
    )


def gelu_slope(values):
    tanh_part = jnp.tanh(gelu_coeff * (values + gelu_cubic * values * values * values))
    return 0.5 * (1.0 + tanh_part) + 0.5 * values * (1.0 - tanh_part * tanh_part) * gelu_coeff * (
        1.0 + 3.0 * gelu_cubic * values * values
    )


def dot(left, right):
    return jnp.dot(left, right, preferred_element_type=F32)


def dot_nt(left, right):
    return lax.dot_general(left, right, (((1,), (1,)), ((), ())), preferred_element_type=F32)


def dot_tn(left, right):
    return lax.dot_general(left, right, (((0,), (0,)), ((), ())), preferred_element_type=F32)


def rotate_lanes(x, cos_t, low_t, high_t, sign):
    halves = []
    for part in range(x.shape[1] // 128):
        v = x[:, 128 * part : 128 * (part + 1)]
        up = pltpu.roll(v, 128 - ROT // 2, 1)
        down = pltpu.roll(v, ROT // 2, 1)
        halves.append(v * cos_t + sign * (up * low_t + down * high_t))
    return jnp.concatenate(halves, axis=1)


def head_of(shape):
    return lax.broadcasted_iota(jnp.int32, shape, 1) // HD


def attend_kernel(proj_ref, tab_ref, qx_ref, kx_ref, ctx_ref, rot_ref, lse_ref, k_s, v_s, q_s):
    length, width = ctx_ref.shape
    heads = width // HD
    blk = min(256, length)
    cos_t, low_t, high_t = tab_ref[0], tab_ref[1], tab_ref[2]
    q = rotate_lanes(proj_ref[:, :width], cos_t, low_t, high_t, 1.0).astype(BF)
    k = rotate_lanes(proj_ref[:, width : 2 * width], cos_t, low_t, high_t, 1.0).astype(BF)
    v = proj_ref[:, 2 * width :].astype(BF)
    rot_ref[:, :width] = q
    rot_ref[:, width : 2 * width] = k
    rot_ref[:, 2 * width :] = v
    q = q * BF(HD**-0.5)
    head = head_of((length, width))
    zero = jnp.zeros((), BF)
    for h in range(heads):
        ext = (h + 1) % heads
        k_s[h] = jnp.where(head == h, k, jnp.where(head == ext, kx_ref[...], zero))
        v_s[h] = jnp.where(head == h, v, zero)
        q_s[h] = jnp.where(head == ext, qx_ref[...], q)
    tri = lax.broadcasted_iota(jnp.int32, (blk, blk), 0) <= lax.broadcasted_iota(
        jnp.int32, (blk, blk), 1
    )
    for i in range(length // blk):
        lo, hi = i * blk, (i + 1) * blk
        total = jnp.zeros((blk, width), F32)
        for h in range(heads):
            qb = q_s[h, lo:hi]
            diag = jnp.where(tri, dot_nt(k_s[h, lo:hi], qb), -BIG)
            top = jnp.max(diag, axis=0, keepdims=True)
            if i:
                past = dot_nt(k_s[h, :lo], qb)
                top = jnp.maximum(top, jnp.max(past, axis=0, keepdims=True))
            diag = jnp.exp(diag - top)
            mass = jnp.sum(diag, axis=0, keepdims=True)
            if i:
                past = jnp.exp(past - top)
                mass = mass + jnp.sum(past, axis=0, keepdims=True)
            lse_ref[h : h + 1, lo:hi] = top + jnp.log(mass)
            inv = 1.0 / mass
            total += dot_tn((diag * inv).astype(BF), v_s[h, lo:hi])
            if i:
                total += dot_tn((past * inv).astype(BF), v_s[h, :lo])
        ctx_ref[lo:hi] = total.astype(BF)


def attend_back_kernel(
    rot_ref, dctx_ref, lse_ref, tab_ref, qx_ref, kx_ref, out_ref, k_s, v_s, q_s, dk_s, dv_s, dq_s
):
    length, width = dctx_ref.shape
    heads = width // HD
    blk = min(256, length)
    head = head_of((length, width))
    zero = jnp.zeros((), BF)
    q = rot_ref[:, :width]
    k = rot_ref[:, width : 2 * width]
    v = rot_ref[:, 2 * width :]
    scaled = q * BF(HD**-0.5)
    for h in range(heads):
        ext = (h + 1) % heads
        k_s[h] = jnp.where(head == h, k, jnp.where(head == ext, kx_ref[...], zero))
        v_s[h] = jnp.where(head == h, v, zero)
        q_s[h] = jnp.where(head == ext, qx_ref[...], scaled)
    dk_s[...] = jnp.zeros_like(dk_s)
    dv_s[...] = jnp.zeros_like(dv_s)
    head_b = head_of((blk, width))
    tri = lax.broadcasted_iota(jnp.int32, (blk, blk), 0) <= lax.broadcasted_iota(
        jnp.int32, (blk, blk), 1
    )
    for i in range(length // blk):
        lo, hi = i * blk, (i + 1) * blk
        d_all = dctx_ref[lo:hi]
        q_all = rot_ref[lo:hi, :width]
        total = jnp.zeros((blk, width), F32)
        for h in range(heads):
            qb = q_s[h, lo:hi]
            d_h = jnp.where(head_b == h, d_all, zero)
            q_h = jnp.where(head_b == h, q_all, zero)
            lse = lse_ref[h : h + 1, lo:hi]
            p_d = jnp.exp(jnp.where(tri, dot_nt(k_s[h, lo:hi], qb), -BIG) - lse)
            g_d = dot_nt(v_s[h, lo:hi], d_all)
            delta = jnp.sum(p_d * g_d, axis=0, keepdims=True)
            if i:
                p_p = jnp.exp(dot_nt(k_s[h, :lo], qb) - lse)
                g_p = dot_nt(v_s[h, :lo], d_all)
                delta = delta + jnp.sum(p_p * g_p, axis=0, keepdims=True)
            s_d = (p_d * (g_d - delta)).astype(BF)
            dv_s[lo:hi] += dot(p_d.astype(BF), d_h)
            dk_s[lo:hi] += dot(s_d, q_h)
            k_d = jnp.where(head_b == h, rot_ref[lo:hi, width : 2 * width], zero)
            total += dot_tn(s_d, k_d)
            if i:
                s_p = (p_p * (g_p - delta)).astype(BF)
                dv_s[:lo] += dot(p_p.astype(BF), d_h)
                dk_s[:lo] += dot(s_p, q_h)
                k_p = jnp.where(head_of((lo, width)) == h, rot_ref[:lo, width : 2 * width], zero)
                total += dot_tn(s_p, k_p)
        dq_s[lo:hi] = total
    scale = HD**-0.5
    cos_t, low_t, high_t = tab_ref[0], tab_ref[1], tab_ref[2]
    for n, ref in ((0, dq_s), (1, dk_s)):
        low = (ref[...] * scale).astype(BF).astype(F32)
        out_ref[:, n * width : (n + 1) * width] = rotate_lanes(
            low, cos_t, low_t, high_t, -1.0
        ).astype(BF)
    out_ref[:, 2 * width :] = dv_s[...].astype(BF)


def attend(proj, tables, q_ext, k_ext):
    length, width = proj.shape[0], proj.shape[1] // 3
    heads = width // HD
    return pl.pallas_call(
        attend_kernel,
        out_shape=(
            jax.ShapeDtypeStruct((length, width), BF),
            jax.ShapeDtypeStruct((length, 3 * width), BF),
            jax.ShapeDtypeStruct((8, length), F32),
        ),
        scratch_shapes=[pltpu.VMEM((heads, length, width), BF)] * 3,
        compiler_params=pltpu.CompilerParams(vmem_limit_bytes=50 << 20),
        cost_estimate=pl.CostEstimate(
            flops=heads * length * length * width * 2,
            bytes_accessed=length * width * 24,
            transcendentals=heads * length * length // 2,
        ),
        name="attend",
    )(proj, tables, q_ext, k_ext)


def attend_back(rot, d_context, lse, tables, q_ext, k_ext):
    length, width = d_context.shape
    heads = width // HD
    return pl.pallas_call(
        attend_back_kernel,
        out_shape=jax.ShapeDtypeStruct((length, 3 * width), BF),
        scratch_shapes=[pltpu.VMEM((heads, length, width), BF)] * 3
        + [pltpu.VMEM((length, width), F32)] * 3,
        compiler_params=pltpu.CompilerParams(vmem_limit_bytes=50 << 20),
        cost_estimate=pl.CostEstimate(
            flops=heads * length * length * width * 5,
            bytes_accessed=length * width * 24,
            transcendentals=heads * length * length // 2,
        ),
        name="attend_back",
    )(rot, d_context, lse, tables, q_ext, k_ext)


@functools.lru_cache(maxsize=None)
def row_moves(n_seq, rows_here, length):
    local = length // n_seq
    per_dev = rows_here * local
    edges = {}
    for t in range(TP):
        for z in range(n_seq):
            for k in range(rows_here):
                row = rows_here * t + k
                token = (row // n_seq) * length + z * local
                target = (token // per_dev) * n_seq + row % n_seq
                edges.setdefault(t * n_seq + z, []).append((target, k, token % per_dev // local))
    steps = []
    for _ in range(rows_here):
        taken = {}

        def place(source, seen):
            for edge in edges[source]:
                if edge[0] not in seen:
                    seen.add(edge[0])
                    if edge[0] not in taken or place(taken[edge[0]][0], seen):
                        taken[edge[0]] = (source, edge)
                        return True
            return False

        for source in edges:
            assert place(source, set())
        pick = np.zeros(TP * n_seq, np.int32)
        put = np.zeros(TP * n_seq, np.int32)
        pairs = []
        for target, (source, edge) in taken.items():
            edges[source].remove(edge)
            pick[source] = edge[1]
            put[target] = edge[2]
            pairs.append((source, target))
        steps.append((sorted(pairs), pick, put))
    return steps


def adam_update(weights, grads, moment_one, moment_two, rate, decay):
    new_one = beta_first * moment_one + (1.0 - beta_first) * grads
    new_two = beta_second * moment_two + (1.0 - beta_second) * grads * grads
    corrected_one = new_one / (1.0 - beta_first**STEP)
    corrected_two = new_two / (1.0 - beta_second**STEP)
    new_weights = weights - rate * (
        corrected_one / (jnp.sqrt(corrected_two) + adam_epsilon) + decay * weights
    )
    return (new_weights, new_one, new_two)


def body(
    tokens,
    cotangent,
    lengths,
    owners,
    masters,
    first_moment,
    second_moment,
    small_params,
    small_first,
    small_second,
):
    n_dp = lax.axis_size("dp")
    n_seq = lax.axis_size("seq")
    n_g = n_dp // TP
    capacity, piece = masters.shape
    n_blocks = owners.shape[0]
    rows_here, local, width = tokens.shape
    length = local * n_seq
    per_dev = rows_here * local
    group_rows = TP * per_dev // length
    cols = width // TP
    chunks = piece // width // n_g
    place_dp = lax.axis_index("dp")
    place_z = lax.axis_index("seq")
    t = place_dp % TP
    g = place_dp // TP
    core, side = t % 2, t // 2
    groups = [[TP * a + b for b in range(TP)] for a in range(n_g)]
    across = [[TP * a + b for a in range(n_g)] for b in range(TP)]

    def swap(value, bit):
        return lax.ppermute(value, "dp", [(i, i ^ bit) for i in range(n_dp)])

    def order(first, second, flag):
        return jnp.concatenate(
            [jnp.where(flag == 0, first, second), jnp.where(flag == 0, second, first)], axis=0
        )

    steps = row_moves(n_seq, rows_here, length)

    def row_pairs(pairs, back):
        out = []
        for source, target in pairs:
            for a in range(n_g):
                ends = (a * TP * n_seq + source, a * TP * n_seq + target)
                out.append(ends[::-1] if back else ends)
        return out

    me = t * n_seq + place_z

    def to_rows(value):
        parts = []
        for pairs, pick, _ in steps:
            send = lax.dynamic_index_in_dim(value, jnp.asarray(pick)[me], 0, keepdims=False)
            parts.append(lax.ppermute(send, ("dp", "seq"), row_pairs(pairs, False)))
        puts = [jnp.asarray(put)[me] for _, _, put in steps]
        slots = []
        for s in range(rows_here):
            out = parts[0]
            for j in range(1, rows_here):
                out = jnp.where(puts[j] == s, parts[j], out)
            slots.append(out)
        return jnp.concatenate(slots, axis=0)

    def from_rows(value):
        value = value.reshape(rows_here, local, width)
        parts = []
        for pairs, _, put in steps:
            send = lax.dynamic_index_in_dim(value, jnp.asarray(put)[me], 0, keepdims=False)
            parts.append(lax.ppermute(send, ("dp", "seq"), row_pairs(pairs, True)))
        picks = [jnp.asarray(pick)[me] for _, pick, _ in steps]
        slots = []
        for s in range(rows_here):
            out = parts[0]
            for j in range(1, rows_here):
                out = jnp.where(picks[j] == s, parts[j], out)
            slots.append(out)
        return jnp.stack(slots, axis=0)

    block_index = jnp.arange(n_blocks, dtype=jnp.int32)
    same_owner = owners[:, None] == owners[None, :]
    earlier = block_index[None, :] < block_index[:, None]
    slot_rank = jnp.sum((same_owner & earlier).astype(jnp.int32), axis=1)
    slot_of_block = owners * capacity + slot_rank
    slot_ids = jnp.arange(n_dp * capacity, dtype=jnp.int32)
    hit = slot_of_block[None, :] == slot_ids[:, None]
    block_of_slot = jnp.sum(jnp.where(hit, block_index[None, :], 0), axis=1) + jnp.where(
        jnp.any(hit, axis=1), 0, n_blocks
    )

    packed = (
        masters.astype(BF)
        .reshape(capacity, n_g, chunks, TP, cols)
        .transpose(1, 3, 0, 2, 4)
        .reshape(n_dp, capacity, chunks, cols)
    )
    spread = lax.all_to_all(packed, "dp", split_axis=0, concat_axis=0, tiled=True)
    blocks = spread.reshape(n_dp * capacity, chunks, cols)[slot_of_block]

    small_all = lax.all_gather(small_params.astype(BF), ("dp", "seq"), axis=0, tiled=True)

    unit_rows = n_seq * n_g * chunks
    n_qkv = 3 * width // unit_rows
    n_out = width // unit_rows
    n_in = FF // unit_rows
    per_layer = n_qkv + n_out + 2 * n_in
    my_out = n_out // TP
    fold = FF // width

    def gather_blocks(value):
        by_z = lax.all_gather(value, "seq", axis=0)
        if n_g == 2:
            other = swap(by_z, TP)
            both = jnp.stack([jnp.where(g == 0, by_z, other), jnp.where(g == 0, other, by_z)])
        else:
            both = lax.all_gather(by_z, "dp", axis=0, axis_index_groups=across)
        units, rest = value.shape[0], value.shape[2]
        return both.transpose(2, 1, 0, 3, 4).reshape(units * unit_rows, rest)

    weights = []
    for layer in range(LAYERS):
        start = layer * per_layer
        mine = blocks[start : start + per_layer]
        w_qkv = gather_blocks(mine[:n_qkv]).reshape(width, 3 * cols)
        w_in = gather_blocks(mine[n_qkv + n_out : n_qkv + n_out + n_in]).reshape(width, fold * cols)
        outs = mine[n_qkv : n_qkv + n_out].reshape(TP, my_out, chunks, cols)
        downs = (
            mine[n_qkv + n_out + n_in :]
            .reshape(fold, TP, my_out, chunks, cols)
            .transpose(1, 0, 2, 3, 4)
            .reshape(TP, fold * my_out, chunks, cols)
        )
        both = lax.all_to_all(
            jnp.concatenate([outs, downs], axis=1),
            "dp",
            split_axis=0,
            concat_axis=0,
            tiled=True,
            axis_index_groups=groups,
        )
        both = both.transpose(1, 2, 0, 3).reshape((1 + fold) * my_out, chunks, width)
        both = gather_blocks(both)
        w_out, w_down = both[:cols], both[cols:]
        base = layer * (3 * width + FF)
        small_f = small_all[base : base + 3 * width + FF].astype(F32)
        gain = small_f[:width]
        shift = small_f[width : 2 * width]
        bias_in = lax.dynamic_index_in_dim(
            small_f[2 * width : 2 * width + FF].reshape(fold, TP, cols), t, 1, keepdims=False
        ).reshape(-1)
        bias_out = small_f[2 * width + FF :]
        weights.append((w_qkv, w_out, w_in, w_down, gain, shift, bias_in, bias_out))

    near = jnp.stack([lengths, swap(lengths, 1)])
    near = jnp.concatenate([near, swap(near, 2)])
    near = near[jnp.arange(TP) ^ t].reshape(TP * rows_here, -1)
    mine_rows = jnp.arange(group_rows) * n_seq + place_z
    if group_rows == 2:
        mine_rows = jnp.where(side == 0, mine_rows, mine_rows[::-1])
    row_lengths = near[mine_rows]
    ends = jnp.cumsum(row_lengths, axis=1)
    starts = ends - row_lengths
    places = jnp.arange(length, dtype=jnp.int32)
    segment = jnp.sum((places[None, :, None] >= ends[:, None, :]).astype(jnp.int32), axis=2)
    which = segment[:, :, None] == jnp.arange(lengths.shape[1], dtype=jnp.int32)[None, None, :]
    within = places[None, :] - jnp.sum(jnp.where(which, starts[:, None, :], 0), axis=2)
    lane = jnp.arange(128)
    feature = lane % HD
    inverse = 1.0 / 10000.0 ** (jnp.arange(0, ROT, 2, dtype=F32) / ROT)
    angle = within.astype(F32)[..., None] * jnp.tile(inverse, 128 // (ROT // 2))
    cosine, sine = jnp.cos(angle), jnp.sin(angle)
    tables = jnp.stack(
        [
            jnp.where(feature < ROT, cosine, 1.0),
            jnp.where(feature < ROT // 2, -sine, 0.0),
            jnp.where((feature >= ROT // 2) & (feature < ROT), sine, 0.0),
        ],
        axis=1,
    )
    wide = jnp.arange(cols) % HD
    hits = segment[:, :, None] == wide[None, None, :]
    q_ext = jnp.where(hits, 1.0, 0.0).astype(BF)
    k_ext = jnp.where(hits | (wide >= lengths.shape[1])[None, None, :], 0.0, -BIG).astype(BF)

    def gather_group(value):
        own = order(value, swap(value, 1), core)
        other = swap(own, 2)
        if group_rows == 2:
            return [own, other]
        return [order(own, other, side)]

    def scatter_group(parts):
        if group_rows == 2:
            own, other = parts
        else:
            pair = parts[0].reshape(2, 2 * per_dev, width)
            own = lax.dynamic_index_in_dim(pair, side, 0, keepdims=False)
            other = lax.dynamic_index_in_dim(pair, 1 - side, 0, keepdims=False)

        def halve(value):
            value = value.reshape(2, per_dev, width)
            keep = lax.dynamic_index_in_dim(value, core, 0, keepdims=False)
            send = lax.dynamic_index_in_dim(value, 1 - core, 0, keepdims=False)
            return keep + swap(send.astype(BF), 1).astype(F32)

        far = swap(halve(other).astype(BF), 2)
        return halve(own) + far.astype(F32)

    state = to_rows(tokens).astype(F32)
    stored = []
    for layer in range(LAYERS):
        w_qkv, w_out, w_in, w_down, gain, shift, bias_in, bias_out = weights[layer]
        centered = state - jnp.mean(state, axis=-1, keepdims=True)
        inv_std = lax.rsqrt(jnp.mean(centered * centered, axis=-1, keepdims=True) + norm_epsilon)
        normed = centered * inv_std
        hiddens = gather_group((normed * gain + shift).astype(BF))
        kept, parts = [], []
        for r, hidden in enumerate(hiddens):
            context, rot, lse = attend(dot(hidden, w_qkv), tables[r], q_ext[r], k_ext[r])
            inner = dot(hidden, w_in) + bias_in
            activated = gelu_tanh(inner).astype(BF)
            parts.append(dot(context, w_out) + dot(activated, w_down))
            kept.append((hidden, context, rot, lse, inner, activated))
        stored.append((normed, inv_std, kept))
        state = state + scatter_group(parts) + bias_out
    outputs = from_rows(state.astype(BF))

    d_state = to_rows(cotangent).astype(F32)
    big = [None] * LAYERS
    small_grads = [None] * LAYERS

    def reduce_blocks(value, units):
        rest = value.shape[1]
        value = value.astype(BF).reshape(units, n_seq, n_g, chunks, rest).transpose(2, 1, 0, 3, 4)
        if n_g == 2:
            keep = lax.dynamic_index_in_dim(value, g, 0, keepdims=False)
            send = lax.dynamic_index_in_dim(value, 1 - g, 0, keepdims=False)
            value = (keep.astype(F32) + swap(send, TP).astype(F32)).astype(BF)
        else:
            value = lax.psum_scatter(
                value, "dp", scatter_dimension=0, axis_index_groups=across, tiled=False
            )
        return lax.psum_scatter(value, "seq", scatter_dimension=0, tiled=False)

    for layer in reversed(range(LAYERS)):
        w_qkv, w_out, w_in, w_down, gain, shift, bias_in, bias_out = weights[layer]
        normed, inv_std, kept = stored[layer]
        d_branch = d_state.astype(BF)
        g_bias_out = jnp.sum(d_branch.astype(F32), axis=0)
        g_down = g_out = g_in = g_qkv = g_bias_in = 0.0
        parts = []
        for r, d_row in enumerate(gather_group(d_branch)):
            hidden, context, rot, lse, inner, activated = kept[r]
            d_context = dot_nt(d_row, w_out).astype(BF)
            d_projected = attend_back(rot, d_context, lse, tables[r], q_ext[r], k_ext[r])
            d_inner = (dot_nt(d_row, w_down) * gelu_slope(inner)).astype(BF)
            parts.append(dot_nt(d_inner, w_in) + dot_nt(d_projected, w_qkv))
            g_down += dot_tn(activated, d_row)
            g_out += dot_tn(context, d_row)
            g_in += dot_tn(hidden, d_inner)
            g_qkv += dot_tn(hidden, d_projected)
            g_bias_in += jnp.sum(d_inner.astype(F32), axis=0)
        d_hidden = scatter_group(parts)
        g_gain = jnp.sum(d_hidden * normed, axis=0)
        g_shift = jnp.sum(d_hidden, axis=0)
        d_normed = d_hidden * gain
        d_state = d_state + inv_std * (
            d_normed
            - jnp.mean(d_normed, axis=-1, keepdims=True)
            - normed * jnp.mean(d_normed * normed, axis=-1, keepdims=True)
        )
        r_qkv = reduce_blocks(g_qkv.reshape(3 * width, cols), n_qkv)
        r_in = reduce_blocks(g_in.reshape(FF, cols), n_in)
        both = reduce_blocks(jnp.concatenate([g_out, g_down]), (1 + fold) * my_out)
        both = both.reshape((1 + fold) * my_out, chunks, TP, cols).transpose(2, 0, 1, 3)
        both = lax.all_to_all(
            both, "dp", split_axis=0, concat_axis=0, tiled=True, axis_index_groups=groups
        )
        r_out = both[:, :my_out].reshape(n_out, chunks, cols)
        r_down = (
            both[:, my_out:]
            .reshape(TP, fold, my_out, chunks, cols)
            .transpose(1, 0, 2, 3, 4)
            .reshape(n_in, chunks, cols)
        )
        big[layer] = jnp.concatenate([r_qkv, r_out, r_in, r_down])
        wide_bias = (
            (jnp.arange(TP) == t).astype(F32)[None, :, None] * g_bias_in.reshape(fold, 1, cols)
        ).reshape(-1)
        small_grads[layer] = jnp.concatenate([g_gain, g_shift, wide_bias, g_bias_out])
    grad_in = from_rows(d_state.astype(BF))

    grads = jnp.concatenate(big + [jnp.zeros((1, chunks, cols), BF)])
    slots = grads[block_of_slot].reshape(n_dp, capacity, chunks, cols)
    owned = lax.all_to_all(slots, "dp", split_axis=0, concat_axis=0, tiled=True)
    owned = (
        owned.reshape(n_g, TP, capacity, chunks, cols)
        .transpose(2, 0, 3, 1, 4)
        .reshape(capacity, piece)
        .astype(F32)
    )
    small_owned = lax.psum_scatter(
        jnp.concatenate(small_grads), ("dp", "seq"), scatter_dimension=0, tiled=True
    )
    new_masters, new_first, new_second = adam_update(
        masters, owned, first_moment, second_moment, learn_rate, decay_rate
    )
    small_new, small_first_new, small_second_new = adam_update(
        small_params, small_owned, small_first, small_second, small_rate, 0.0
    )
    return (
        outputs,
        grad_in,
        new_masters,
        new_first,
        new_second,
        new_masters.astype(BF),
        small_new,
        small_first_new,
        small_second_new,
    )


def solution(mesh):
    placed = (
        P("dp", "seq", None),
        P("dp", "seq", None),
        P("dp", None),
        P(),
        P("dp", "seq"),
        P("dp", "seq"),
        P("dp", "seq"),
        P(("dp", "seq")),
        P(("dp", "seq")),
        P(("dp", "seq")),
    )
    return jax.shard_map(
        body,
        mesh=mesh,
        in_specs=placed,
        out_specs=(
            P("dp", "seq", None),
            P("dp", "seq", None),
            P("dp", "seq"),
            P("dp", "seq"),
            P("dp", "seq"),
            P("dp", "seq"),
            P(("dp", "seq")),
            P(("dp", "seq")),
            P(("dp", "seq")),
        ),
        check_vma=False,
    )
```

```python
import functools

import jax
import jax.numpy as jnp
import numpy as np
from jax import lax
from jax.experimental import pallas as pl
from jax.experimental.pallas import tpu as pltpu
from jax.sharding import Mesh
from jax.sharding import PartitionSpec as P

HEADS = 16
HD = 64
ROT = 32
FF = 4096
LAYERS = 2
STEP = 10
DP = ("g", "x", "core")
ALL = ("g", "x", "core", "seq")
TP = 4

norm_epsilon = 1e-05
gelu_coeff = 0.7978845608
gelu_cubic = 0.044715
beta_first = 0.9
beta_second = 0.999
learn_rate = 0.05
small_rate = 0.3
decay_rate = 0.1
adam_epsilon = 1e-08
BIG = 1e30
BF = jnp.bfloat16
F32 = jnp.float32


def dot(left, right):
    return jnp.dot(left, right, preferred_element_type=F32)


def dot_nt(left, right):
    return lax.dot_general(left, right, (((1,), (1,)), ((), ())), preferred_element_type=F32)


def dot_tn(left, right):
    return lax.dot_general(left, right, (((0,), (0,)), ((), ())), preferred_element_type=F32)


def rotate_lanes(x, cos_t, low_t, high_t, sign):
    halves = []
    for part in range(x.shape[1] // 128):
        v = x[:, 128 * part : 128 * (part + 1)]
        up = pltpu.roll(v, 128 - ROT // 2, 1)
        down = pltpu.roll(v, ROT // 2, 1)
        halves.append(v * cos_t + sign * (up * low_t + down * high_t))
    return jnp.concatenate(halves, axis=1)


def head_of(shape):
    return lax.broadcasted_iota(jnp.int32, shape, 1) // HD


def half_place(flip_ref, row, half):
    if half is None:
        return row
    return pl.multiple_of((row // half + flip_ref[0]) % 2 * half + row % half, 256)


def attend_kernel(
    half, flip_ref, proj_ref, tab_ref, qx_ref, kx_ref, ctx_ref, rot_ref, lse_ref, k_s, v_s, q_s
):
    length, width = ctx_ref.shape
    heads = width // HD
    blk = min(256, length)
    span = half or length
    zero = jnp.zeros((), BF)
    head = head_of((span, width))
    for start in range(0, length, span):
        here = pl.ds(half_place(flip_ref, start, half), span)
        cos_t, low_t, high_t = tab_ref[0, here], tab_ref[1, here], tab_ref[2, here]
        proj = proj_ref[start : start + span]
        q = rotate_lanes(proj[:, :width], cos_t, low_t, high_t, 1.0).astype(BF)
        k = rotate_lanes(proj[:, width : 2 * width], cos_t, low_t, high_t, 1.0).astype(BF)
        v = proj[:, 2 * width :].astype(BF)
        rot_ref[here, :width] = q
        rot_ref[here, width : 2 * width] = k
        rot_ref[here, 2 * width :] = v
        q = q * BF(HD**-0.5)
        for h in range(heads):
            ext = (h + 1) % heads
            k_s[h, here] = jnp.where(head == h, k, jnp.where(head == ext, kx_ref[here], zero))
            v_s[h, here] = jnp.where(head == h, v, zero)
            q_s[h, here] = jnp.where(head == ext, qx_ref[here], q)
    tri = lax.broadcasted_iota(jnp.int32, (blk, blk), 0) <= lax.broadcasted_iota(
        jnp.int32, (blk, blk), 1
    )
    for i in range(length // blk):
        lo, hi = i * blk, (i + 1) * blk
        total = jnp.zeros((blk, width), F32)
        for h in range(heads):
            qb = q_s[h, lo:hi]
            diag = jnp.where(tri, dot_nt(k_s[h, lo:hi], qb), -BIG)
            top = jnp.max(diag, axis=0, keepdims=True)
            if i:
                past = dot_nt(k_s[h, :lo], qb)
                top = jnp.maximum(top, jnp.max(past, axis=0, keepdims=True))
            diag = jnp.exp(diag - top)
            mass = jnp.sum(diag, axis=0, keepdims=True)
            if i:
                past = jnp.exp(past - top)
                mass = mass + jnp.sum(past, axis=0, keepdims=True)
            lse_ref[h : h + 1, lo:hi] = top + jnp.log(mass)
            inv = 1.0 / mass
            total += dot_tn((diag * inv).astype(BF), v_s[h, lo:hi])
            if i:
                total += dot_tn((past * inv).astype(BF), v_s[h, :lo])
        ctx_ref[pl.ds(half_place(flip_ref, lo, half), blk)] = total.astype(BF)


def attend_back_kernel(
    half,
    flip_ref,
    rot_ref,
    dctx_ref,
    lse_ref,
    tab_ref,
    qx_ref,
    kx_ref,
    out_ref,
    k_s,
    v_s,
    q_s,
    dk_s,
    dv_s,
    dq_s,
):
    length, width = dctx_ref.shape
    heads = width // HD
    blk = min(256, length)
    head = head_of((length, width))
    zero = jnp.zeros((), BF)
    q = rot_ref[:, :width]
    k = rot_ref[:, width : 2 * width]
    v = rot_ref[:, 2 * width :]
    scaled = q * BF(HD**-0.5)
    for h in range(heads):
        ext = (h + 1) % heads
        k_s[h] = jnp.where(head == h, k, jnp.where(head == ext, kx_ref[...], zero))
        v_s[h] = jnp.where(head == h, v, zero)
        q_s[h] = jnp.where(head == ext, qx_ref[...], scaled)
    dk_s[...] = jnp.zeros_like(dk_s)
    dv_s[...] = jnp.zeros_like(dv_s)
    head_b = head_of((blk, width))
    tri = lax.broadcasted_iota(jnp.int32, (blk, blk), 0) <= lax.broadcasted_iota(
        jnp.int32, (blk, blk), 1
    )
    for i in range(length // blk):
        lo, hi = i * blk, (i + 1) * blk
        d_all = dctx_ref[pl.ds(half_place(flip_ref, lo, half), blk)]
        q_all = rot_ref[lo:hi, :width]
        total = jnp.zeros((blk, width), F32)
        for h in range(heads):
            qb = q_s[h, lo:hi]
            d_h = jnp.where(head_b == h, d_all, zero)
            q_h = jnp.where(head_b == h, q_all, zero)
            lse = lse_ref[h : h + 1, lo:hi]
            p_d = jnp.exp(jnp.where(tri, dot_nt(k_s[h, lo:hi], qb), -BIG) - lse)
            g_d = dot_nt(v_s[h, lo:hi], d_all)
            delta = jnp.sum(p_d * g_d, axis=0, keepdims=True)
            if i:
                p_p = jnp.exp(dot_nt(k_s[h, :lo], qb) - lse)
                g_p = dot_nt(v_s[h, :lo], d_all)
                delta = delta + jnp.sum(p_p * g_p, axis=0, keepdims=True)
            s_d = (p_d * (g_d - delta)).astype(BF)
            dv_s[lo:hi] += dot(p_d.astype(BF), d_h)
            dk_s[lo:hi] += dot(s_d, q_h)
            k_d = jnp.where(head_b == h, rot_ref[lo:hi, width : 2 * width], zero)
            total += dot_tn(s_d, k_d)
            if i:
                s_p = (p_p * (g_p - delta)).astype(BF)
                dv_s[:lo] += dot(p_p.astype(BF), d_h)
                dk_s[:lo] += dot(s_p, q_h)
                k_p = jnp.where(head_of((lo, width)) == h, rot_ref[:lo, width : 2 * width], zero)
                total += dot_tn(s_p, k_p)
        dq_s[lo:hi] = total
    scale = HD**-0.5
    cos_t, low_t, high_t = tab_ref[0], tab_ref[1], tab_ref[2]
    dq = rotate_lanes((dq_s[...] * scale).astype(BF).astype(F32), cos_t, low_t, high_t, -1.0)
    dk = rotate_lanes((dk_s[...] * scale).astype(BF).astype(F32), cos_t, low_t, high_t, -1.0)
    dv = dv_s[...]
    span = half or length
    for start in range(0, length, span):
        here = pl.ds(half_place(flip_ref, start, half), span)
        for n, grad in enumerate((dq, dk, dv)):
            out_ref[here, n * width : (n + 1) * width] = grad[start : start + span].astype(BF)


def attend(flip, half, proj, tables, q_ext, k_ext):
    length, width = proj.shape[0], proj.shape[1] // 3
    heads = width // HD
    return pl.pallas_call(
        functools.partial(attend_kernel, half),
        in_specs=[pl.BlockSpec(memory_space=pltpu.SMEM)]
        + [pl.BlockSpec(memory_space=pltpu.VMEM)] * 4,
        out_shape=(
            jax.ShapeDtypeStruct((length, width), BF),
            jax.ShapeDtypeStruct((length, 3 * width), BF),
            jax.ShapeDtypeStruct((8, length), F32),
        ),
        scratch_shapes=[pltpu.VMEM((heads, length, width), BF)] * 3,
        compiler_params=pltpu.CompilerParams(vmem_limit_bytes=50 << 20),
        cost_estimate=pl.CostEstimate(
            flops=heads * length * length * width * 2,
            bytes_accessed=length * width * 24,
            transcendentals=heads * length * length // 2,
        ),
        name="attend",
    )(flip, proj, tables, q_ext, k_ext)


def attend_back(flip, half, rot, d_context, lse, tables, q_ext, k_ext):
    length, width = d_context.shape
    heads = width // HD
    return pl.pallas_call(
        functools.partial(attend_back_kernel, half),
        in_specs=[pl.BlockSpec(memory_space=pltpu.SMEM)]
        + [pl.BlockSpec(memory_space=pltpu.VMEM)] * 6,
        out_shape=jax.ShapeDtypeStruct((length, 3 * width), BF),
        scratch_shapes=[pltpu.VMEM((heads, length, width), BF)] * 3
        + [pltpu.VMEM((length, width), F32)] * 3,
        compiler_params=pltpu.CompilerParams(vmem_limit_bytes=50 << 20),
        cost_estimate=pl.CostEstimate(
            flops=heads * length * length * width * 5,
            bytes_accessed=length * width * 24,
            transcendentals=heads * length * length // 2,
        ),
        name="attend_back",
    )(flip, rot, d_context, lse, tables, q_ext, k_ext)


def piece_row(at_ref, slot, side):
    z = (at_ref[1] + at_ref[2] * slot + 4) % 4
    g = at_ref[0] if side == 0 else 1 - at_ref[0]
    return pl.multiple_of(z * 32 + g * 16, 16)


def assemble_kernel(sources, plan, at_ref, *refs):
    n_in = 1 + max(source[0] for source in sources)
    ins, outs, flat = refs[:n_in], refs[n_in:-1], refs[-1]
    pieces = [
        (ins[ref] if index is None else ins[ref].at[index], piece_row(at_ref, slot, side))
        for ref, index, slot, side in sources
    ]
    for out_ref, (first, units, fold, parts) in zip(outs, plan):
        if fold == 1:
            rows = units // parts

            def put(u, carry):
                for part in range(parts):
                    for ref, row in pieces:
                        out_ref[pl.ds(u * 128 + row, 16), part * 256 : part * 256 + 256] = ref[
                            first + part * rows + u
                        ]
                return carry

            lax.fori_loop(0, rows, put, 0)
            continue

        def lay(u, carry):
            for ref, row in pieces:
                value = ref[first + u].astype(F32)
                for half in range(2):
                    flat[half, pl.ds(u * 128 + row, 16)] = value[:, 128 * half : 128 * (half + 1)]
            return carry

        lax.fori_loop(0, units, lay, 0)
        step = 128

        def take(n, carry):
            for p in range(fold):
                for half in range(2):
                    lane = p * 256 + half * 128
                    out_ref[pl.ds(n * step, step), lane : lane + 128] = flat[
                        half, pl.ds(n * step * fold + p, step, fold)
                    ].astype(BF)
            return carry

        lax.fori_loop(0, out_ref.shape[0] // step, take, 0)


def assemble(at, ins, sources, plan):
    vmem = pl.BlockSpec(memory_space=pltpu.VMEM)
    tall = max(units if fold > 1 else 1 for _, units, fold, _ in plan)
    total = sum(units for _, units, _, _ in plan)
    return pl.pallas_call(
        functools.partial(assemble_kernel, sources, plan),
        in_specs=[pl.BlockSpec(memory_space=pltpu.SMEM)] + [vmem] * len(ins),
        out_specs=[vmem] * len(plan),
        out_shape=[
            jax.ShapeDtypeStruct((units // parts * 128 // fold, 256 * fold * parts), BF)
            for _, units, fold, parts in plan
        ],
        scratch_shapes=[pltpu.VMEM((2, tall * 128, 128), F32)],
        compiler_params=pltpu.CompilerParams(vmem_limit_bytes=48 << 20),
        cost_estimate=pl.CostEstimate(
            flops=0, bytes_accessed=4 * total * 128 * 256, transcendentals=0
        ),
        name="assemble",
    )(at, *ins)


def disassemble_kernel(plan, at_ref, *refs):
    grads, outs, flat = refs[: len(plan)], refs[len(plan) : -1], refs[-1]
    pieces = [
        (
            outs[side].at[z] if len(outs) == 2 else outs[0].at[4 * side + z],
            piece_row(at_ref, z, side),
        )
        for side in range(2)
        for z in range(4)
    ]
    for g_ref, (first, units, fold, parts) in zip(grads, plan):
        if fold == 1:
            rows = units // parts

            def split(u, carry):
                for part in range(parts):
                    for ref, row in pieces:
                        ref[first + part * rows + u] = g_ref[
                            pl.ds(u * 128 + row, 16), part * 256 : part * 256 + 256
                        ].astype(BF)
                return carry

            lax.fori_loop(0, rows, split, 0)
            continue
        step = 128

        def lay(n, carry):
            for p in range(fold):
                for half in range(2):
                    lane = p * 256 + half * 128
                    flat[half, pl.ds(n * step * fold + p, step, fold)] = g_ref[
                        pl.ds(n * step, step), lane : lane + 128
                    ].astype(F32)
            return carry

        lax.fori_loop(0, g_ref.shape[0] // step, lay, 0)

        def give(u, carry):
            for ref, row in pieces:
                for half in range(2):
                    ref[first + u, :, 128 * half : 128 * (half + 1)] = flat[
                        half, pl.ds(u * 128 + row, 16)
                    ].astype(BF)
            return carry

        lax.fori_loop(0, units, give, 0)


def disassemble(at, grads, plan, one):
    vmem = pl.BlockSpec(memory_space=pltpu.VMEM)
    total = sum(units for _, units, _, _ in plan)
    tall = max(units if fold > 1 else 1 for _, units, fold, _ in plan)
    out = [jax.ShapeDtypeStruct((8 if one else 4, total, 16, 256), BF)] * (1 if one else 2)
    return pl.pallas_call(
        functools.partial(disassemble_kernel, plan),
        in_specs=[pl.BlockSpec(memory_space=pltpu.SMEM)] + [vmem] * len(grads),
        out_specs=[vmem] * len(out),
        out_shape=out,
        scratch_shapes=[pltpu.VMEM((2, tall * 128, 128), F32)],
        compiler_params=pltpu.CompilerParams(vmem_limit_bytes=48 << 20),
        cost_estimate=pl.CostEstimate(
            flops=0, bytes_accessed=6 * total * 128 * 256, transcendentals=0
        ),
        name="disassemble",
    )(at, *grads)


def adam_update(weights, grads, moment_one, moment_two, rate, decay):
    new_one = beta_first * moment_one + (1.0 - beta_first) * grads
    new_two = beta_second * moment_two + (1.0 - beta_second) * grads * grads
    corrected_one = new_one / (1.0 - beta_first**STEP)
    corrected_two = new_two / (1.0 - beta_second**STEP)
    new_weights = weights - rate * (
        corrected_one / (jnp.sqrt(corrected_two) + adam_epsilon) + decay * weights
    )
    return (new_weights, new_one, new_two)


def pack_kernel(masters_ref, out_ref, flat):
    slots = masters_ref.shape[0]
    for c in range(32):
        for part in range(8):
            place = (c // 16) * TP + part // 2
            flat[part % 2, pl.ds(place * slots * 16 + c % 16, slots, 16)] = masters_ref[
                :, c * 1024 + part * 128 : c * 1024 + part * 128 + 128
            ]
    for place in range(8):
        for side in range(2):
            out_ref[place, :, side * 128 : side * 128 + 128] = flat[
                side, place * slots * 16 : (place + 1) * slots * 16
            ].astype(BF)


def pack(masters):
    slots, piece = masters.shape
    return pl.pallas_call(
        pack_kernel,
        grid=(slots // 8,),
        in_specs=[pl.BlockSpec((8, piece), lambda i: (i, 0))],
        out_specs=pl.BlockSpec((8, 128, 256), lambda i: (0, i, 0)),
        out_shape=jax.ShapeDtypeStruct((8, slots * 16, 256), BF),
        scratch_shapes=[pltpu.VMEM((2, 1024, 128), F32)],
        compiler_params=pltpu.CompilerParams(vmem_limit_bytes=60 << 20),
        cost_estimate=pl.CostEstimate(
            flops=0, bytes_accessed=6 * slots * piece, transcendentals=0
        ),
        name="pack",
    )(masters)


def select_kernel(picks, table_ref, from_ref, *outs):
    for out_ref, blocks in zip(outs, picks):
        for n, block in enumerate(blocks):
            out_ref[n] = from_ref[pl.ds(pl.multiple_of(table_ref[block] * 16, 16), 16)]


def select(table, received, picks):
    vmem = pl.BlockSpec(memory_space=pltpu.VMEM)
    rows = received.shape[0]
    return pl.pallas_call(
        functools.partial(select_kernel, picks),
        in_specs=[pl.BlockSpec(memory_space=pltpu.SMEM), vmem],
        out_specs=[vmem] * len(picks),
        out_shape=[jax.ShapeDtypeStruct((len(p), 16, 256), BF) for p in picks],
        compiler_params=pltpu.CompilerParams(vmem_limit_bytes=60 << 20),
        cost_estimate=pl.CostEstimate(flops=0, bytes_accessed=rows * 900, transcendentals=0),
        name="select",
    )(table, received)


def place_kernel(takes, table_ref, turn_ref, extra_ref, *refs):
    ins, out_ref = refs[:-1], refs[-1]
    slots = out_ref.shape[1] // 16 - 1
    out_ref[...] = jnp.zeros_like(out_ref)
    for place in range(out_ref.shape[0]):
        out_ref[place, slots * 16 :] = extra_ref[place]
    for ref, take in zip(ins, takes):
        for n, (block, turn) in enumerate(take):
            if turn is not None:
                block = block + 2 * (turn_ref[0] ^ turn)
            slot = table_ref[block]
            out_ref[slot // slots, pl.ds(pl.multiple_of(slot % slots * 16, 16), 16)] = ref[n]


def place_blocks(table, turn, extra, ins, takes, slots):
    vmem = pl.BlockSpec(memory_space=pltpu.VMEM)
    smem = pl.BlockSpec(memory_space=pltpu.SMEM)
    return pl.pallas_call(
        functools.partial(place_kernel, takes),
        in_specs=[smem, smem, vmem] + [vmem] * len(ins),
        out_specs=vmem,
        out_shape=jax.ShapeDtypeStruct((8, slots * 16 + 16, 256), BF),
        compiler_params=pltpu.CompilerParams(vmem_limit_bytes=60 << 20),
        cost_estimate=pl.CostEstimate(flops=0, bytes_accessed=4 << 20, transcendentals=0),
        name="place",
    )(table, turn, extra, *ins)


def adam_kernel(from_ref, w_ref, one_ref, two_ref, w_out, one_out, two_out, low_out, flat):
    slots = w_ref.shape[0]
    part = pl.program_id(1)

    @pl.when(part == 0)
    def _():
        for place in range(8):
            for side in range(2):
                flat[side, place * slots * 16 : (place + 1) * slots * 16] = from_ref[
                    place, :, side * 128 : side * 128 + 128
                ].astype(F32)

    for c in range(8):
        for lane in range(8):
            at = slice(c * 1024 + lane * 128, c * 1024 + lane * 128 + 128)
            row = ((part // 2) * TP + lane // 2) * slots * 16 + (part % 2) * 8 + c
            grads = flat[lane % 2, pl.ds(row, slots, 16)]
            new, one, two = adam_update(
                w_ref[:, at], grads, one_ref[:, at], two_ref[:, at], learn_rate, decay_rate
            )
            w_out[:, at] = new
            one_out[:, at] = one
            two_out[:, at] = two
            low_out[:, at] = new.astype(BF)


def adam(received, masters, first_moment, second_moment):
    slots, piece = masters.shape
    block = pl.BlockSpec((16, piece // 4), lambda i, j: (i, j))
    whole = jax.ShapeDtypeStruct(masters.shape, F32)
    return pl.pallas_call(
        adam_kernel,
        grid=(slots // 16, 4),
        in_specs=[pl.BlockSpec((8, 256, 256), lambda i, j: (0, i, 0))] + [block] * 3,
        out_specs=[block] * 4,
        out_shape=[whole, whole, whole, jax.ShapeDtypeStruct(masters.shape, BF)],
        scratch_shapes=[pltpu.VMEM((2, 2048, 128), F32)],
        compiler_params=pltpu.CompilerParams(vmem_limit_bytes=60 << 20),
        cost_estimate=pl.CostEstimate(
            flops=20 * slots * piece, bytes_accessed=28 * slots * piece, transcendentals=0
        ),
        name="adam",
    )(received, masters, first_moment, second_moment)


@functools.lru_cache(maxsize=None)
def row_moves(n_seq, rows_here, length):
    local = length // n_seq
    per_dev = rows_here * local
    edges = {}
    for t in range(TP):
        for z in range(n_seq):
            for k in range(rows_here):
                row = rows_here * t + k
                token = (row // n_seq) * length + z * local
                target = (token // per_dev) * n_seq + row % n_seq
                edges.setdefault(t * n_seq + z, []).append((target, k, token % per_dev // local))
    steps = []
    for _ in range(rows_here):
        taken = {}

        def place(source, seen):
            for edge in edges[source]:
                if edge[0] not in seen:
                    seen.add(edge[0])
                    if edge[0] not in taken or place(taken[edge[0]][0], seen):
                        taken[edge[0]] = (source, edge)
                        return True
            return False

        for source in edges:
            assert place(source, set())
        pick = np.zeros(TP * n_seq, np.int32)
        put = np.zeros(TP * n_seq, np.int32)
        pairs = []
        for target, (source, edge) in taken.items():
            edges[source].remove(edge)
            pick[source] = edge[1]
            put[target] = edge[2]
            pairs.append((source, target))
        steps.append((sorted(pairs), pick, put))
    return steps


def body(
    tokens,
    cotangent,
    lengths,
    owners,
    masters,
    first_moment,
    second_moment,
    small_params,
    small_first,
    small_second,
):
    n_g = lax.axis_size("g")
    n_seq = lax.axis_size("seq")
    n_dp = n_g * TP
    capacity, piece = masters.shape
    n_blocks = owners.shape[0]
    rows_here, local, width = tokens.shape
    length = local * n_seq
    per_dev = rows_here * local
    group_rows = TP * per_dev // length
    cols = width // TP
    chunks = piece // width // n_g
    place_dp = lax.axis_index(DP)
    place_z = lax.axis_index("seq")
    t = place_dp % TP
    g = place_dp // TP
    core, side = t % 2, t // 2

    def swap(value, bit):
        return lax.ppermute(value, DP, [(i, i ^ bit) for i in range(n_dp)])

    pieces = n_seq == 4 and n_g == 2 and chunks == 16 and cols == 256 and capacity % 16 == 0
    at_hops = jnp.stack([g, place_z, -1]).astype(jnp.int32)
    at_near = jnp.stack([g, 0, 1]).astype(jnp.int32)
    at_all = jnp.array([0, 0, 1], jnp.int32)
    tie = lax.optimization_barrier
    n_all = n_dp * n_seq

    def to_all(value):
        return lax.all_to_all(
            value, ALL, split_axis=0, concat_axis=0, tiled=True
        )

    def order(first, second, flag):
        return jnp.concatenate(
            [jnp.where(flag == 0, first, second), jnp.where(flag == 0, second, first)], axis=0
        )

    steps = row_moves(n_seq, rows_here, length)

    def row_pairs(pairs, back):
        out = []
        for source, target in pairs:
            for a in range(n_g):
                ends = (a * TP * n_seq + source, a * TP * n_seq + target)
                out.append(ends[::-1] if back else ends)
        return out

    me = t * n_seq + place_z

    def to_rows(value):
        parts = []
        for pairs, pick, _ in steps:
            send = lax.dynamic_index_in_dim(value, jnp.asarray(pick)[me], 1, keepdims=False)
            parts.append(lax.ppermute(send, ALL, row_pairs(pairs, False)))
        puts = [jnp.asarray(put)[me] for _, _, put in steps]
        slots = []
        for s in range(rows_here):
            out = parts[0]
            for j in range(1, rows_here):
                out = jnp.where(puts[j] == s, parts[j], out)
            slots.append(out)
        return jnp.concatenate(slots, axis=1)

    def from_rows(value):
        value = value.reshape(rows_here, local, width)
        parts = []
        for pairs, _, put in steps:
            send = lax.dynamic_index_in_dim(value, jnp.asarray(put)[me], 0, keepdims=False)
            parts.append(lax.ppermute(send, ALL, row_pairs(pairs, True)))
        picks = [jnp.asarray(pick)[me] for _, pick, _ in steps]
        slots = []
        for s in range(rows_here):
            out = parts[0]
            for j in range(1, rows_here):
                out = jnp.where(picks[j] == s, parts[j], out)
            slots.append(out)
        return jnp.stack(slots, axis=0)

    block_index = jnp.arange(n_blocks, dtype=jnp.int32)
    same_owner = owners[:, None] == owners[None, :]
    earlier = block_index[None, :] < block_index[:, None]
    slot_rank = jnp.sum((same_owner & earlier).astype(jnp.int32), axis=1)
    slot_of_block = owners * capacity + slot_rank
    slot_ids = jnp.arange(n_dp * capacity, dtype=jnp.int32)
    hit = slot_of_block[None, :] == slot_ids[:, None]
    block_of_slot = jnp.sum(jnp.where(hit, block_index[None, :], 0), axis=1) + jnp.where(
        jnp.any(hit, axis=1), 0, n_blocks
    )

    if pieces:
        packed = pack(masters)
    else:
        packed = masters.astype(BF).reshape(capacity, n_g, chunks, TP, cols)
        packed = packed.transpose(1, 3, 0, 2, 4).reshape(n_dp, capacity * chunks, cols)
    small_here = small_params.shape[0]
    small_width = -(-(small_here + 2 * lengths.size) // 512) * 512
    note = jnp.concatenate(
        [
            small_params.astype(BF),
            (lengths.reshape(-1) // 32).astype(BF),
            (lengths.reshape(-1) % 32).astype(BF),
        ]
    )
    note = jnp.pad(note, (0, small_width - note.shape[0]))
    tokens, cotangent, packed = tie((tokens, cotangent, packed))
    both_rows = to_rows(jnp.stack([tokens, cotangent]))
    received = lax.all_to_all(packed, DP, split_axis=0, concat_axis=0, tiled=True)
    note, received, both_rows = tie((note, received, both_rows))
    token_rows, cotangent_rows = both_rows[0], both_rows[1]
    notes = to_all(jnp.broadcast_to(note[None], (n_all, small_width)))

    unit_rows = n_seq * n_g * chunks
    n_qkv = 3 * width // unit_rows
    n_out = width // unit_rows
    n_in = FF // unit_rows
    per_layer = n_qkv + n_out + 2 * n_in
    my_out = n_out // TP
    fold = FF // width

    def spread(value):
        return lax.all_gather(value, ("g", "seq"), axis=0)

    def build_hops(hops, plan):
        if not pieces:
            return build(hops, plan)
        own, along = hops
        ins = [own, *along, swap(own, TP), swap(jnp.stack(along), TP)]
        sources = [(by, None, by, 0) for by in range(n_seq)]
        sources += [(n_seq, None, 0, 1)]
        sources += [(n_seq + 1, by - 1, by, 1) for by in range(1, n_seq)]
        return assemble(at_hops, ins, sources, plan)

    def build(every, plan):
        if pieces:
            sources = [(0, a * n_seq + z, z, a) for a in range(n_g) for z in range(n_seq)]
            return assemble(at_all, [every], sources, plan)
        out = []
        for first, units, fold, parts in plan:
            rows = units // parts
            part = every[:, first : first + units]
            part = part.reshape(n_g, n_seq, parts, rows, chunks, cols).transpose(3, 1, 0, 4, 2, 5)
            out.append(part.reshape(rows * unit_rows // fold, parts * cols * fold))
        return out

    my_units = (1 + fold) * my_out
    n_both = TP * my_units

    def parts_of(layer):
        start = layer * per_layer
        qkv = list(range(start, start + n_qkv))
        inner = list(range(start + n_qkv + n_out, start + n_qkv + n_out + n_in))
        turned = []
        for a in range(TP):
            turned.append([start + n_qkv + my_out * a + e for e in range(my_out)])
            for q in range(fold):
                down = start + n_qkv + n_out + n_in + (q * TP + a) * my_out
                turned[a] += [down + e for e in range(my_out)]
        return qkv, inner, turned

    qkv0, in0, turned0 = parts_of(0)
    qkv1, in1, turned1 = parts_of(1)
    turned = [b for a in range(TP) for b in turned0[a] + turned1[a]]
    picks = [qkv0, in0, turned, qkv1 + in1]
    if pieces:
        m_qkv0, m_in0, swapped, m_rest1 = select(
            slot_of_block, received.reshape(n_dp * capacity * chunks, cols), picks
        )
    else:
        blocks = received.reshape(n_dp * capacity, chunks, cols)[slot_of_block]
        m_qkv0, m_in0, swapped, m_rest1 = [blocks[jnp.array(p)] for p in picks]
    swapped = swapped.reshape(TP, 2 * my_units, chunks, cols)
    plan_qkv = (0, n_qkv, 3, 1)
    plan_both = (0, n_both, 1, TP)
    def hop_z(value):
        return [
            lax.ppermute(value, "seq", [(i, (i + by) % n_seq) for i in range(n_seq)])
            for by in range(1, n_seq)
        ]

    m_qkv0, swapped, notes = tie((m_qkv0, swapped, notes))
    z_qkv0 = (m_qkv0, hop_z(m_qkv0)) if pieces else spread(m_qkv0)
    swapped = lax.all_to_all(swapped, ("x", "core"), split_axis=0, concat_axis=0, tiled=True)
    m_both0 = swapped[:, :my_units].reshape(n_both, chunks, cols)
    m_both1 = swapped[:, my_units:].reshape(n_both, chunks, cols)
    z_rest0 = spread(jnp.concatenate([m_in0, m_both0]))
    z_rest1 = spread(jnp.concatenate([m_rest1, m_both1]))

    small_all = notes[:, :small_here].reshape(-1)
    pairs = notes[::n_seq, small_here : small_here + 2 * lengths.size].astype(jnp.int32)
    pairs = pairs.reshape(n_dp, 2, rows_here, lengths.shape[1])
    all_lengths = (pairs[:, 0] * 32 + pairs[:, 1]).reshape(n_dp * rows_here, -1)
    vectors = []
    for layer in range(LAYERS):
        base = layer * (3 * width + FF)
        small_f = small_all[base : base + 3 * width + FF].astype(F32)
        bias_in = lax.dynamic_index_in_dim(
            small_f[2 * width : 2 * width + FF].reshape(fold, TP, cols), t, 1, keepdims=False
        ).reshape(-1)
        vectors.append(
            (small_f[:width], small_f[width : 2 * width], bias_in, small_f[2 * width + FF :])
        )

    mine_rows = jnp.arange(group_rows) * n_seq + place_z
    if group_rows == 2:
        mine_rows = jnp.where(side == 0, mine_rows, mine_rows[::-1])
    row_lengths = all_lengths[g * TP * rows_here + mine_rows]
    ends = jnp.cumsum(row_lengths, axis=1)
    starts = ends - row_lengths
    places = jnp.arange(length, dtype=jnp.int32)
    segment = jnp.sum((places[None, :, None] >= ends[:, None, :]).astype(jnp.int32), axis=2)
    which = segment[:, :, None] == jnp.arange(lengths.shape[1], dtype=jnp.int32)[None, None, :]
    within = places[None, :] - jnp.sum(jnp.where(which, starts[:, None, :], 0), axis=2)
    lane = jnp.arange(128)
    feature = lane % HD
    inverse = 1.0 / 10000.0 ** (jnp.arange(0, ROT, 2, dtype=F32) / ROT)
    angle = within.astype(F32)[..., None] * jnp.tile(inverse, 128 // (ROT // 2))
    cosine, sine = jnp.cos(angle), jnp.sin(angle)
    tables = jnp.stack(
        [
            jnp.where(feature < ROT, cosine, 1.0),
            jnp.where(feature < ROT // 2, -sine, 0.0),
            jnp.where((feature >= ROT // 2) & (feature < ROT), sine, 0.0),
        ],
        axis=1,
    )
    wide = jnp.arange(cols) % HD
    hits = segment[:, :, None] == wide[None, None, :]
    q_ext = jnp.where(hits, 1.0, 0.0).astype(BF)
    k_ext = jnp.where(hits | (wide >= lengths.shape[1])[None, None, :], 0.0, -BIG).astype(BF)

    half = 2 * per_dev // 2 if group_rows == 2 else None
    flip = jnp.full((1,), core, jnp.int32)

    def gather_group(value):
        far = swap(value, 2)
        near = swap(value, 1)
        far_near = swap(far, 1)
        if group_rows == 2:
            return [jnp.concatenate([value, near]), jnp.concatenate([far, far_near])]
        own, other = order(value, near, core), order(far, far_near, core)
        return [order(own, other, side)]

    def halve(value):
        if group_rows == 2:
            keep, send = value[:per_dev], value[per_dev:]
        else:
            value = value.reshape(2, per_dev, width)
            keep = lax.dynamic_index_in_dim(value, core, 0, keepdims=False)
            send = lax.dynamic_index_in_dim(value, 1 - core, 0, keepdims=False)
        return keep + swap(send.astype(BF), 1).astype(F32)

    def scatter_far(part):
        return swap(halve(part).astype(BF), 2)

    def scatter_pair(parts):
        if group_rows == 2:
            return parts
        pair = parts[0].reshape(2, 2 * per_dev, width)
        own = lax.dynamic_index_in_dim(pair, side, 0, keepdims=False)
        other = lax.dynamic_index_in_dim(pair, 1 - side, 0, keepdims=False)
        return own, other

    def scatter_group(parts):
        own, other = scatter_pair(parts)
        far = scatter_far(other)
        return halve(own) + far.astype(F32)

    state = token_rows.astype(F32)

    def norm(state, vector):
        gain, shift = vector[0], vector[1]
        centered = state - jnp.mean(state, axis=-1, keepdims=True)
        inv_std = lax.rsqrt(jnp.mean(centered * centered, axis=-1, keepdims=True) + norm_epsilon)
        normed = centered * inv_std
        return normed, inv_std, (normed * gain + shift).astype(BF)

    def front(hiddens, w_qkv):
        return [dot(hidden, w_qkv) for hidden in hiddens]

    def attention(projs):
        return [attend(flip, half, proj, tables[r], q_ext[r], k_ext[r]) for r, proj in enumerate(projs)]

    def gelu_pair(inner):
        tanh_part = jnp.tanh(gelu_coeff * (inner + gelu_cubic * inner * inner * inner))
        active = 0.5 * inner * (1.0 + tanh_part)
        slope = 0.5 * (1.0 + tanh_part) + 0.5 * inner * (1.0 - tanh_part * tanh_part) * (
            gelu_coeff * (1.0 + 3.0 * gelu_cubic * inner * inner)
        )
        return active.astype(BF), slope.astype(BF)

    def inside(hiddens, w_in, bias_in):
        pairs = [gelu_pair(dot(hidden, w_in) + bias_in) for hidden in hiddens]
        return [slope for _, slope in pairs], [active for active, _ in pairs]

    normed0, inv_std0, hidden = norm(state, vectors[0])
    hiddens0 = gather_group(hidden)
    (w_qkv0,) = build_hops(z_qkv0, [plan_qkv])
    attended0 = attention(front(hiddens0, w_qkv0))
    d_branch, attended0[0] = tie((cotangent_rows, attended0[0]))
    d_branch_rows = gather_group(d_branch)
    z_rest0, d_branch_rows = tie((z_rest0, d_branch_rows))
    w_in0, both = build(z_rest0, [(0, n_in, fold, 1), (n_in, n_both, 1, TP)])
    inners0, actives0 = inside(hiddens0, w_in0, vectors[0][2])
    w_out0, w_down0 = both[:cols], both[cols:]
    parts = [None] * len(hiddens0)
    for r in reversed(range(len(hiddens0))):
        parts[r] = dot(attended0[r][0], w_out0) + dot(actives0[r], w_down0)
    state = state + scatter_group(parts) + vectors[0][3]
    normed1, inv_std1, hidden = norm(state, vectors[1])
    hiddens1 = gather_group(hidden)
    w_qkv1, w_in1, both = build(
        z_rest1, [plan_qkv, (n_qkv, n_in, fold, 1), (n_qkv + n_in, n_both, 1, TP)]
    )
    attended1 = attention(front(hiddens1, w_qkv1))
    inners1, actives1 = inside(hiddens1, w_in1, vectors[1][2])
    w_out1, w_down1 = both[:cols], both[cols:]
    parts = [
        dot(attended1[r][0], w_out1) + dot(actives1[r], w_down1) for r in range(len(hiddens1))
    ]
    outputs = (state + scatter_group(parts) + vectors[1][3]).astype(BF)

    def lay_out(grads, plan):
        if pieces:
            return disassemble(at_all, grads, plan, True)[0]
        every = []
        for grad, (_, units, fold, parts) in zip(grads, plan):
            rows = units // parts
            grad = grad.astype(BF).reshape(rows, n_seq, n_g, chunks, parts, cols)
            grad = grad.transpose(2, 1, 4, 0, 3, 5)
            every.append(grad.reshape(n_g * n_seq, units, chunks, cols))
        return jnp.concatenate(every, axis=1)

    def sum_all(laid):
        return lax.psum_scatter(laid, ("g", "seq"), scatter_dimension=0, tiled=False)

    def lay_near(grads, plan):
        return disassemble(at_near, grads, plan, False) if pieces else lay_out(grads, plan)

    def sum_g(laid):
        if not pieces:
            return sum_all(laid)
        keep, send = laid
        return (keep.astype(F32) + swap(send, TP).astype(F32)).astype(BF)

    def sum_z(total):
        if not pieces:
            return total
        total = lax.all_to_all(total, "seq", split_axis=0, concat_axis=0, tiled=True)
        return jnp.sum(total.astype(F32), axis=0).astype(BF)

    def both_grads(d_rows, attended, actives):
        g_out = sum(dot_tn(a[0], d) for a, d in zip(attended, d_rows))
        g_down = sum(dot_tn(a, d) for a, d in zip(actives, d_rows))
        return jnp.concatenate([g_out, g_down])

    def back_inner(d_row, inner, w_down):
        return (dot_nt(d_row, w_down) * inner.astype(F32)).astype(BF)

    def back_attention(r, d_row, attended, w_out):
        d_context = dot_nt(d_row, w_out).astype(BF)
        return attend_back(flip, half, attended[1], d_context, attended[2], tables[r], q_ext[r], k_ext[r])

    def back_norm(d_state, d_hidden, normed, inv_std, vector):
        d_normed = d_hidden * vector[0]
        return d_state + inv_std * (
            d_normed
            - jnp.mean(d_normed, axis=-1, keepdims=True)
            - normed * jnp.mean(d_normed * normed, axis=-1, keepdims=True)
        )

    def sums(d_hidden, normed, d_inners, d_branch):
        g_bias_in = sum(jnp.sum(d.astype(F32), axis=0) for d in d_inners)
        wide_bias = (
            (jnp.arange(TP) == t).astype(F32)[None, :, None] * g_bias_in.reshape(fold, 1, cols)
        ).reshape(-1)
        return jnp.concatenate(
            [
                jnp.sum(d_hidden * normed, axis=0),
                jnp.sum(d_hidden, axis=0),
                wide_bias,
                jnp.sum(d_branch.astype(F32), axis=0),
            ]
        )

    turns = range(group_rows)
    last = group_rows - 1
    d_inners1, d_projs1, parts = [None] * group_rows, [None] * group_rows, [None] * group_rows
    d_rows = d_branch_rows
    for r in turns:
        d_inners1[r] = back_inner(d_rows[r], inners1[r], w_down1)
    g_in = sum(dot_tn(hiddens1[r], d_inners1[r]) for r in turns)
    laid = lay_out(
        [g_in, both_grads(d_rows, attended1, actives1)],
        [(0, n_in, fold, 1), (n_in, n_both, 1, TP)],
    )
    laid, d_rows, d_inners1 = tie((laid, d_rows, d_inners1))
    r_early1 = sum_all(laid)
    for r in reversed(turns):
        d_projs1[r] = back_attention(r, d_rows[r], attended1[r], w_out1)
        parts[r] = dot_nt(d_inners1[r], w_in1) + dot_nt(d_projs1[r], w_qkv1)
        if r == last and last:
            parts[r], d_rows, outputs = tie((parts[r], d_rows, outputs))
    d_state = cotangent_rows.astype(F32)
    d_hidden1 = scatter_group(parts)
    d_state = back_norm(d_state, d_hidden1, normed1, inv_std1, vectors[1])
    d_branch = d_state.astype(BF)
    d_branch, d_projs1, r_early1, outputs = tie((d_branch, d_projs1, r_early1, outputs))
    outputs = from_rows(outputs)
    d_rows = gather_group(d_branch)
    g_qkv = sum(dot_tn(hiddens1[r], d_projs1[r]) for r in turns)
    laid = lay_out([g_qkv], [plan_qkv])
    d_rows[0], laid = tie((d_rows[0], laid))
    r_qkv1 = sum_all(laid)
    d_inners0, d_projs0 = [None] * group_rows, [None] * group_rows
    d_inners0[0] = back_inner(d_rows[0], inners0[0], w_down0)
    d_projs0[0] = back_attention(0, d_rows[0], attended0[0], w_out0)
    d_rows, d_projs0[0], d_inners0[0] = tie((d_rows, d_projs0[0], d_inners0[0]))
    laid = lay_near([both_grads(d_rows, attended0, actives0)], [plan_both])
    d_rows, laid = tie((d_rows, laid))
    s_both0 = sum_g(laid)
    for r in turns[1:]:
        d_inners0[r] = back_inner(d_rows[r], inners0[r], w_down0)
    g_in = sum(dot_tn(hiddens0[r], d_inners0[r]) for r in turns)
    laid = lay_near([g_in], [(0, n_in, fold, 1)])
    d_rows, laid, s_both0 = tie((d_rows, laid, s_both0))
    r_both0 = sum_z(s_both0)
    s_in0 = sum_g(laid)
    for r in turns[1:]:
        d_projs0[r] = back_attention(r, d_rows[r], attended0[r], w_out0)
    g_qkv = sum(dot_tn(hiddens0[r], d_projs0[r]) for r in turns)
    laid = lay_near([g_qkv], [plan_qkv])
    d_projs0, laid, s_in0 = tie((d_projs0, laid, s_in0))
    s_qkv0 = sum_g(laid)
    for r in reversed(turns):
        parts[r] = dot_nt(d_inners0[r], w_in0) + dot_nt(d_projs0[r], w_qkv0)
    parts, r_both0, s_in0, r_qkv1 = tie((parts, r_both0, s_in0, r_qkv1))
    r_in0 = sum_z(s_in0)
    s_qkv0, r_in0 = tie((s_qkv0, r_in0))
    r_qkv0 = sum_z(s_qkv0)
    d_hidden0 = scatter_group(parts)
    small_grads = [
        sums(d_hidden0, normed0, d_inners0, d_branch),
        sums(d_hidden1, normed1, d_inners1, cotangent_rows),
    ]
    d_state = back_norm(d_state, d_hidden0, normed0, inv_std0, vectors[0])
    swapped = jnp.concatenate(
        [r.reshape(TP, my_units, chunks, cols) for r in (r_both0, r_early1[n_in:])], axis=1
    )
    mine = [lax.dynamic_index_in_dim(swapped, t ^ k, 0, keepdims=False) for k in range(TP)]
    mine = [mine[0]] + [swap(mine[k], k) for k in range(1, TP)]
    grad_in = from_rows(d_state.astype(BF))
    small_flat = jnp.concatenate(small_grads).reshape(n_all, small_here)
    small_flat = jnp.pad(small_flat, ((0, 0), (0, small_width - small_here)))
    if pieces:
        extra = small_flat.astype(BF).reshape(n_dp, -1, cols)
        extra = jnp.pad(extra, ((0, 0), (0, 16 - extra.shape[1]), (0, 0)))
        ins = [r_qkv0, r_in0, r_qkv1, r_early1[:n_in]] + mine
        takes = [[(b, None) for b in blocks] for blocks in (qkv0, in0, qkv1, in1)]
        takes += [[(b, k) for b in turned0[0] + turned1[0]] for k in range(TP)]
        slots = place_blocks(
            slot_of_block, jnp.full((1,), t, jnp.int32), extra, ins, takes, capacity
        )
        owned = lax.all_to_all(slots, DP, split_axis=0, concat_axis=0, tiled=True)
        small_part = owned[:, capacity * chunks :].astype(F32).sum(axis=0)
        small_part = small_part.reshape(-1, small_width)[:n_seq]
        small_owned = lax.all_to_all(
            small_part, "seq", split_axis=0, concat_axis=0, tiled=True
        ).sum(axis=0)[:small_here]
    else:
        swapped = jnp.stack(mine)[jnp.arange(TP) ^ t]
        ordered = [r_qkv0, r_in0, swapped.reshape(-1, chunks, cols), r_qkv1, r_early1[:n_in]]
        index = np.zeros(n_blocks + 1, np.int32)
        index[np.array(qkv0 + in0 + turned + qkv1 + in1)] = np.arange(n_blocks)
        index[n_blocks] = n_blocks
        grads = jnp.concatenate(ordered + [jnp.zeros((1, chunks, cols), BF)])
        slots = grads[jnp.asarray(index)[block_of_slot]].reshape(n_dp, capacity, chunks, cols)
        owned = lax.all_to_all(slots, DP, split_axis=0, concat_axis=0, tiled=True)
        owned = owned.reshape(n_g, TP, capacity, chunks, cols)
        owned = owned.transpose(2, 0, 3, 1, 4).reshape(capacity, piece).astype(F32)
        small_owned = jnp.sum(to_all(small_flat), axis=0)[:small_here]
    if pieces:
        new_masters, new_first, new_second, new_low = adam(
            owned, masters, first_moment, second_moment
        )
    else:
        new_masters, new_first, new_second = adam_update(
            masters, owned, first_moment, second_moment, learn_rate, decay_rate
        )
        new_low = new_masters.astype(BF)
    small_new, small_first_new, small_second_new = adam_update(
        small_params, small_owned, small_first, small_second, small_rate, 0.0
    )
    return (
        outputs,
        grad_in,
        new_masters,
        new_first,
        new_second,
        new_low,
        small_new,
        small_first_new,
        small_second_new,
    )


def solution(mesh):
    n_dp, n_seq = mesh.devices.shape
    cut = Mesh(mesh.devices.reshape(n_dp // TP, 2, 2, n_seq), ALL)
    placed = (
        P(DP, "seq", None),
        P(DP, "seq", None),
        P(DP, None),
        P(),
        P(DP, "seq"),
        P(DP, "seq"),
        P(DP, "seq"),
        P(ALL),
        P(ALL),
        P(ALL),
    )
    return jax.shard_map(
        body,
        mesh=cut,
        in_specs=placed,
        out_specs=(
            P(DP, "seq", None),
            P(DP, "seq", None),
            P(DP, "seq"),
            P(DP, "seq"),
            P(DP, "seq"),
            P(DP, "seq"),
            P(ALL),
            P(ALL),
            P(ALL),
        ),
        check_vma=False,
    )
```

```python
import functools

import jax
import jax.numpy as jnp
import numpy as np
from jax import lax
from jax.experimental import pallas as pl
from jax.experimental.pallas import tpu as pltpu
from jax.sharding import Mesh
from jax.sharding import PartitionSpec as P

HEADS = 16
HD = 64
ROT = 32
FF = 4096
LAYERS = 2
STEP = 10
DP = ("g", "x", "core")
ALL = ("g", "x", "core", "seq")
TP = 4

norm_epsilon = 1e-05
gelu_coeff = 0.7978845608
gelu_cubic = 0.044715
beta_first = 0.9
beta_second = 0.999
learn_rate = 0.05
small_rate = 0.3
decay_rate = 0.1
adam_epsilon = 1e-08
BIG = 1e30
BF = jnp.bfloat16
F32 = jnp.float32


def dot(left, right):
    return jnp.dot(left, right, preferred_element_type=F32)


def dot_nt(left, right):
    return lax.dot_general(left, right, (((1,), (1,)), ((), ())), preferred_element_type=F32)


def dot_tn(left, right):
    return lax.dot_general(left, right, (((0,), (0,)), ((), ())), preferred_element_type=F32)


def rotate_lanes(x, cos_t, low_t, high_t, sign):
    halves = []
    for part in range(x.shape[1] // 128):
        v = x[:, 128 * part : 128 * (part + 1)]
        up = pltpu.roll(v, 128 - ROT // 2, 1)
        down = pltpu.roll(v, ROT // 2, 1)
        halves.append(v * cos_t + sign * (up * low_t + down * high_t))
    return jnp.concatenate(halves, axis=1)


def head_of(shape):
    return lax.broadcasted_iota(jnp.int32, shape, 1) // HD


def half_place(flip_ref, row, half):
    if half is None:
        return row
    return pl.multiple_of((row // half + flip_ref[0]) % 2 * half + row % half, 256)


def attend_kernel(
    half, flip_ref, proj_ref, tab_ref, qx_ref, kx_ref, ctx_ref, rot_ref, lse_ref, k_s, v_s, q_s
):
    length, width = ctx_ref.shape
    heads = width // HD
    blk = min(256, length)
    span = half or length
    zero = jnp.zeros((), BF)
    head = head_of((span, width))
    for start in range(0, length, span):
        here = pl.ds(half_place(flip_ref, start, half), span)
        cos_t, low_t, high_t = tab_ref[0, here], tab_ref[1, here], tab_ref[2, here]
        proj = proj_ref[start : start + span]
        q = rotate_lanes(proj[:, :width], cos_t, low_t, high_t, 1.0).astype(BF)
        k = rotate_lanes(proj[:, width : 2 * width], cos_t, low_t, high_t, 1.0).astype(BF)
        v = proj[:, 2 * width :].astype(BF)
        rot_ref[here, :width] = q
        rot_ref[here, width : 2 * width] = k
        rot_ref[here, 2 * width :] = v
        q = q * BF(HD**-0.5)
        for h in range(heads):
            ext = (h + 1) % heads
            k_s[h, here] = jnp.where(head == h, k, jnp.where(head == ext, kx_ref[here], zero))
            v_s[h, here] = jnp.where(head == h, v, zero)
            q_s[h, here] = jnp.where(head == ext, qx_ref[here], q)
    tri = lax.broadcasted_iota(jnp.int32, (blk, blk), 0) <= lax.broadcasted_iota(
        jnp.int32, (blk, blk), 1
    )
    for i in range(length // blk):
        lo, hi = i * blk, (i + 1) * blk
        total = jnp.zeros((blk, width), F32)
        for h in range(heads):
            qb = q_s[h, lo:hi]
            diag = jnp.where(tri, dot_nt(k_s[h, lo:hi], qb), -BIG)
            top = jnp.max(diag, axis=0, keepdims=True)
            if i:
                past = dot_nt(k_s[h, :lo], qb)
                top = jnp.maximum(top, jnp.max(past, axis=0, keepdims=True))
            diag = jnp.exp(diag - top)
            mass = jnp.sum(diag, axis=0, keepdims=True)
            if i:
                past = jnp.exp(past - top)
                mass = mass + jnp.sum(past, axis=0, keepdims=True)
            lse_ref[h : h + 1, lo:hi] = top + jnp.log(mass)
            inv = 1.0 / mass
            total += dot_tn((diag * inv).astype(BF), v_s[h, lo:hi])
            if i:
                total += dot_tn((past * inv).astype(BF), v_s[h, :lo])
        ctx_ref[pl.ds(half_place(flip_ref, lo, half), blk)] = total.astype(BF)


def attend_back_kernel(
    half,
    flip_ref,
    rot_ref,
    dctx_ref,
    lse_ref,
    tab_ref,
    qx_ref,
    kx_ref,
    out_ref,
    k_s,
    v_s,
    q_s,
    dk_s,
    dv_s,
    dq_s,
):
    length, width = dctx_ref.shape
    heads = width // HD
    blk = min(256, length)
    head = head_of((length, width))
    zero = jnp.zeros((), BF)
    q = rot_ref[:, :width]
    k = rot_ref[:, width : 2 * width]
    v = rot_ref[:, 2 * width :]
    scaled = q * BF(HD**-0.5)
    for h in range(heads):
        ext = (h + 1) % heads
        k_s[h] = jnp.where(head == h, k, jnp.where(head == ext, kx_ref[...], zero))
        v_s[h] = jnp.where(head == h, v, zero)
        q_s[h] = jnp.where(head == ext, qx_ref[...], scaled)
    dk_s[...] = jnp.zeros_like(dk_s)
    dv_s[...] = jnp.zeros_like(dv_s)
    head_b = head_of((blk, width))
    tri = lax.broadcasted_iota(jnp.int32, (blk, blk), 0) <= lax.broadcasted_iota(
        jnp.int32, (blk, blk), 1
    )
    for i in range(length // blk):
        lo, hi = i * blk, (i + 1) * blk
        d_all = dctx_ref[pl.ds(half_place(flip_ref, lo, half), blk)]
        q_all = rot_ref[lo:hi, :width]
        total = jnp.zeros((blk, width), F32)
        for h in range(heads):
            qb = q_s[h, lo:hi]
            d_h = jnp.where(head_b == h, d_all, zero)
            q_h = jnp.where(head_b == h, q_all, zero)
            lse = lse_ref[h : h + 1, lo:hi]
            p_d = jnp.exp(jnp.where(tri, dot_nt(k_s[h, lo:hi], qb), -BIG) - lse)
            g_d = dot_nt(v_s[h, lo:hi], d_all)
            delta = jnp.sum(p_d * g_d, axis=0, keepdims=True)
            if i:
                p_p = jnp.exp(dot_nt(k_s[h, :lo], qb) - lse)
                g_p = dot_nt(v_s[h, :lo], d_all)
                delta = delta + jnp.sum(p_p * g_p, axis=0, keepdims=True)
            s_d = (p_d * (g_d - delta)).astype(BF)
            dv_s[lo:hi] += dot(p_d.astype(BF), d_h)
            dk_s[lo:hi] += dot(s_d, q_h)
            k_d = jnp.where(head_b == h, rot_ref[lo:hi, width : 2 * width], zero)
            total += dot_tn(s_d, k_d)
            if i:
                s_p = (p_p * (g_p - delta)).astype(BF)
                dv_s[:lo] += dot(p_p.astype(BF), d_h)
                dk_s[:lo] += dot(s_p, q_h)
                k_p = jnp.where(head_of((lo, width)) == h, rot_ref[:lo, width : 2 * width], zero)
                total += dot_tn(s_p, k_p)
        dq_s[lo:hi] = total
    scale = HD**-0.5
    cos_t, low_t, high_t = tab_ref[0], tab_ref[1], tab_ref[2]
    dq = rotate_lanes((dq_s[...] * scale).astype(BF).astype(F32), cos_t, low_t, high_t, -1.0)
    dk = rotate_lanes((dk_s[...] * scale).astype(BF).astype(F32), cos_t, low_t, high_t, -1.0)
    dv = dv_s[...]
    span = half or length
    for start in range(0, length, span):
        here = pl.ds(half_place(flip_ref, start, half), span)
        for n, grad in enumerate((dq, dk, dv)):
            out_ref[here, n * width : (n + 1) * width] = grad[start : start + span].astype(BF)


def attend(flip, half, proj, tables, q_ext, k_ext):
    length, width = proj.shape[0], proj.shape[1] // 3
    heads = width // HD
    return pl.pallas_call(
        functools.partial(attend_kernel, half),
        in_specs=[pl.BlockSpec(memory_space=pltpu.SMEM)]
        + [pl.BlockSpec(memory_space=pltpu.VMEM)] * 4,
        out_shape=(
            jax.ShapeDtypeStruct((length, width), BF),
            jax.ShapeDtypeStruct((length, 3 * width), BF),
            jax.ShapeDtypeStruct((8, length), F32),
        ),
        scratch_shapes=[pltpu.VMEM((heads, length, width), BF)] * 3,
        compiler_params=pltpu.CompilerParams(vmem_limit_bytes=50 << 20),
        cost_estimate=pl.CostEstimate(
            flops=heads * length * length * width * 2,
            bytes_accessed=length * width * 24,
            transcendentals=heads * length * length // 2,
        ),
        name="attend",
    )(flip, proj, tables, q_ext, k_ext)


def attend_back(flip, half, rot, d_context, lse, tables, q_ext, k_ext):
    length, width = d_context.shape
    heads = width // HD
    return pl.pallas_call(
        functools.partial(attend_back_kernel, half),
        in_specs=[pl.BlockSpec(memory_space=pltpu.SMEM)]
        + [pl.BlockSpec(memory_space=pltpu.VMEM)] * 6,
        out_shape=jax.ShapeDtypeStruct((length, 3 * width), BF),
        scratch_shapes=[pltpu.VMEM((heads, length, width), BF)] * 3
        + [pltpu.VMEM((length, width), F32)] * 3,
        compiler_params=pltpu.CompilerParams(vmem_limit_bytes=50 << 20),
        cost_estimate=pl.CostEstimate(
            flops=heads * length * length * width * 5,
            bytes_accessed=length * width * 24,
            transcendentals=heads * length * length // 2,
        ),
        name="attend_back",
    )(flip, rot, d_context, lse, tables, q_ext, k_ext)


def piece_row(at_ref, slot, side):
    z = (at_ref[1] + at_ref[2] * slot + 4) % 4
    g = at_ref[0] if side == 0 else 1 - at_ref[0]
    return pl.multiple_of(z * 32 + g * 16, 16)


def assemble_kernel(sources, plan, at_ref, *refs):
    n_in = 1 + max(source[0] for source in sources)
    ins, outs, flat = refs[:n_in], refs[n_in:-1], refs[-1]
    pieces = [
        (ins[ref] if index is None else ins[ref].at[index], piece_row(at_ref, slot, side))
        for ref, index, slot, side in sources
    ]
    for out_ref, (first, units, fold, parts) in zip(outs, plan):
        if fold == 1:
            rows = units // parts

            def put(u, carry):
                for part in range(parts):
                    for ref, row in pieces:
                        out_ref[pl.ds(u * 128 + row, 16), part * 256 : part * 256 + 256] = ref[
                            first + part * rows + u
                        ]
                return carry

            lax.fori_loop(0, rows, put, 0)
            continue

        def lay(u, carry):
            for ref, row in pieces:
                value = ref[first + u].astype(F32)
                for half in range(2):
                    flat[half, pl.ds(u * 128 + row, 16)] = value[:, 128 * half : 128 * (half + 1)]
            return carry

        lax.fori_loop(0, units, lay, 0)
        step = 128

        def take(n, carry):
            for p in range(fold):
                for half in range(2):
                    lane = p * 256 + half * 128
                    out_ref[pl.ds(n * step, step), lane : lane + 128] = flat[
                        half, pl.ds(n * step * fold + p, step, fold)
                    ].astype(BF)
            return carry

        lax.fori_loop(0, out_ref.shape[0] // step, take, 0)


def assemble(at, ins, sources, plan):
    vmem = pl.BlockSpec(memory_space=pltpu.VMEM)
    tall = max(units if fold > 1 else 1 for _, units, fold, _ in plan)
    total = sum(units for _, units, _, _ in plan)
    return pl.pallas_call(
        functools.partial(assemble_kernel, sources, plan),
        in_specs=[pl.BlockSpec(memory_space=pltpu.SMEM)] + [vmem] * len(ins),
        out_specs=[vmem] * len(plan),
        out_shape=[
            jax.ShapeDtypeStruct((units // parts * 128 // fold, 256 * fold * parts), BF)
            for _, units, fold, parts in plan
        ],
        scratch_shapes=[pltpu.VMEM((2, tall * 128, 128), F32)],
        compiler_params=pltpu.CompilerParams(vmem_limit_bytes=48 << 20),
        cost_estimate=pl.CostEstimate(
            flops=0, bytes_accessed=4 * total * 128 * 256, transcendentals=0
        ),
        name="assemble",
    )(at, *ins)


def disassemble_kernel(plan, at_ref, *refs):
    grads, outs, flat = refs[: len(plan)], refs[len(plan) : -1], refs[-1]
    pieces = [
        (
            outs[side].at[z] if len(outs) == 2 else outs[0].at[4 * side + z],
            piece_row(at_ref, z, side),
        )
        for side in range(2)
        for z in range(4)
    ]
    for g_ref, (first, units, fold, parts, *stride) in zip(grads, plan):
        if fold == 1:
            rows = units // parts
            (apart,) = stride or (rows,)

            def split(u, carry):
                for part in range(parts):
                    for ref, row in pieces:
                        ref[first + part * apart + u] = g_ref[
                            pl.ds(u * 128 + row, 16), part * 256 : part * 256 + 256
                        ].astype(BF)
                return carry

            lax.fori_loop(0, rows, split, 0)
            continue
        step = 128

        def lay(n, carry):
            for p in range(fold):
                for half in range(2):
                    lane = p * 256 + half * 128
                    flat[half, pl.ds(n * step * fold + p, step, fold)] = g_ref[
                        pl.ds(n * step, step), lane : lane + 128
                    ].astype(F32)
            return carry

        lax.fori_loop(0, g_ref.shape[0] // step, lay, 0)

        def give(u, carry):
            for ref, row in pieces:
                for half in range(2):
                    ref[first + u, :, 128 * half : 128 * (half + 1)] = flat[
                        half, pl.ds(u * 128 + row, 16)
                    ].astype(BF)
            return carry

        lax.fori_loop(0, units, give, 0)


def disassemble(at, grads, plan, one):
    vmem = pl.BlockSpec(memory_space=pltpu.VMEM)
    total = sum(entry[1] for entry in plan)
    tall = max(entry[1] if entry[2] > 1 else 1 for entry in plan)
    out = [jax.ShapeDtypeStruct((8 if one else 4, total, 16, 256), BF)] * (1 if one else 2)
    return pl.pallas_call(
        functools.partial(disassemble_kernel, plan),
        in_specs=[pl.BlockSpec(memory_space=pltpu.SMEM)] + [vmem] * len(grads),
        out_specs=[vmem] * len(out),
        out_shape=out,
        scratch_shapes=[pltpu.VMEM((2, tall * 128, 128), F32)],
        compiler_params=pltpu.CompilerParams(vmem_limit_bytes=48 << 20),
        cost_estimate=pl.CostEstimate(
            flops=0, bytes_accessed=6 * total * 128 * 256, transcendentals=0
        ),
        name="disassemble",
    )(at, *grads)


def adam_update(weights, grads, moment_one, moment_two, rate, decay):
    new_one = beta_first * moment_one + (1.0 - beta_first) * grads
    new_two = beta_second * moment_two + (1.0 - beta_second) * grads * grads
    corrected_one = new_one / (1.0 - beta_first**STEP)
    corrected_two = new_two / (1.0 - beta_second**STEP)
    new_weights = weights - rate * (
        corrected_one / (jnp.sqrt(corrected_two) + adam_epsilon) + decay * weights
    )
    return (new_weights, new_one, new_two)


def pack_kernel(masters_ref, out_ref, flat):
    slots = masters_ref.shape[0]
    for c in range(32):
        for part in range(8):
            place = (c // 16) * TP + part // 2
            flat[part % 2, pl.ds(place * slots * 16 + c % 16, slots, 16)] = masters_ref[
                :, c * 1024 + part * 128 : c * 1024 + part * 128 + 128
            ]
    for place in range(8):
        for side in range(2):
            out_ref[place, :, side * 128 : side * 128 + 128] = flat[
                side, place * slots * 16 : (place + 1) * slots * 16
            ].astype(BF)


def pack(masters):
    slots, piece = masters.shape
    return pl.pallas_call(
        pack_kernel,
        grid=(slots // 8,),
        in_specs=[pl.BlockSpec((8, piece), lambda i: (i, 0))],
        out_specs=pl.BlockSpec((8, 128, 256), lambda i: (0, i, 0)),
        out_shape=jax.ShapeDtypeStruct((8, slots * 16, 256), BF),
        scratch_shapes=[pltpu.VMEM((2, 1024, 128), F32)],
        compiler_params=pltpu.CompilerParams(vmem_limit_bytes=60 << 20),
        cost_estimate=pl.CostEstimate(
            flops=0, bytes_accessed=6 * slots * piece, transcendentals=0
        ),
        name="pack",
    )(masters)


def select_kernel(picks, table_ref, from_ref, *outs):
    for out_ref, blocks in zip(outs, picks):
        for n, block in enumerate(blocks):
            out_ref[n] = from_ref[pl.ds(pl.multiple_of(table_ref[block] * 16, 16), 16)]


def select(table, received, picks):
    vmem = pl.BlockSpec(memory_space=pltpu.VMEM)
    rows = received.shape[0]
    return pl.pallas_call(
        functools.partial(select_kernel, picks),
        in_specs=[pl.BlockSpec(memory_space=pltpu.SMEM), vmem],
        out_specs=[vmem] * len(picks),
        out_shape=[jax.ShapeDtypeStruct((len(p), 16, 256), BF) for p in picks],
        compiler_params=pltpu.CompilerParams(vmem_limit_bytes=60 << 20),
        cost_estimate=pl.CostEstimate(flops=0, bytes_accessed=rows * 900, transcendentals=0),
        name="select",
    )(table, received)


def place_kernel(takes, table_ref, turn_ref, extra_ref, *refs):
    ins, out_ref = refs[:-1], refs[-1]
    slots = out_ref.shape[1] // 16 - 1
    out_ref[...] = jnp.zeros_like(out_ref)
    for place in range(out_ref.shape[0]):
        out_ref[place, slots * 16 :] = extra_ref[place]
    for ref, take in zip(ins, takes):
        for n, (block, turn) in enumerate(take):
            if turn is not None:
                block = block + 2 * (turn_ref[0] ^ turn)
            slot = table_ref[block]
            out_ref[slot // slots, pl.ds(pl.multiple_of(slot % slots * 16, 16), 16)] = ref[n]


def place_blocks(table, turn, extra, ins, takes, slots):
    vmem = pl.BlockSpec(memory_space=pltpu.VMEM)
    smem = pl.BlockSpec(memory_space=pltpu.SMEM)
    return pl.pallas_call(
        functools.partial(place_kernel, takes),
        in_specs=[smem, smem, vmem] + [vmem] * len(ins),
        out_specs=vmem,
        out_shape=jax.ShapeDtypeStruct((8, slots * 16 + 16, 256), BF),
        compiler_params=pltpu.CompilerParams(vmem_limit_bytes=60 << 20),
        cost_estimate=pl.CostEstimate(flops=0, bytes_accessed=4 << 20, transcendentals=0),
        name="place",
    )(table, turn, extra, *ins)


def adam_kernel(from_ref, w_ref, one_ref, two_ref, w_out, one_out, two_out, low_out, flat):
    slots = w_ref.shape[0]
    part = pl.program_id(1)

    @pl.when(part == 0)
    def _():
        for place in range(8):
            for side in range(2):
                flat[side, place * slots * 16 : (place + 1) * slots * 16] = from_ref[
                    place, :, side * 128 : side * 128 + 128
                ].astype(F32)

    for c in range(8):
        for lane in range(8):
            at = slice(c * 1024 + lane * 128, c * 1024 + lane * 128 + 128)
            row = ((part // 2) * TP + lane // 2) * slots * 16 + (part % 2) * 8 + c
            grads = flat[lane % 2, pl.ds(row, slots, 16)]
            new, one, two = adam_update(
                w_ref[:, at], grads, one_ref[:, at], two_ref[:, at], learn_rate, decay_rate
            )
            w_out[:, at] = new
            one_out[:, at] = one
            two_out[:, at] = two
            low_out[:, at] = new.astype(BF)


def adam(received, masters, first_moment, second_moment):
    slots, piece = masters.shape
    block = pl.BlockSpec((16, piece // 4), lambda i, j: (i, j))
    whole = jax.ShapeDtypeStruct(masters.shape, F32)
    return pl.pallas_call(
        adam_kernel,
        grid=(slots // 16, 4),
        in_specs=[pl.BlockSpec((8, 256, 256), lambda i, j: (0, i, 0))] + [block] * 3,
        out_specs=[block] * 4,
        out_shape=[whole, whole, whole, jax.ShapeDtypeStruct(masters.shape, BF)],
        scratch_shapes=[pltpu.VMEM((2, 2048, 128), F32)],
        compiler_params=pltpu.CompilerParams(vmem_limit_bytes=60 << 20),
        cost_estimate=pl.CostEstimate(
            flops=20 * slots * piece, bytes_accessed=28 * slots * piece, transcendentals=0
        ),
        name="adam",
    )(received, masters, first_moment, second_moment)


@functools.lru_cache(maxsize=None)
def row_moves(n_seq, rows_here, length):
    local = length // n_seq
    per_dev = rows_here * local
    edges = {}
    for t in range(TP):
        for z in range(n_seq):
            for k in range(rows_here):
                row = rows_here * t + k
                token = (row // n_seq) * length + z * local
                target = (token // per_dev) * n_seq + row % n_seq
                edges.setdefault(t * n_seq + z, []).append((target, k, token % per_dev // local))
    steps = []
    for _ in range(rows_here):
        taken = {}

        def place(source, seen):
            for edge in edges[source]:
                if edge[0] not in seen:
                    seen.add(edge[0])
                    if edge[0] not in taken or place(taken[edge[0]][0], seen):
                        taken[edge[0]] = (source, edge)
                        return True
            return False

        for source in edges:
            assert place(source, set())
        pick = np.zeros(TP * n_seq, np.int32)
        put = np.zeros(TP * n_seq, np.int32)
        pairs = []
        for target, (source, edge) in taken.items():
            edges[source].remove(edge)
            pick[source] = edge[1]
            put[target] = edge[2]
            pairs.append((source, target))
        steps.append((sorted(pairs), pick, put))
    return steps


def body(
    tokens,
    cotangent,
    lengths,
    owners,
    masters,
    first_moment,
    second_moment,
    small_params,
    small_first,
    small_second,
):
    n_g = lax.axis_size("g")
    n_seq = lax.axis_size("seq")
    n_dp = n_g * TP
    capacity, piece = masters.shape
    n_blocks = owners.shape[0]
    rows_here, local, width = tokens.shape
    length = local * n_seq
    per_dev = rows_here * local
    group_rows = TP * per_dev // length
    cols = width // TP
    chunks = piece // width // n_g
    place_dp = lax.axis_index(DP)
    place_z = lax.axis_index("seq")
    t = place_dp % TP
    g = place_dp // TP
    core, side = t % 2, t // 2

    def swap(value, bit):
        return lax.ppermute(value, DP, [(i, i ^ bit) for i in range(n_dp)])

    pieces = n_seq == 4 and n_g == 2 and chunks == 16 and cols == 256 and capacity % 16 == 0
    at_hops = jnp.stack([g, place_z, -1]).astype(jnp.int32)
    at_near = jnp.stack([g, 0, 1]).astype(jnp.int32)
    at_all = jnp.array([0, 0, 1], jnp.int32)
    tie = lax.optimization_barrier
    n_all = n_dp * n_seq

    def to_all(value):
        return lax.all_to_all(
            value, ALL, split_axis=0, concat_axis=0, tiled=True
        )

    def order(first, second, flag):
        return jnp.concatenate(
            [jnp.where(flag == 0, first, second), jnp.where(flag == 0, second, first)], axis=0
        )

    steps = row_moves(n_seq, rows_here, length)

    def row_pairs(pairs, back):
        out = []
        for source, target in pairs:
            for a in range(n_g):
                ends = (a * TP * n_seq + source, a * TP * n_seq + target)
                out.append(ends[::-1] if back else ends)
        return out

    me = t * n_seq + place_z

    def to_rows(value):
        parts = []
        for pairs, pick, _ in steps:
            send = lax.dynamic_index_in_dim(value, jnp.asarray(pick)[me], 1, keepdims=False)
            parts.append(lax.ppermute(send, ALL, row_pairs(pairs, False)))
        puts = [jnp.asarray(put)[me] for _, _, put in steps]
        slots = []
        for s in range(rows_here):
            out = parts[0]
            for j in range(1, rows_here):
                out = jnp.where(puts[j] == s, parts[j], out)
            slots.append(out)
        return jnp.concatenate(slots, axis=1)

    def from_rows(value):
        value = value.reshape(rows_here, local, width)
        parts = []
        for pairs, _, put in steps:
            send = lax.dynamic_index_in_dim(value, jnp.asarray(put)[me], 0, keepdims=False)
            parts.append(lax.ppermute(send, ALL, row_pairs(pairs, True)))
        picks = [jnp.asarray(pick)[me] for _, pick, _ in steps]
        slots = []
        for s in range(rows_here):
            out = parts[0]
            for j in range(1, rows_here):
                out = jnp.where(picks[j] == s, parts[j], out)
            slots.append(out)
        return jnp.stack(slots, axis=0)

    block_index = jnp.arange(n_blocks, dtype=jnp.int32)
    same_owner = owners[:, None] == owners[None, :]
    earlier = block_index[None, :] < block_index[:, None]
    slot_rank = jnp.sum((same_owner & earlier).astype(jnp.int32), axis=1)
    slot_of_block = owners * capacity + slot_rank
    slot_ids = jnp.arange(n_dp * capacity, dtype=jnp.int32)
    hit = slot_of_block[None, :] == slot_ids[:, None]
    block_of_slot = jnp.sum(jnp.where(hit, block_index[None, :], 0), axis=1) + jnp.where(
        jnp.any(hit, axis=1), 0, n_blocks
    )

    if pieces:
        packed = pack(masters)
    else:
        packed = masters.astype(BF).reshape(capacity, n_g, chunks, TP, cols)
        packed = packed.transpose(1, 3, 0, 2, 4).reshape(n_dp, capacity * chunks, cols)
    small_here = small_params.shape[0]
    small_width = -(-(small_here + 2 * lengths.size) // 512) * 512
    note = jnp.concatenate(
        [
            small_params.astype(BF),
            (lengths.reshape(-1) // 32).astype(BF),
            (lengths.reshape(-1) % 32).astype(BF),
        ]
    )
    note = jnp.pad(note, (0, small_width - note.shape[0]))
    tokens, packed = tie((tokens, packed))
    token_rows = to_rows(tokens[None])[0]
    received = lax.all_to_all(packed, DP, split_axis=0, concat_axis=0, tiled=True)
    note, received, token_rows = tie((note, received, token_rows))
    notes = to_all(jnp.broadcast_to(note[None], (n_all, small_width)))

    unit_rows = n_seq * n_g * chunks
    n_qkv = 3 * width // unit_rows
    n_out = width // unit_rows
    n_in = FF // unit_rows
    per_layer = n_qkv + n_out + 2 * n_in
    my_out = n_out // TP
    fold = FF // width

    def turn(value):
        mine = [lax.dynamic_index_in_dim(value, t ^ k, 0, keepdims=False) for k in range(TP)]
        return [mine[0]] + [swap(mine[k], k) for k in range(1, TP)]

    def spread(value):
        return lax.all_gather(value, ("g", "seq"), axis=0)

    def build_hops(hops, plan):
        if not pieces:
            return build(hops, plan)
        own, along = hops
        ins = [own, *along, swap(own, TP), swap(jnp.stack(along), TP)]
        sources = [(by, None, by, 0) for by in range(n_seq)]
        sources += [(n_seq, None, 0, 1)]
        sources += [(n_seq + 1, by - 1, by, 1) for by in range(1, n_seq)]
        return assemble(at_hops, ins, sources, plan)

    def build(every, plan):
        if pieces:
            sources = [(0, a * n_seq + z, z, a) for a in range(n_g) for z in range(n_seq)]
            return assemble(at_all, [every], sources, plan)
        out = []
        for first, units, fold, parts in plan:
            rows = units // parts
            part = every[:, first : first + units]
            part = part.reshape(n_g, n_seq, parts, rows, chunks, cols).transpose(3, 1, 0, 4, 2, 5)
            out.append(part.reshape(rows * unit_rows // fold, parts * cols * fold))
        return out

    my_units = (1 + fold) * my_out
    n_both = TP * my_units

    def parts_of(layer):
        start = layer * per_layer
        qkv = list(range(start, start + n_qkv))
        inner = list(range(start + n_qkv + n_out, start + n_qkv + n_out + n_in))
        turned = []
        for a in range(TP):
            turned.append([start + n_qkv + my_out * a + e for e in range(my_out)])
            for q in range(fold):
                down = start + n_qkv + n_out + n_in + (q * TP + a) * my_out
                turned[a] += [down + e for e in range(my_out)]
        return qkv, inner, turned

    qkv0, in0, turned0 = parts_of(0)
    qkv1, in1, turned1 = parts_of(1)
    turned = [b for a in range(TP) for b in turned0[a] + turned1[a]]
    picks = [qkv0, in0, turned, qkv1 + in1]
    if pieces:
        m_qkv0, m_in0, swapped, m_rest1 = select(
            slot_of_block, received.reshape(n_dp * capacity * chunks, cols), picks
        )
    else:
        blocks = received.reshape(n_dp * capacity, chunks, cols)[slot_of_block]
        m_qkv0, m_in0, swapped, m_rest1 = [blocks[jnp.array(p)] for p in picks]
    swapped = swapped.reshape(TP, 2 * my_units, chunks, cols)
    plan_qkv = (0, n_qkv, 3, 1)
    plan_both = (0, n_both, 1, TP)
    def hop_z(value):
        return [
            lax.ppermute(value, "seq", [(i, (i + by) % n_seq) for i in range(n_seq)])
            for by in range(1, n_seq)
        ]

    m_qkv0, swapped, notes = tie((m_qkv0, swapped, notes))
    z_qkv0 = (m_qkv0, hop_z(m_qkv0)) if pieces else spread(m_qkv0)
    swapped = jnp.stack(turn(swapped))[jnp.arange(TP) ^ t]
    m_both0 = swapped[:, :my_units].reshape(n_both, chunks, cols)
    m_both1 = swapped[:, my_units:].reshape(n_both, chunks, cols)
    z_rest0 = spread(jnp.concatenate([m_in0, m_both0]))
    z_rest1 = spread(jnp.concatenate([m_rest1, m_both1]))

    small_all = notes[:, :small_here].reshape(-1)
    pairs = notes[::n_seq, small_here : small_here + 2 * lengths.size].astype(jnp.int32)
    pairs = pairs.reshape(n_dp, 2, rows_here, lengths.shape[1])
    all_lengths = (pairs[:, 0] * 32 + pairs[:, 1]).reshape(n_dp * rows_here, -1)
    vectors = []
    for layer in range(LAYERS):
        base = layer * (3 * width + FF)
        small_f = small_all[base : base + 3 * width + FF].astype(F32)
        bias_in = lax.dynamic_index_in_dim(
            small_f[2 * width : 2 * width + FF].reshape(fold, TP, cols), t, 1, keepdims=False
        ).reshape(-1)
        vectors.append(
            (small_f[:width], small_f[width : 2 * width], bias_in, small_f[2 * width + FF :])
        )

    mine_rows = jnp.arange(group_rows) * n_seq + place_z
    if group_rows == 2:
        mine_rows = jnp.where(side == 0, mine_rows, mine_rows[::-1])
    row_lengths = all_lengths[g * TP * rows_here + mine_rows]
    ends = jnp.cumsum(row_lengths, axis=1)
    starts = ends - row_lengths
    places = jnp.arange(length, dtype=jnp.int32)
    segment = jnp.sum((places[None, :, None] >= ends[:, None, :]).astype(jnp.int32), axis=2)
    which = segment[:, :, None] == jnp.arange(lengths.shape[1], dtype=jnp.int32)[None, None, :]
    within = places[None, :] - jnp.sum(jnp.where(which, starts[:, None, :], 0), axis=2)
    lane = jnp.arange(128)
    feature = lane % HD
    inverse = 1.0 / 10000.0 ** (jnp.arange(0, ROT, 2, dtype=F32) / ROT)
    angle = within.astype(F32)[..., None] * jnp.tile(inverse, 128 // (ROT // 2))
    cosine, sine = jnp.cos(angle), jnp.sin(angle)
    tables = jnp.stack(
        [
            jnp.where(feature < ROT, cosine, 1.0),
            jnp.where(feature < ROT // 2, -sine, 0.0),
            jnp.where((feature >= ROT // 2) & (feature < ROT), sine, 0.0),
        ],
        axis=1,
    )
    wide = jnp.arange(cols) % HD
    hits = segment[:, :, None] == wide[None, None, :]
    q_ext = jnp.where(hits, 1.0, 0.0).astype(BF)
    k_ext = jnp.where(hits | (wide >= lengths.shape[1])[None, None, :], 0.0, -BIG).astype(BF)

    half = 2 * per_dev // 2 if group_rows == 2 else None
    flip = jnp.full((1,), core, jnp.int32)

    def gather_group(value):
        far = swap(value, 2)
        near = swap(value, 1)
        far_near = swap(far, 1)
        if group_rows == 2:
            return [jnp.concatenate([value, near]), jnp.concatenate([far, far_near])]
        own, other = order(value, near, core), order(far, far_near, core)
        return [order(own, other, side)]

    def halve(value):
        if group_rows == 2:
            keep, send = value[:per_dev], value[per_dev:]
        else:
            value = value.reshape(2, per_dev, width)
            keep = lax.dynamic_index_in_dim(value, core, 0, keepdims=False)
            send = lax.dynamic_index_in_dim(value, 1 - core, 0, keepdims=False)
        return keep + swap(send.astype(BF), 1).astype(F32)

    def scatter_pair(parts):
        if group_rows == 2:
            return parts
        pair = parts[0].reshape(2, 2 * per_dev, width)
        own = lax.dynamic_index_in_dim(pair, side, 0, keepdims=False)
        other = lax.dynamic_index_in_dim(pair, 1 - side, 0, keepdims=False)
        return own, other

    def scatter_first(part):
        return halve(part).astype(BF) if group_rows == 2 else part

    def scatter_cross(first):
        return swap(first, 2) if group_rows == 2 else first

    def scatter_rest(far, own):
        if group_rows != 2:
            own, far = scatter_pair([own])
            far = swap(halve(far).astype(BF), 2)
        return halve(own) + far.astype(F32)

    state = token_rows.astype(F32)

    def norm(state, vector):
        gain, shift = vector[0], vector[1]
        centered = state - jnp.mean(state, axis=-1, keepdims=True)
        inv_std = lax.rsqrt(jnp.mean(centered * centered, axis=-1, keepdims=True) + norm_epsilon)
        normed = centered * inv_std
        return normed, inv_std, (normed * gain + shift).astype(BF)

    def front(hiddens, w_qkv):
        return [dot(hidden, w_qkv) for hidden in hiddens]

    def attention(projs):
        return [attend(flip, half, proj, tables[r], q_ext[r], k_ext[r]) for r, proj in enumerate(projs)]

    def gelu_pair(inner):
        tanh_part = jnp.tanh(gelu_coeff * (inner + gelu_cubic * inner * inner * inner))
        active = 0.5 * inner * (1.0 + tanh_part)
        slope = 0.5 * (1.0 + tanh_part) + 0.5 * inner * (1.0 - tanh_part * tanh_part) * (
            gelu_coeff * (1.0 + 3.0 * gelu_cubic * inner * inner)
        )
        return active.astype(BF), slope.astype(BF)

    def inside(hiddens, w_in, bias_in):
        pairs = [gelu_pair(dot(hidden, w_in) + bias_in) for hidden in hiddens]
        return [slope for _, slope in pairs], [active for active, _ in pairs]

    normed0, inv_std0, hidden = norm(state, vectors[0])
    hiddens0 = gather_group(hidden)
    (w_qkv0,) = build_hops(z_qkv0, [plan_qkv])
    attended0 = attention(front(hiddens0, w_qkv0))
    w_in0, both = build(z_rest0, [(0, n_in, fold, 1), (n_in, n_both, 1, TP)])
    inners0, actives0 = inside(hiddens0, w_in0, vectors[0][2])
    w_out0, w_down0 = both[:cols], both[cols:]
    def leave(r, attended, actives, w_out, w_down):
        return dot(attended[r][0], w_out) + dot(actives[r], w_down)

    last = group_rows - 1
    first = scatter_first(leave(last, attended0, actives0, w_out0, w_down0))
    own = first
    if last:
        first, actives0 = tie((first, actives0))
        own = leave(0, attended0, actives0, w_out0, w_down0)
    cotangent, own = tie((cotangent, own))
    cotangent_rows = to_rows(cotangent[None])[0]
    state = state + scatter_rest(scatter_cross(first), own) + vectors[0][3]
    normed1, inv_std1, hidden = norm(state, vectors[1])
    hiddens1 = gather_group(hidden)
    w_qkv1, w_in1, both = build(
        z_rest1, [plan_qkv, (n_qkv, n_in, fold, 1), (n_qkv + n_in, n_both, 1, TP)]
    )
    projs = front(hiddens1, w_qkv1)
    d_branch, projs = tie((cotangent_rows, projs))
    d_branch_rows = gather_group(d_branch)
    attended1 = attention(projs)
    inners1, actives1 = inside(hiddens1, w_in1, vectors[1][2])
    w_out1, w_down1 = both[:cols], both[cols:]
    first_out = scatter_first(leave(last, attended1, actives1, w_out1, w_down1))
    own_out = leave(0, attended1, actives1, w_out1, w_down1) if last else first_out

    def lay_out(grads, plan):
        if pieces:
            return disassemble(at_all, grads, plan, True)[0]
        every = []
        for grad, (_, units, fold, parts) in zip(grads, plan):
            rows = units // parts
            grad = grad.astype(BF).reshape(rows, n_seq, n_g, chunks, parts, cols)
            grad = grad.transpose(2, 1, 4, 0, 3, 5)
            every.append(grad.reshape(n_g * n_seq, units, chunks, cols))
        return jnp.concatenate(every, axis=1)

    def sum_all(laid):
        return lax.psum_scatter(laid, ("g", "seq"), scatter_dimension=0, tiled=False)

    def lay_near(grads, plan):
        return disassemble(at_near, grads, plan, False) if pieces else lay_out(grads, plan)

    def sum_g(laid):
        if not pieces:
            return sum_all(laid)
        keep, send = laid
        return (keep.astype(F32) + swap(send, TP).astype(F32)).astype(BF)

    def sum_z(total):
        if not pieces:
            return total
        total = lax.all_to_all(total, "seq", split_axis=0, concat_axis=0, tiled=True)
        return jnp.sum(total.astype(F32), axis=0).astype(BF)

    def both_grads(d_rows, attended, actives):
        g_out = sum(dot_tn(a[0], d) for a, d in zip(attended, d_rows))
        g_down = sum(dot_tn(a, d) for a, d in zip(actives, d_rows))
        return [g_out, g_down] if pieces else [jnp.concatenate([g_out, g_down])]

    def both_plan(start):
        if not pieces:
            return [(start, n_both, 1, TP)]
        return [
            (start, TP * my_out, 1, TP, my_units),
            (start + my_out, TP * fold * my_out, 1, TP, my_units),
        ]

    def back_inner(d_row, inner, w_down):
        return (dot_nt(d_row, w_down) * inner.astype(F32)).astype(BF)

    def back_attention(r, d_row, attended, w_out):
        d_context = dot_nt(d_row, w_out).astype(BF)
        return attend_back(flip, half, attended[1], d_context, attended[2], tables[r], q_ext[r], k_ext[r])

    def back_norm(d_state, d_hidden, normed, inv_std, vector):
        d_normed = d_hidden * vector[0]
        return d_state + inv_std * (
            d_normed
            - jnp.mean(d_normed, axis=-1, keepdims=True)
            - normed * jnp.mean(d_normed * normed, axis=-1, keepdims=True)
        )

    def sums(d_hidden, normed, d_inners, d_branch):
        g_bias_in = sum(jnp.sum(d.astype(F32), axis=0) for d in d_inners)
        wide_bias = (
            (jnp.arange(TP) == t).astype(F32)[None, :, None] * g_bias_in.reshape(fold, 1, cols)
        ).reshape(-1)
        return jnp.concatenate(
            [
                jnp.sum(d_hidden * normed, axis=0),
                jnp.sum(d_hidden, axis=0),
                wide_bias,
                jnp.sum(d_branch.astype(F32), axis=0),
            ]
        )

    turns = range(group_rows)
    d_inners1, d_projs1 = [None] * group_rows, [None] * group_rows
    d_rows = d_branch_rows
    for r in turns:
        d_inners1[r] = back_inner(d_rows[r], inners1[r], w_down1)
    g_in = sum(dot_tn(hiddens1[r], d_inners1[r]) for r in turns)
    laid = lay_out(
        [g_in, *both_grads(d_rows, attended1, actives1)],
        [(0, n_in, fold, 1), *both_plan(n_in)],
    )
    laid, d_rows, d_inners1, first_out = tie((laid, d_rows, d_inners1, first_out))
    r_early1 = sum_all(laid)

    def back_part(r, d_inners, d_projs, w_in, w_qkv):
        return dot_nt(d_inners[r], w_in) + dot_nt(d_projs[r], w_qkv)

    d_projs1[last] = back_attention(last, d_rows[last], attended1[last], w_out1)
    far_out = scatter_cross(first_out)
    d_projs1[last], far_out = tie((d_projs1[last], far_out))
    first = scatter_first(back_part(last, d_inners1, d_projs1, w_in1, w_qkv1))
    outputs = (state + scatter_rest(far_out, own_out) + vectors[1][3]).astype(BF)
    own, far = first, first
    if last:
        first, d_rows, outputs = tie((first, d_rows, outputs))
        d_projs1[0] = back_attention(0, d_rows[0], attended1[0], w_out1)
        far = scatter_cross(first)
        d_projs1[0], far = tie((d_projs1[0], far))
        own = back_part(0, d_inners1, d_projs1, w_in1, w_qkv1)
    d_state = cotangent_rows.astype(F32)
    d_hidden1 = scatter_rest(far, own)
    d_state = back_norm(d_state, d_hidden1, normed1, inv_std1, vectors[1])
    d_branch = d_state.astype(BF)
    d_branch, d_projs1, outputs = tie((d_branch, d_projs1, outputs))
    outputs = from_rows(outputs)
    d_rows = gather_group(d_branch)
    g_qkv = sum(dot_tn(hiddens1[r], d_projs1[r]) for r in turns)
    laid = lay_out([g_qkv], [plan_qkv])
    d_rows[0], laid, r_early1 = tie((d_rows[0], laid, r_early1))
    r_qkv1 = sum_all(laid)
    d_inners0, d_projs0 = [None] * group_rows, [None] * group_rows
    d_inners0[0] = back_inner(d_rows[0], inners0[0], w_down0)
    d_projs0[0] = back_attention(0, d_rows[0], attended0[0], w_out0)
    d_rows, d_projs0[0], d_inners0[0] = tie((d_rows, d_projs0[0], d_inners0[0]))
    laid = lay_near(both_grads(d_rows, attended0, actives0), both_plan(0))
    d_rows, laid, outputs = tie((d_rows, laid, outputs))
    s_both0 = sum_g(laid)
    for r in turns[1:]:
        d_inners0[r] = back_inner(d_rows[r], inners0[r], w_down0)
    g_in = sum(dot_tn(hiddens0[r], d_inners0[r]) for r in turns)
    laid = lay_near([g_in], [(0, n_in, fold, 1)])
    d_rows, laid, s_both0 = tie((d_rows, laid, s_both0))
    r_both0 = sum_z(s_both0)
    s_in0 = sum_g(laid)
    for r in turns[1:]:
        d_projs0[r] = back_attention(r, d_rows[r], attended0[r], w_out0)
    g_qkv = sum(dot_tn(hiddens0[r], d_projs0[r]) for r in turns)
    laid = lay_near([g_qkv], [plan_qkv])
    d_projs0, laid, s_in0, r_both0 = tie((d_projs0, laid, s_in0, r_both0))
    s_qkv0 = sum_g(laid)
    r_in0 = sum_z(s_in0)
    first = scatter_first(back_part(last, d_inners0, d_projs0, w_in0, w_qkv0))
    own = first
    if last:
        first, d_inners0, r_in0 = tie((first, d_inners0, r_in0))
        own = back_part(0, d_inners0, d_projs0, w_in0, w_qkv0)
    s_qkv0, r_in0 = tie((s_qkv0, r_in0))
    r_qkv0 = sum_z(s_qkv0)
    own, far = tie((own, scatter_cross(first)))
    d_hidden0 = scatter_rest(far, own)
    d_hidden0, r_qkv0, r_qkv1 = tie((d_hidden0, r_qkv0, r_qkv1))
    small_grads = [
        sums(d_hidden0, normed0, d_inners0, d_branch),
        sums(d_hidden1, normed1, d_inners1, cotangent_rows),
    ]
    d_state = back_norm(d_state, d_hidden0, normed0, inv_std0, vectors[0])
    swapped = jnp.concatenate(
        [r.reshape(TP, my_units, chunks, cols) for r in (r_both0, r_early1[n_in:])], axis=1
    )
    mine = turn(swapped)
    grad_in = from_rows(d_state.astype(BF))
    small_flat = jnp.concatenate(small_grads).reshape(n_all, small_here)
    small_flat = jnp.pad(small_flat, ((0, 0), (0, small_width - small_here)))
    if pieces:
        extra = small_flat.astype(BF).reshape(n_dp, -1, cols)
        extra = jnp.pad(extra, ((0, 0), (0, 16 - extra.shape[1]), (0, 0)))
        ins = [r_qkv0, r_in0, r_qkv1, r_early1] + mine
        takes = [[(b, None) for b in blocks] for blocks in (qkv0, in0, qkv1, in1)]
        takes += [[(b, k) for b in turned0[0] + turned1[0]] for k in range(TP)]
        slots = place_blocks(
            slot_of_block, jnp.full((1,), t, jnp.int32), extra, ins, takes, capacity
        )
        owned = lax.all_to_all(slots, DP, split_axis=0, concat_axis=0, tiled=True)
        small_part = owned[:, capacity * chunks :].astype(F32).sum(axis=0)
        small_part = small_part.reshape(-1, small_width)[:n_seq]
        small_owned = lax.all_to_all(
            small_part, "seq", split_axis=0, concat_axis=0, tiled=True
        ).sum(axis=0)[:small_here]
    else:
        swapped = jnp.stack(mine)[jnp.arange(TP) ^ t]
        ordered = [r_qkv0, r_in0, swapped.reshape(-1, chunks, cols), r_qkv1, r_early1[:n_in]]
        index = np.zeros(n_blocks + 1, np.int32)
        index[np.array(qkv0 + in0 + turned + qkv1 + in1)] = np.arange(n_blocks)
        index[n_blocks] = n_blocks
        grads = jnp.concatenate(ordered + [jnp.zeros((1, chunks, cols), BF)])
        slots = grads[jnp.asarray(index)[block_of_slot]].reshape(n_dp, capacity, chunks, cols)
        owned = lax.all_to_all(slots, DP, split_axis=0, concat_axis=0, tiled=True)
        owned = owned.reshape(n_g, TP, capacity, chunks, cols)
        owned = owned.transpose(2, 0, 3, 1, 4).reshape(capacity, piece).astype(F32)
        small_owned = jnp.sum(to_all(small_flat), axis=0)[:small_here]
    if pieces:
        new_masters, new_first, new_second, new_low = adam(
            owned, masters, first_moment, second_moment
        )
    else:
        new_masters, new_first, new_second = adam_update(
            masters, owned, first_moment, second_moment, learn_rate, decay_rate
        )
        new_low = new_masters.astype(BF)
    small_new, small_first_new, small_second_new = adam_update(
        small_params, small_owned, small_first, small_second, small_rate, 0.0
    )
    return (
        outputs,
        grad_in,
        new_masters,
        new_first,
        new_second,
        new_low,
        small_new,
        small_first_new,
        small_second_new,
    )


def solution(mesh):
    n_dp, n_seq = mesh.devices.shape
    cut = Mesh(mesh.devices.reshape(n_dp // TP, 2, 2, n_seq), ALL)
    placed = (
        P(DP, "seq", None),
        P(DP, "seq", None),
        P(DP, None),
        P(),
        P(DP, "seq"),
        P(DP, "seq"),
        P(DP, "seq"),
        P(ALL),
        P(ALL),
        P(ALL),
    )
    return jax.shard_map(
        body,
        mesh=cut,
        in_specs=placed,
        out_specs=(
            P(DP, "seq", None),
            P(DP, "seq", None),
            P(DP, "seq"),
            P(DP, "seq"),
            P(DP, "seq"),
            P(DP, "seq"),
            P(ALL),
            P(ALL),
            P(ALL),
        ),
        check_vma=False,
    )
```

```python
import functools

import jax
import jax.numpy as jnp
import numpy as np
from jax import lax
from jax.experimental import pallas as pl
from jax.experimental.pallas import tpu as pltpu
from jax.sharding import Mesh
from jax.sharding import PartitionSpec as P

HEADS = 16
HD = 64
ROT = 32
FF = 4096
LAYERS = 2
STEP = 10
DP = ("g", "x", "core")
ALL = ("g", "x", "core", "seq")
TP = 4

norm_epsilon = 1e-05
gelu_coeff = 0.7978845608
gelu_cubic = 0.044715
beta_first = 0.9
beta_second = 0.999
learn_rate = 0.05
small_rate = 0.3
decay_rate = 0.1
adam_epsilon = 1e-08
BIG = 1e30
BF = jnp.bfloat16
F32 = jnp.float32


def dot(left, right):
    return jnp.dot(left, right, preferred_element_type=F32)


def dot_nt(left, right):
    return lax.dot_general(left, right, (((1,), (1,)), ((), ())), preferred_element_type=F32)


def dot_tn(left, right):
    return lax.dot_general(left, right, (((0,), (0,)), ((), ())), preferred_element_type=F32)


def rotate_lanes(x, cos_t, low_t, high_t, sign):
    halves = []
    for part in range(x.shape[1] // 128):
        v = x[:, 128 * part : 128 * (part + 1)]
        up = pltpu.roll(v, 128 - ROT // 2, 1)
        down = pltpu.roll(v, ROT // 2, 1)
        halves.append(v * cos_t + sign * (up * low_t + down * high_t))
    return jnp.concatenate(halves, axis=1)


def head_of(shape):
    return lax.broadcasted_iota(jnp.int32, shape, 1) // HD


def half_place(flip_ref, row, half):
    if half is None:
        return row
    return pl.multiple_of((row // half + flip_ref[0]) % 2 * half + row % half, 256)


def attend_kernel(
    half, flip_ref, proj_ref, tab_ref, qx_ref, kx_ref, ctx_ref, rot_ref, lse_ref, k_s, v_s, q_s
):
    length, width = ctx_ref.shape
    heads = width // HD
    blk = min(256, length)
    span = half or length
    zero = jnp.zeros((), BF)
    head = head_of((span, width))
    for start in range(0, length, span):
        here = pl.ds(half_place(flip_ref, start, half), span)
        cos_t, low_t, high_t = tab_ref[0, here], tab_ref[1, here], tab_ref[2, here]
        proj = proj_ref[start : start + span]
        q = rotate_lanes(proj[:, :width], cos_t, low_t, high_t, 1.0).astype(BF)
        k = rotate_lanes(proj[:, width : 2 * width], cos_t, low_t, high_t, 1.0).astype(BF)
        v = proj[:, 2 * width :].astype(BF)
        rot_ref[here, :width] = q
        rot_ref[here, width : 2 * width] = k
        rot_ref[here, 2 * width :] = v
        q = q * BF(HD**-0.5)
        for h in range(heads):
            ext = (h + 1) % heads
            k_s[h, here] = jnp.where(head == h, k, jnp.where(head == ext, kx_ref[here], zero))
            v_s[h, here] = jnp.where(head == h, v, zero)
            q_s[h, here] = jnp.where(head == ext, qx_ref[here], q)
    tri = lax.broadcasted_iota(jnp.int32, (blk, blk), 0) <= lax.broadcasted_iota(
        jnp.int32, (blk, blk), 1
    )
    for i in range(length // blk):
        lo, hi = i * blk, (i + 1) * blk
        total = jnp.zeros((blk, width), F32)
        for h in range(heads):
            qb = q_s[h, lo:hi]
            diag = jnp.where(tri, dot_nt(k_s[h, lo:hi], qb), -BIG)
            top = jnp.max(diag, axis=0, keepdims=True)
            if i:
                past = dot_nt(k_s[h, :lo], qb)
                top = jnp.maximum(top, jnp.max(past, axis=0, keepdims=True))
            diag = jnp.exp(diag - top)
            mass = jnp.sum(diag, axis=0, keepdims=True)
            if i:
                past = jnp.exp(past - top)
                mass = mass + jnp.sum(past, axis=0, keepdims=True)
            lse_ref[h : h + 1, lo:hi] = top + jnp.log(mass)
            inv = 1.0 / mass
            total += dot_tn((diag * inv).astype(BF), v_s[h, lo:hi])
            if i:
                total += dot_tn((past * inv).astype(BF), v_s[h, :lo])
        ctx_ref[pl.ds(half_place(flip_ref, lo, half), blk)] = total.astype(BF)


def attend_back_kernel(
    half,
    flip_ref,
    rot_ref,
    dctx_ref,
    lse_ref,
    tab_ref,
    qx_ref,
    kx_ref,
    out_ref,
    k_s,
    v_s,
    q_s,
    dk_s,
    dv_s,
    dq_s,
):
    length, width = dctx_ref.shape
    heads = width // HD
    blk = min(256, length)
    head = head_of((length, width))
    zero = jnp.zeros((), BF)
    q = rot_ref[:, :width]
    k = rot_ref[:, width : 2 * width]
    v = rot_ref[:, 2 * width :]
    scaled = q * BF(HD**-0.5)
    for h in range(heads):
        ext = (h + 1) % heads
        k_s[h] = jnp.where(head == h, k, jnp.where(head == ext, kx_ref[...], zero))
        v_s[h] = jnp.where(head == h, v, zero)
        q_s[h] = jnp.where(head == ext, qx_ref[...], scaled)
    dk_s[...] = jnp.zeros_like(dk_s)
    dv_s[...] = jnp.zeros_like(dv_s)
    head_b = head_of((blk, width))
    tri = lax.broadcasted_iota(jnp.int32, (blk, blk), 0) <= lax.broadcasted_iota(
        jnp.int32, (blk, blk), 1
    )
    for i in range(length // blk):
        lo, hi = i * blk, (i + 1) * blk
        d_all = dctx_ref[pl.ds(half_place(flip_ref, lo, half), blk)]
        q_all = rot_ref[lo:hi, :width]
        total = jnp.zeros((blk, width), F32)
        for h in range(heads):
            qb = q_s[h, lo:hi]
            d_h = jnp.where(head_b == h, d_all, zero)
            q_h = jnp.where(head_b == h, q_all, zero)
            lse = lse_ref[h : h + 1, lo:hi]
            p_d = jnp.exp(jnp.where(tri, dot_nt(k_s[h, lo:hi], qb), -BIG) - lse)
            g_d = dot_nt(v_s[h, lo:hi], d_all)
            delta = jnp.sum(p_d * g_d, axis=0, keepdims=True)
            if i:
                p_p = jnp.exp(dot_nt(k_s[h, :lo], qb) - lse)
                g_p = dot_nt(v_s[h, :lo], d_all)
                delta = delta + jnp.sum(p_p * g_p, axis=0, keepdims=True)
            s_d = (p_d * (g_d - delta)).astype(BF)
            dv_s[lo:hi] += dot(p_d.astype(BF), d_h)
            dk_s[lo:hi] += dot(s_d, q_h)
            k_d = jnp.where(head_b == h, rot_ref[lo:hi, width : 2 * width], zero)
            total += dot_tn(s_d, k_d)
            if i:
                s_p = (p_p * (g_p - delta)).astype(BF)
                dv_s[:lo] += dot(p_p.astype(BF), d_h)
                dk_s[:lo] += dot(s_p, q_h)
                k_p = jnp.where(head_of((lo, width)) == h, rot_ref[:lo, width : 2 * width], zero)
                total += dot_tn(s_p, k_p)
        dq_s[lo:hi] = total
    scale = HD**-0.5
    cos_t, low_t, high_t = tab_ref[0], tab_ref[1], tab_ref[2]
    dq = rotate_lanes((dq_s[...] * scale).astype(BF).astype(F32), cos_t, low_t, high_t, -1.0)
    dk = rotate_lanes((dk_s[...] * scale).astype(BF).astype(F32), cos_t, low_t, high_t, -1.0)
    dv = dv_s[...]
    span = half or length
    for start in range(0, length, span):
        here = pl.ds(half_place(flip_ref, start, half), span)
        for n, grad in enumerate((dq, dk, dv)):
            out_ref[here, n * width : (n + 1) * width] = grad[start : start + span].astype(BF)


def attend(flip, half, proj, tables, q_ext, k_ext):
    length, width = proj.shape[0], proj.shape[1] // 3
    heads = width // HD
    return pl.pallas_call(
        functools.partial(attend_kernel, half),
        in_specs=[pl.BlockSpec(memory_space=pltpu.SMEM)]
        + [pl.BlockSpec(memory_space=pltpu.VMEM)] * 4,
        out_shape=(
            jax.ShapeDtypeStruct((length, width), BF),
            jax.ShapeDtypeStruct((length, 3 * width), BF),
            jax.ShapeDtypeStruct((8, length), F32),
        ),
        scratch_shapes=[pltpu.VMEM((heads, length, width), BF)] * 3,
        compiler_params=pltpu.CompilerParams(vmem_limit_bytes=50 << 20),
        cost_estimate=pl.CostEstimate(
            flops=heads * length * length * width * 2,
            bytes_accessed=length * width * 24,
            transcendentals=heads * length * length // 2,
        ),
        name="attend",
    )(flip, proj, tables, q_ext, k_ext)


def attend_back(flip, half, rot, d_context, lse, tables, q_ext, k_ext):
    length, width = d_context.shape
    heads = width // HD
    return pl.pallas_call(
        functools.partial(attend_back_kernel, half),
        in_specs=[pl.BlockSpec(memory_space=pltpu.SMEM)]
        + [pl.BlockSpec(memory_space=pltpu.VMEM)] * 6,
        out_shape=jax.ShapeDtypeStruct((length, 3 * width), BF),
        scratch_shapes=[pltpu.VMEM((heads, length, width), BF)] * 3
        + [pltpu.VMEM((length, width), F32)] * 3,
        compiler_params=pltpu.CompilerParams(vmem_limit_bytes=50 << 20),
        cost_estimate=pl.CostEstimate(
            flops=heads * length * length * width * 5,
            bytes_accessed=length * width * 24,
            transcendentals=heads * length * length // 2,
        ),
        name="attend_back",
    )(flip, rot, d_context, lse, tables, q_ext, k_ext)


def piece_row(at_ref, slot, side):
    z = (at_ref[1] + at_ref[2] * slot + 4) % 4
    g = at_ref[0] if side == 0 else 1 - at_ref[0]
    return pl.multiple_of(z * 32 + g * 16, 16)


def assemble_kernel(sources, plan, at_ref, *refs):
    n_in = 1 + max(source[0] for source in sources)
    ins, outs, flat = refs[:n_in], refs[n_in:-1], refs[-1]
    pieces = [
        (ins[ref] if index is None else ins[ref].at[index], piece_row(at_ref, slot, side))
        for ref, index, slot, side in sources
    ]
    for out_ref, (first, units, fold, parts) in zip(outs, plan):
        if fold == 1:
            rows = units // parts

            def put(u, carry):
                for part in range(parts):
                    for ref, row in pieces:
                        out_ref[pl.ds(u * 128 + row, 16), part * 256 : part * 256 + 256] = ref[
                            first + part * rows + u
                        ]
                return carry

            lax.fori_loop(0, rows, put, 0)
            continue

        def lay(u, carry):
            for ref, row in pieces:
                value = ref[first + u].astype(F32)
                for half in range(2):
                    flat[half, pl.ds(u * 128 + row, 16)] = value[:, 128 * half : 128 * (half + 1)]
            return carry

        lax.fori_loop(0, units, lay, 0)
        step = 128

        def take(n, carry):
            for p in range(fold):
                for half in range(2):
                    lane = p * 256 + half * 128
                    out_ref[pl.ds(n * step, step), lane : lane + 128] = flat[
                        half, pl.ds(n * step * fold + p, step, fold)
                    ].astype(BF)
            return carry

        lax.fori_loop(0, out_ref.shape[0] // step, take, 0)


def assemble(at, ins, sources, plan):
    vmem = pl.BlockSpec(memory_space=pltpu.VMEM)
    tall = max(units if fold > 1 else 1 for _, units, fold, _ in plan)
    total = sum(units for _, units, _, _ in plan)
    return pl.pallas_call(
        functools.partial(assemble_kernel, sources, plan),
        in_specs=[pl.BlockSpec(memory_space=pltpu.SMEM)] + [vmem] * len(ins),
        out_specs=[vmem] * len(plan),
        out_shape=[
            jax.ShapeDtypeStruct((units // parts * 128 // fold, 256 * fold * parts), BF)
            for _, units, fold, parts in plan
        ],
        scratch_shapes=[pltpu.VMEM((2, tall * 128, 128), F32)],
        compiler_params=pltpu.CompilerParams(vmem_limit_bytes=48 << 20),
        cost_estimate=pl.CostEstimate(
            flops=0, bytes_accessed=4 * total * 128 * 256, transcendentals=0
        ),
        name="assemble",
    )(at, *ins)


def disassemble_kernel(plan, at_ref, *refs):
    grads, outs, flat = refs[: len(plan)], refs[len(plan) : -1], refs[-1]
    pieces = [
        (
            outs[side].at[z] if len(outs) == 2 else outs[0].at[4 * side + z],
            piece_row(at_ref, z, side),
        )
        for side in range(2)
        for z in range(4)
    ]
    for g_ref, (first, units, fold, parts, *stride) in zip(grads, plan):
        if fold == 1:
            rows = units // parts
            (apart,) = stride or (rows,)

            def split(u, carry):
                for part in range(parts):
                    for ref, row in pieces:
                        ref[first + part * apart + u] = g_ref[
                            pl.ds(u * 128 + row, 16), part * 256 : part * 256 + 256
                        ].astype(BF)
                return carry

            lax.fori_loop(0, rows, split, 0)
            continue
        step = 128

        def lay(n, carry):
            for p in range(fold):
                for half in range(2):
                    lane = p * 256 + half * 128
                    flat[half, pl.ds(n * step * fold + p, step, fold)] = g_ref[
                        pl.ds(n * step, step), lane : lane + 128
                    ].astype(F32)
            return carry

        lax.fori_loop(0, g_ref.shape[0] // step, lay, 0)

        def give(u, carry):
            for ref, row in pieces:
                for half in range(2):
                    ref[first + u, :, 128 * half : 128 * (half + 1)] = flat[
                        half, pl.ds(u * 128 + row, 16)
                    ].astype(BF)
            return carry

        lax.fori_loop(0, units, give, 0)


def disassemble(at, grads, plan, one):
    vmem = pl.BlockSpec(memory_space=pltpu.VMEM)
    total = sum(entry[1] for entry in plan)
    tall = max(entry[1] if entry[2] > 1 else 1 for entry in plan)
    out = [jax.ShapeDtypeStruct((8 if one else 4, total, 16, 256), BF)] * (1 if one else 2)
    return pl.pallas_call(
        functools.partial(disassemble_kernel, plan),
        in_specs=[pl.BlockSpec(memory_space=pltpu.SMEM)] + [vmem] * len(grads),
        out_specs=[vmem] * len(out),
        out_shape=out,
        scratch_shapes=[pltpu.VMEM((2, tall * 128, 128), F32)],
        compiler_params=pltpu.CompilerParams(vmem_limit_bytes=48 << 20),
        cost_estimate=pl.CostEstimate(
            flops=0, bytes_accessed=6 * total * 128 * 256, transcendentals=0
        ),
        name="disassemble",
    )(at, *grads)


def adam_update(weights, grads, moment_one, moment_two, rate, decay):
    new_one = beta_first * moment_one + (1.0 - beta_first) * grads
    new_two = beta_second * moment_two + (1.0 - beta_second) * grads * grads
    corrected_one = new_one / (1.0 - beta_first**STEP)
    corrected_two = new_two / (1.0 - beta_second**STEP)
    new_weights = weights - rate * (
        corrected_one / (jnp.sqrt(corrected_two) + adam_epsilon) + decay * weights
    )
    return (new_weights, new_one, new_two)


def pack_kernel(masters_ref, out_ref, flat):
    slots = masters_ref.shape[0]
    for c in range(32):
        for part in range(8):
            place = (c // 16) * TP + part // 2
            flat[part % 2, pl.ds(place * slots * 16 + c % 16, slots, 16)] = masters_ref[
                :, c * 1024 + part * 128 : c * 1024 + part * 128 + 128
            ]
    for place in range(8):
        for side in range(2):
            out_ref[place, :, side * 128 : side * 128 + 128] = flat[
                side, place * slots * 16 : (place + 1) * slots * 16
            ].astype(BF)


def pack(masters):
    slots, piece = masters.shape
    return pl.pallas_call(
        pack_kernel,
        grid=(slots // 8,),
        in_specs=[pl.BlockSpec((8, piece), lambda i: (i, 0))],
        out_specs=pl.BlockSpec((8, 128, 256), lambda i: (0, i, 0)),
        out_shape=jax.ShapeDtypeStruct((8, slots * 16, 256), BF),
        scratch_shapes=[pltpu.VMEM((2, 1024, 128), F32)],
        compiler_params=pltpu.CompilerParams(vmem_limit_bytes=60 << 20),
        cost_estimate=pl.CostEstimate(
            flops=0, bytes_accessed=6 * slots * piece, transcendentals=0
        ),
        name="pack",
    )(masters)


def select_kernel(picks, table_ref, from_ref, *outs):
    for out_ref, blocks in zip(outs, picks):
        for n, block in enumerate(blocks):
            out_ref[n] = from_ref[pl.ds(pl.multiple_of(table_ref[block] * 16, 16), 16)]


def select(table, received, picks):
    vmem = pl.BlockSpec(memory_space=pltpu.VMEM)
    rows = received.shape[0]
    return pl.pallas_call(
        functools.partial(select_kernel, picks),
        in_specs=[pl.BlockSpec(memory_space=pltpu.SMEM), vmem],
        out_specs=[vmem] * len(picks),
        out_shape=[jax.ShapeDtypeStruct((len(p), 16, 256), BF) for p in picks],
        compiler_params=pltpu.CompilerParams(vmem_limit_bytes=60 << 20),
        cost_estimate=pl.CostEstimate(flops=0, bytes_accessed=rows * 900, transcendentals=0),
        name="select",
    )(table, received)


def place_kernel(takes, table_ref, turn_ref, extra_ref, *refs):
    ins, out_ref = refs[:-1], refs[-1]
    slots = out_ref.shape[1] // 16 - 1
    out_ref[...] = jnp.zeros_like(out_ref)
    for place in range(out_ref.shape[0]):
        out_ref[place, slots * 16 :] = extra_ref[place]
    for ref, take in zip(ins, takes):
        for n, (block, turn) in enumerate(take):
            if turn is not None:
                block = block + 2 * (turn_ref[0] ^ turn)
            slot = table_ref[block]
            out_ref[slot // slots, pl.ds(pl.multiple_of(slot % slots * 16, 16), 16)] = ref[n]


def place_blocks(table, turn, extra, ins, takes, slots):
    vmem = pl.BlockSpec(memory_space=pltpu.VMEM)
    smem = pl.BlockSpec(memory_space=pltpu.SMEM)
    return pl.pallas_call(
        functools.partial(place_kernel, takes),
        in_specs=[smem, smem, vmem] + [vmem] * len(ins),
        out_specs=vmem,
        out_shape=jax.ShapeDtypeStruct((8, slots * 16 + 16, 256), BF),
        compiler_params=pltpu.CompilerParams(vmem_limit_bytes=60 << 20),
        cost_estimate=pl.CostEstimate(flops=0, bytes_accessed=4 << 20, transcendentals=0),
        name="place",
    )(table, turn, extra, *ins)


def adam_kernel(from_ref, w_ref, one_ref, two_ref, w_out, one_out, two_out, low_out, flat):
    slots = w_ref.shape[0]
    part = pl.program_id(1)

    @pl.when(part == 0)
    def _():
        for place in range(8):
            for side in range(2):
                flat[side, place * slots * 16 : (place + 1) * slots * 16] = from_ref[
                    place, :, side * 128 : side * 128 + 128
                ].astype(F32)

    for c in range(8):
        for lane in range(8):
            at = slice(c * 1024 + lane * 128, c * 1024 + lane * 128 + 128)
            row = ((part // 2) * TP + lane // 2) * slots * 16 + (part % 2) * 8 + c
            grads = flat[lane % 2, pl.ds(row, slots, 16)]
            new, one, two = adam_update(
                w_ref[:, at], grads, one_ref[:, at], two_ref[:, at], learn_rate, decay_rate
            )
            w_out[:, at] = new
            one_out[:, at] = one
            two_out[:, at] = two
            low_out[:, at] = new.astype(BF)


def adam(received, masters, first_moment, second_moment):
    slots, piece = masters.shape
    block = pl.BlockSpec((16, piece // 4), lambda i, j: (i, j))
    whole = jax.ShapeDtypeStruct(masters.shape, F32)
    return pl.pallas_call(
        adam_kernel,
        grid=(slots // 16, 4),
        in_specs=[pl.BlockSpec((8, 256, 256), lambda i, j: (0, i, 0))] + [block] * 3,
        out_specs=[block] * 4,
        out_shape=[whole, whole, whole, jax.ShapeDtypeStruct(masters.shape, BF)],
        scratch_shapes=[pltpu.VMEM((2, 2048, 128), F32)],
        compiler_params=pltpu.CompilerParams(vmem_limit_bytes=60 << 20),
        cost_estimate=pl.CostEstimate(
            flops=20 * slots * piece, bytes_accessed=28 * slots * piece, transcendentals=0
        ),
        name="adam",
    )(received, masters, first_moment, second_moment)


@functools.lru_cache(maxsize=None)
def row_moves(n_seq, rows_here, length):
    local = length // n_seq
    per_dev = rows_here * local
    edges = {}
    for t in range(TP):
        for z in range(n_seq):
            for k in range(rows_here):
                row = rows_here * t + k
                token = (row // n_seq) * length + z * local
                target = (token // per_dev) * n_seq + row % n_seq
                edges.setdefault(t * n_seq + z, []).append((target, k, token % per_dev // local))
    steps = []
    for _ in range(rows_here):
        taken = {}

        def place(source, seen):
            for edge in edges[source]:
                if edge[0] not in seen:
                    seen.add(edge[0])
                    if edge[0] not in taken or place(taken[edge[0]][0], seen):
                        taken[edge[0]] = (source, edge)
                        return True
            return False

        for source in edges:
            assert place(source, set())
        pick = np.zeros(TP * n_seq, np.int32)
        put = np.zeros(TP * n_seq, np.int32)
        pairs = []
        for target, (source, edge) in taken.items():
            edges[source].remove(edge)
            pick[source] = edge[1]
            put[target] = edge[2]
            pairs.append((source, target))
        steps.append((sorted(pairs), pick, put))
    return steps


def body(
    tokens,
    cotangent,
    lengths,
    owners,
    masters,
    first_moment,
    second_moment,
    small_params,
    small_first,
    small_second,
):
    n_g = lax.axis_size("g")
    n_seq = lax.axis_size("seq")
    n_dp = n_g * TP
    capacity, piece = masters.shape
    n_blocks = owners.shape[0]
    rows_here, local, width = tokens.shape
    length = local * n_seq
    per_dev = rows_here * local
    group_rows = TP * per_dev // length
    cols = width // TP
    chunks = piece // width // n_g
    place_dp = lax.axis_index(DP)
    place_z = lax.axis_index("seq")
    t = place_dp % TP
    g = place_dp // TP
    core, side = t % 2, t // 2

    def swap(value, bit):
        return lax.ppermute(value, DP, [(i, i ^ bit) for i in range(n_dp)])

    pieces = n_seq == 4 and n_g == 2 and chunks == 16 and cols == 256 and capacity % 16 == 0
    at_hops = jnp.stack([g, place_z, -1]).astype(jnp.int32)
    at_near = jnp.stack([g, 0, 1]).astype(jnp.int32)
    at_all = jnp.array([0, 0, 1], jnp.int32)
    tie = lax.optimization_barrier
    n_all = n_dp * n_seq

    def to_all(value):
        return lax.all_to_all(
            value, ALL, split_axis=0, concat_axis=0, tiled=True
        )

    def order(first, second, flag):
        return jnp.concatenate(
            [jnp.where(flag == 0, first, second), jnp.where(flag == 0, second, first)], axis=0
        )

    steps = row_moves(n_seq, rows_here, length)

    def row_pairs(pairs, back):
        out = []
        for source, target in pairs:
            for a in range(n_g):
                ends = (a * TP * n_seq + source, a * TP * n_seq + target)
                out.append(ends[::-1] if back else ends)
        return out

    me = t * n_seq + place_z

    def to_rows(value):
        parts = []
        for pairs, pick, _ in steps:
            send = lax.dynamic_index_in_dim(value, jnp.asarray(pick)[me], 1, keepdims=False)
            parts.append(lax.ppermute(send, ALL, row_pairs(pairs, False)))
        puts = [jnp.asarray(put)[me] for _, _, put in steps]
        slots = []
        for s in range(rows_here):
            out = parts[0]
            for j in range(1, rows_here):
                out = jnp.where(puts[j] == s, parts[j], out)
            slots.append(out)
        return jnp.concatenate(slots, axis=1)

    def from_rows(value):
        value = value.reshape(rows_here, local, width)
        parts = []
        for pairs, _, put in steps:
            send = lax.dynamic_index_in_dim(value, jnp.asarray(put)[me], 0, keepdims=False)
            parts.append(lax.ppermute(send, ALL, row_pairs(pairs, True)))
        picks = [jnp.asarray(pick)[me] for _, pick, _ in steps]
        slots = []
        for s in range(rows_here):
            out = parts[0]
            for j in range(1, rows_here):
                out = jnp.where(picks[j] == s, parts[j], out)
            slots.append(out)
        return jnp.stack(slots, axis=0)

    block_index = jnp.arange(n_blocks, dtype=jnp.int32)
    same_owner = owners[:, None] == owners[None, :]
    earlier = block_index[None, :] < block_index[:, None]
    slot_rank = jnp.sum((same_owner & earlier).astype(jnp.int32), axis=1)
    slot_of_block = owners * capacity + slot_rank
    slot_ids = jnp.arange(n_dp * capacity, dtype=jnp.int32)
    hit = slot_of_block[None, :] == slot_ids[:, None]
    block_of_slot = jnp.sum(jnp.where(hit, block_index[None, :], 0), axis=1) + jnp.where(
        jnp.any(hit, axis=1), 0, n_blocks
    )

    if pieces:
        packed = pack(masters)
    else:
        packed = masters.astype(BF).reshape(capacity, n_g, chunks, TP, cols)
        packed = packed.transpose(1, 3, 0, 2, 4).reshape(n_dp, capacity * chunks, cols)
    small_here = small_params.shape[0]
    small_width = -(-(small_here + 2 * lengths.size) // 512) * 512
    note = jnp.concatenate(
        [
            small_params.astype(BF),
            (lengths.reshape(-1) // 32).astype(BF),
            (lengths.reshape(-1) % 32).astype(BF),
        ]
    )
    note = jnp.pad(note, (0, small_width - note.shape[0]))
    tokens, packed = tie((tokens, packed))
    token_rows = to_rows(tokens[None])[0]
    received = lax.all_to_all(packed, DP, split_axis=0, concat_axis=0, tiled=True)
    note, received, token_rows = tie((note, received, token_rows))
    notes = to_all(jnp.broadcast_to(note[None], (n_all, small_width)))

    unit_rows = n_seq * n_g * chunks
    n_qkv = 3 * width // unit_rows
    n_out = width // unit_rows
    n_in = FF // unit_rows
    per_layer = n_qkv + n_out + 2 * n_in
    my_out = n_out // TP
    fold = FF // width

    def turn(value):
        mine = [lax.dynamic_index_in_dim(value, t ^ k, 0, keepdims=False) for k in range(TP)]
        return [mine[0]] + [swap(mine[k], k) for k in range(1, TP)]

    def spread(value):
        return lax.all_gather(value, ("g", "seq"), axis=0)

    def build_hops(hops, plan):
        if not pieces:
            return build(hops, plan)
        own, along = hops
        ins = [own, *along, swap(own, TP), swap(jnp.stack(along), TP)]
        sources = [(by, None, by, 0) for by in range(n_seq)]
        sources += [(n_seq, None, 0, 1)]
        sources += [(n_seq + 1, by - 1, by, 1) for by in range(1, n_seq)]
        return assemble(at_hops, ins, sources, plan)

    def build(every, plan):
        if pieces:
            sources = [(0, a * n_seq + z, z, a) for a in range(n_g) for z in range(n_seq)]
            return assemble(at_all, [every], sources, plan)
        out = []
        for first, units, fold, parts in plan:
            rows = units // parts
            part = every[:, first : first + units]
            part = part.reshape(n_g, n_seq, parts, rows, chunks, cols).transpose(3, 1, 0, 4, 2, 5)
            out.append(part.reshape(rows * unit_rows // fold, parts * cols * fold))
        return out

    my_units = (1 + fold) * my_out
    n_both = TP * my_units

    def parts_of(layer):
        start = layer * per_layer
        qkv = list(range(start, start + n_qkv))
        inner = list(range(start + n_qkv + n_out, start + n_qkv + n_out + n_in))
        turned = []
        for a in range(TP):
            turned.append([start + n_qkv + my_out * a + e for e in range(my_out)])
            for q in range(fold):
                down = start + n_qkv + n_out + n_in + (q * TP + a) * my_out
                turned[a] += [down + e for e in range(my_out)]
        return qkv, inner, turned

    qkv0, in0, turned0 = parts_of(0)
    qkv1, in1, turned1 = parts_of(1)
    turned = [b for a in range(TP) for b in turned0[a] + turned1[a]]
    picks = [qkv0, in0, turned, qkv1 + in1]
    if pieces:
        m_qkv0, m_in0, swapped, m_rest1 = select(
            slot_of_block, received.reshape(n_dp * capacity * chunks, cols), picks
        )
    else:
        blocks = received.reshape(n_dp * capacity, chunks, cols)[slot_of_block]
        m_qkv0, m_in0, swapped, m_rest1 = [blocks[jnp.array(p)] for p in picks]
    swapped = swapped.reshape(TP, 2 * my_units, chunks, cols)
    plan_qkv = (0, n_qkv, 3, 1)
    plan_both = (0, n_both, 1, TP)
    def hop_z(value):
        return [
            lax.ppermute(value, "seq", [(i, (i + by) % n_seq) for i in range(n_seq)])
            for by in range(1, n_seq)
        ]

    m_qkv0, swapped, notes = tie((m_qkv0, swapped, notes))
    z_qkv0 = (m_qkv0, hop_z(m_qkv0)) if pieces else spread(m_qkv0)
    swapped = jnp.stack(turn(swapped))[jnp.arange(TP) ^ t]
    m_both0 = swapped[:, :my_units].reshape(n_both, chunks, cols)
    m_both1 = swapped[:, my_units:].reshape(n_both, chunks, cols)
    z_rest0 = spread(jnp.concatenate([m_in0, m_both0]))
    z_rest1 = spread(jnp.concatenate([m_rest1, m_both1]))

    small_all = notes[:, :small_here].reshape(-1)
    pairs = notes[::n_seq, small_here : small_here + 2 * lengths.size].astype(jnp.int32)
    pairs = pairs.reshape(n_dp, 2, rows_here, lengths.shape[1])
    all_lengths = (pairs[:, 0] * 32 + pairs[:, 1]).reshape(n_dp * rows_here, -1)
    vectors = []
    for layer in range(LAYERS):
        base = layer * (3 * width + FF)
        small_f = small_all[base : base + 3 * width + FF].astype(F32)
        bias_in = lax.dynamic_index_in_dim(
            small_f[2 * width : 2 * width + FF].reshape(fold, TP, cols), t, 1, keepdims=False
        ).reshape(-1)
        vectors.append(
            (small_f[:width], small_f[width : 2 * width], bias_in, small_f[2 * width + FF :])
        )

    mine_rows = jnp.arange(group_rows) * n_seq + place_z
    if group_rows == 2:
        mine_rows = jnp.where(side == 0, mine_rows, mine_rows[::-1])
    row_lengths = all_lengths[g * TP * rows_here + mine_rows]
    ends = jnp.cumsum(row_lengths, axis=1)
    starts = ends - row_lengths
    places = jnp.arange(length, dtype=jnp.int32)
    segment = jnp.sum((places[None, :, None] >= ends[:, None, :]).astype(jnp.int32), axis=2)
    which = segment[:, :, None] == jnp.arange(lengths.shape[1], dtype=jnp.int32)[None, None, :]
    within = places[None, :] - jnp.sum(jnp.where(which, starts[:, None, :], 0), axis=2)
    lane = jnp.arange(128)
    feature = lane % HD
    inverse = 1.0 / 10000.0 ** (jnp.arange(0, ROT, 2, dtype=F32) / ROT)
    angle = within.astype(F32)[..., None] * jnp.tile(inverse, 128 // (ROT // 2))
    cosine, sine = jnp.cos(angle), jnp.sin(angle)
    tables = jnp.stack(
        [
            jnp.where(feature < ROT, cosine, 1.0),
            jnp.where(feature < ROT // 2, -sine, 0.0),
            jnp.where((feature >= ROT // 2) & (feature < ROT), sine, 0.0),
        ],
        axis=1,
    )
    wide = jnp.arange(cols) % HD
    hits = segment[:, :, None] == wide[None, None, :]
    q_ext = jnp.where(hits, 1.0, 0.0).astype(BF)
    k_ext = jnp.where(hits | (wide >= lengths.shape[1])[None, None, :], 0.0, -BIG).astype(BF)

    half = 2 * per_dev // 2 if group_rows == 2 else None
    flip = jnp.full((1,), core, jnp.int32)

    def gather_group(value):
        far = swap(value, 2)
        near = swap(value, 1)
        far_near = swap(far, 1)
        if group_rows == 2:
            return [jnp.concatenate([value, near]), jnp.concatenate([far, far_near])]
        own, other = order(value, near, core), order(far, far_near, core)
        return [order(own, other, side)]

    def halve(value):
        if group_rows == 2:
            keep, send = value[:per_dev], value[per_dev:]
        else:
            value = value.reshape(2, per_dev, width)
            keep = lax.dynamic_index_in_dim(value, core, 0, keepdims=False)
            send = lax.dynamic_index_in_dim(value, 1 - core, 0, keepdims=False)
        return keep + swap(send.astype(BF), 1).astype(F32)

    def scatter_pair(parts):
        if group_rows == 2:
            return parts
        pair = parts[0].reshape(2, 2 * per_dev, width)
        own = lax.dynamic_index_in_dim(pair, side, 0, keepdims=False)
        other = lax.dynamic_index_in_dim(pair, 1 - side, 0, keepdims=False)
        return own, other

    def scatter_first(part):
        return halve(part).astype(BF) if group_rows == 2 else part

    def scatter_cross(first):
        return swap(first, 2) if group_rows == 2 else first

    def scatter_rest(far, own):
        if group_rows != 2:
            own, far = scatter_pair([own])
            far = swap(halve(far).astype(BF), 2)
        return halve(own) + far.astype(F32)

    state = token_rows.astype(F32)

    def norm(state, vector):
        gain, shift = vector[0], vector[1]
        centered = state - jnp.mean(state, axis=-1, keepdims=True)
        inv_std = lax.rsqrt(jnp.mean(centered * centered, axis=-1, keepdims=True) + norm_epsilon)
        normed = centered * inv_std
        return normed, inv_std, (normed * gain + shift).astype(BF)

    def front(hiddens, w_qkv):
        return [dot(hidden, w_qkv) for hidden in hiddens]

    def attention(projs):
        return [attend(flip, half, proj, tables[r], q_ext[r], k_ext[r]) for r, proj in enumerate(projs)]

    def gelu_pair(inner):
        tanh_part = jnp.tanh(gelu_coeff * (inner + gelu_cubic * inner * inner * inner))
        active = 0.5 * inner * (1.0 + tanh_part)
        slope = 0.5 * (1.0 + tanh_part) + 0.5 * inner * (1.0 - tanh_part * tanh_part) * (
            gelu_coeff * (1.0 + 3.0 * gelu_cubic * inner * inner)
        )
        return active.astype(BF), slope.astype(BF)

    def inside(hiddens, w_in, bias_in):
        pairs = [gelu_pair(dot(hidden, w_in) + bias_in) for hidden in hiddens]
        return [slope for _, slope in pairs], [active for active, _ in pairs]

    normed0, inv_std0, hidden = norm(state, vectors[0])
    hiddens0 = gather_group(hidden)
    (w_qkv0,) = build_hops(z_qkv0, [plan_qkv])
    attended0 = attention(front(hiddens0, w_qkv0))
    w_in0, both = build(z_rest0, [(0, n_in, fold, 1), (n_in, n_both, 1, TP)])
    inners0, actives0 = inside(hiddens0, w_in0, vectors[0][2])
    w_out0, w_down0 = both[:cols], both[cols:]
    def leave(r, attended, actives, w_out, w_down):
        return dot(attended[r][0], w_out) + dot(actives[r], w_down)

    last = group_rows - 1
    first = scatter_first(leave(last, attended0, actives0, w_out0, w_down0))
    own = first
    if last:
        first, actives0 = tie((first, actives0))
        own = leave(0, attended0, actives0, w_out0, w_down0)
    cotangent, own = tie((cotangent, own))
    cotangent_rows = to_rows(cotangent[None])[0]
    state = state + scatter_rest(scatter_cross(first), own) + vectors[0][3]
    normed1, inv_std1, hidden = norm(state, vectors[1])
    hiddens1 = gather_group(hidden)
    w_qkv1, w_in1, both = build(
        z_rest1, [plan_qkv, (n_qkv, n_in, fold, 1), (n_qkv + n_in, n_both, 1, TP)]
    )
    projs = front(hiddens1, w_qkv1)
    d_branch, projs = tie((cotangent_rows, projs))
    d_branch_rows = gather_group(d_branch)
    attended1 = attention(projs)
    inners1, actives1 = inside(hiddens1, w_in1, vectors[1][2])
    w_out1, w_down1 = both[:cols], both[cols:]
    first_out = scatter_first(leave(last, attended1, actives1, w_out1, w_down1))
    own_out = leave(0, attended1, actives1, w_out1, w_down1) if last else first_out

    def lay_out(grads, plan):
        if pieces:
            return disassemble(at_all, grads, plan, True)[0]
        every = []
        for grad, (_, units, fold, parts) in zip(grads, plan):
            rows = units // parts
            grad = grad.astype(BF).reshape(rows, n_seq, n_g, chunks, parts, cols)
            grad = grad.transpose(2, 1, 4, 0, 3, 5)
            every.append(grad.reshape(n_g * n_seq, units, chunks, cols))
        return jnp.concatenate(every, axis=1)

    def sum_all(laid):
        return lax.psum_scatter(laid, ("g", "seq"), scatter_dimension=0, tiled=False)

    def lay_near(grads, plan):
        return disassemble(at_near, grads, plan, False) if pieces else lay_out(grads, plan)

    def sum_g(laid):
        if not pieces:
            return sum_all(laid)
        keep, send = laid
        return (keep.astype(F32) + swap(send, TP).astype(F32)).astype(BF)

    def sum_z(total):
        if not pieces:
            return total
        total = lax.all_to_all(total, "seq", split_axis=0, concat_axis=0, tiled=True)
        return jnp.sum(total.astype(F32), axis=0).astype(BF)

    def both_grads(d_rows, attended, actives):
        g_out = sum(dot_tn(a[0], d) for a, d in zip(attended, d_rows))
        g_down = sum(dot_tn(a, d) for a, d in zip(actives, d_rows))
        return [g_out, g_down] if pieces else [jnp.concatenate([g_out, g_down])]

    def both_plan(start):
        if not pieces:
            return [(start, n_both, 1, TP)]
        return [
            (start, TP * my_out, 1, TP, my_units),
            (start + my_out, TP * fold * my_out, 1, TP, my_units),
        ]

    def back_inner(d_row, inner, w_down):
        return (dot_nt(d_row, w_down) * inner.astype(F32)).astype(BF)

    def back_attention(r, d_row, attended, w_out):
        d_context = dot_nt(d_row, w_out).astype(BF)
        return attend_back(flip, half, attended[1], d_context, attended[2], tables[r], q_ext[r], k_ext[r])

    def back_norm(d_state, d_hidden, normed, inv_std, vector):
        d_normed = d_hidden * vector[0]
        return d_state + inv_std * (
            d_normed
            - jnp.mean(d_normed, axis=-1, keepdims=True)
            - normed * jnp.mean(d_normed * normed, axis=-1, keepdims=True)
        )

    def sums(d_hidden, normed, d_inners, d_branch):
        g_bias_in = sum(jnp.sum(d.astype(F32), axis=0) for d in d_inners)
        wide_bias = (
            (jnp.arange(TP) == t).astype(F32)[None, :, None] * g_bias_in.reshape(fold, 1, cols)
        ).reshape(-1)
        return jnp.concatenate(
            [
                jnp.sum(d_hidden * normed, axis=0),
                jnp.sum(d_hidden, axis=0),
                wide_bias,
                jnp.sum(d_branch.astype(F32), axis=0),
            ]
        )

    turns = range(group_rows)
    d_inners1, d_projs1 = [None] * group_rows, [None] * group_rows
    d_rows = d_branch_rows
    for r in turns:
        d_inners1[r] = back_inner(d_rows[r], inners1[r], w_down1)
    g_in = sum(dot_tn(hiddens1[r], d_inners1[r]) for r in turns)
    laid = lay_out(
        [g_in, *both_grads(d_rows, attended1, actives1)],
        [(0, n_in, fold, 1), *both_plan(n_in)],
    )
    laid, d_rows, d_inners1, first_out = tie((laid, d_rows, d_inners1, first_out))
    r_early1 = sum_all(laid)

    def back_part(r, d_inners, d_projs, w_in, w_qkv):
        return dot_nt(d_inners[r], w_in) + dot_nt(d_projs[r], w_qkv)

    d_projs1[last] = back_attention(last, d_rows[last], attended1[last], w_out1)
    far_out = scatter_cross(first_out)
    d_projs1[last], far_out = tie((d_projs1[last], far_out))
    first = scatter_first(back_part(last, d_inners1, d_projs1, w_in1, w_qkv1))
    outputs = (state + scatter_rest(far_out, own_out) + vectors[1][3]).astype(BF)
    own, far = first, first
    if last:
        first, d_rows, outputs = tie((first, d_rows, outputs))
        d_projs1[0] = back_attention(0, d_rows[0], attended1[0], w_out1)
        far = scatter_cross(first)
        d_projs1[0], far = tie((d_projs1[0], far))
        own = back_part(0, d_inners1, d_projs1, w_in1, w_qkv1)
    d_state = cotangent_rows.astype(F32)
    d_hidden1 = scatter_rest(far, own)
    d_state = back_norm(d_state, d_hidden1, normed1, inv_std1, vectors[1])
    d_branch = d_state.astype(BF)
    d_branch, d_projs1, outputs = tie((d_branch, d_projs1, outputs))
    if group_rows == 2:
        d_rows = [jnp.concatenate([d_branch, swap(d_branch, 1)]), swap(d_branch, 2)]
    else:
        d_rows = gather_group(d_branch)
    g_qkv = sum(dot_tn(hiddens1[r], d_projs1[r]) for r in turns)
    laid = lay_out([g_qkv], [plan_qkv])
    d_rows[0], laid, r_early1, outputs = tie((d_rows[0], laid, r_early1, outputs))
    outputs = from_rows(outputs)
    r_qkv1 = sum_all(laid)
    d_inners0, d_projs0 = [None] * group_rows, [None] * group_rows
    d_inners0[0] = back_inner(d_rows[0], inners0[0], w_down0)
    d_projs0[0] = back_attention(0, d_rows[0], attended0[0], w_out0)
    d_rows, d_projs0[0], d_inners0[0], outputs = tie(
        (d_rows, d_projs0[0], d_inners0[0], outputs)
    )
    if group_rows == 2:
        d_rows[1] = jnp.concatenate([d_rows[1], swap(d_rows[1], 1)])
    laid = lay_near(both_grads(d_rows, attended0, actives0), both_plan(0))
    d_rows, laid = tie((d_rows, laid))
    s_both0 = sum_g(laid)
    for r in turns[1:]:
        d_inners0[r] = back_inner(d_rows[r], inners0[r], w_down0)
    g_in = sum(dot_tn(hiddens0[r], d_inners0[r]) for r in turns)
    laid = lay_near([g_in], [(0, n_in, fold, 1)])
    d_rows, laid, s_both0 = tie((d_rows, laid, s_both0))
    r_both0 = sum_z(s_both0)
    s_in0 = sum_g(laid)
    for r in turns[1:]:
        d_projs0[r] = back_attention(r, d_rows[r], attended0[r], w_out0)
    g_qkv = sum(dot_tn(hiddens0[r], d_projs0[r]) for r in turns)
    laid = lay_near([g_qkv], [plan_qkv])
    d_projs0, laid, s_in0, r_both0, r_qkv1 = tie((d_projs0, laid, s_in0, r_both0, r_qkv1))
    s_qkv0 = sum_g(laid)
    r_in0 = sum_z(s_in0)
    first = scatter_first(back_part(last, d_inners0, d_projs0, w_in0, w_qkv0))
    own = first
    if last:
        first, d_inners0, r_in0 = tie((first, d_inners0, r_in0))
        own = back_part(0, d_inners0, d_projs0, w_in0, w_qkv0)
    s_qkv0, r_in0 = tie((s_qkv0, r_in0))
    r_qkv0 = sum_z(s_qkv0)
    own, far = tie((own, scatter_cross(first)))
    d_hidden0 = scatter_rest(far, own)
    d_hidden0, r_qkv0 = tie((d_hidden0, r_qkv0))
    small_grads = [
        sums(d_hidden0, normed0, d_inners0, d_branch),
        sums(d_hidden1, normed1, d_inners1, cotangent_rows),
    ]
    d_state = back_norm(d_state, d_hidden0, normed0, inv_std0, vectors[0])
    swapped = jnp.concatenate(
        [r.reshape(TP, my_units, chunks, cols) for r in (r_both0, r_early1[n_in:])], axis=1
    )
    mine = turn(swapped)
    grad_in = from_rows(d_state.astype(BF))
    small_flat = jnp.concatenate(small_grads).reshape(n_all, small_here)
    small_flat = jnp.pad(small_flat, ((0, 0), (0, small_width - small_here)))
    if pieces:
        extra = small_flat.astype(BF).reshape(n_dp, -1, cols)
        extra = jnp.pad(extra, ((0, 0), (0, 16 - extra.shape[1]), (0, 0)))
        ins = [r_qkv0, r_in0, r_qkv1, r_early1] + mine
        takes = [[(b, None) for b in blocks] for blocks in (qkv0, in0, qkv1, in1)]
        takes += [[(b, k) for b in turned0[0] + turned1[0]] for k in range(TP)]
        slots = place_blocks(
            slot_of_block, jnp.full((1,), t, jnp.int32), extra, ins, takes, capacity
        )
        owned = lax.all_to_all(slots, DP, split_axis=0, concat_axis=0, tiled=True)
        small_part = owned[:, capacity * chunks :].astype(F32).sum(axis=0)
        small_part = small_part.reshape(-1, small_width)[:n_seq]
        small_owned = lax.all_to_all(
            small_part, "seq", split_axis=0, concat_axis=0, tiled=True
        ).sum(axis=0)[:small_here]
    else:
        swapped = jnp.stack(mine)[jnp.arange(TP) ^ t]
        ordered = [r_qkv0, r_in0, swapped.reshape(-1, chunks, cols), r_qkv1, r_early1[:n_in]]
        index = np.zeros(n_blocks + 1, np.int32)
        index[np.array(qkv0 + in0 + turned + qkv1 + in1)] = np.arange(n_blocks)
        index[n_blocks] = n_blocks
        grads = jnp.concatenate(ordered + [jnp.zeros((1, chunks, cols), BF)])
        slots = grads[jnp.asarray(index)[block_of_slot]].reshape(n_dp, capacity, chunks, cols)
        owned = lax.all_to_all(slots, DP, split_axis=0, concat_axis=0, tiled=True)
        owned = owned.reshape(n_g, TP, capacity, chunks, cols)
        owned = owned.transpose(2, 0, 3, 1, 4).reshape(capacity, piece).astype(F32)
        small_owned = jnp.sum(to_all(small_flat), axis=0)[:small_here]
    if pieces:
        new_masters, new_first, new_second, new_low = adam(
            owned, masters, first_moment, second_moment
        )
    else:
        new_masters, new_first, new_second = adam_update(
            masters, owned, first_moment, second_moment, learn_rate, decay_rate
        )
        new_low = new_masters.astype(BF)
    small_new, small_first_new, small_second_new = adam_update(
        small_params, small_owned, small_first, small_second, small_rate, 0.0
    )
    return (
        outputs,
        grad_in,
        new_masters,
        new_first,
        new_second,
        new_low,
        small_new,
        small_first_new,
        small_second_new,
    )


def solution(mesh):
    n_dp, n_seq = mesh.devices.shape
    cut = Mesh(mesh.devices.reshape(n_dp // TP, 2, 2, n_seq), ALL)
    placed = (
        P(DP, "seq", None),
        P(DP, "seq", None),
        P(DP, None),
        P(),
        P(DP, "seq"),
        P(DP, "seq"),
        P(DP, "seq"),
        P(ALL),
        P(ALL),
        P(ALL),
    )
    return jax.shard_map(
        body,
        mesh=cut,
        in_specs=placed,
        out_specs=(
            P(DP, "seq", None),
            P(DP, "seq", None),
            P(DP, "seq"),
            P(DP, "seq"),
            P(DP, "seq"),
            P(DP, "seq"),
            P(ALL),
            P(ALL),
            P(ALL),
        ),
        check_vma=False,
    )
```

```python
import functools

import jax
import jax.numpy as jnp
import numpy as np
from jax import lax
from jax.experimental import pallas as pl
from jax.experimental.pallas import tpu as pltpu
from jax.sharding import Mesh
from jax.sharding import PartitionSpec as P

HEADS = 16
HD = 64
ROT = 32
FF = 4096
LAYERS = 2
STEP = 10
DP = ("g", "x", "core")
ALL = ("g", "x", "core", "seq")
TP = 4

norm_epsilon = 1e-05
gelu_coeff = 0.7978845608
gelu_cubic = 0.044715
beta_first = 0.9
beta_second = 0.999
learn_rate = 0.05
small_rate = 0.3
decay_rate = 0.1
adam_epsilon = 1e-08
BIG = 1e30
BF = jnp.bfloat16
F32 = jnp.float32


def dot(left, right):
    return jnp.dot(left, right, preferred_element_type=F32)


def dot_nt(left, right):
    return lax.dot_general(left, right, (((1,), (1,)), ((), ())), preferred_element_type=F32)


def dot_tn(left, right):
    return lax.dot_general(left, right, (((0,), (0,)), ((), ())), preferred_element_type=F32)


def rotate_lanes(x, cos_t, low_t, high_t, sign):
    halves = []
    for part in range(x.shape[1] // 128):
        v = x[:, 128 * part : 128 * (part + 1)]
        up = pltpu.roll(v, 128 - ROT // 2, 1)
        down = pltpu.roll(v, ROT // 2, 1)
        halves.append(v * cos_t + sign * (up * low_t + down * high_t))
    return jnp.concatenate(halves, axis=1)


def head_of(shape):
    return lax.broadcasted_iota(jnp.int32, shape, 1) // HD


def half_place(flip_ref, row, half):
    if half is None:
        return row
    return pl.multiple_of((row // half + flip_ref[0]) % 2 * half + row % half, 256)


def attend_kernel(
    half, flip_ref, proj_ref, tab_ref, qx_ref, kx_ref, ctx_ref, rot_ref, lse_ref, k_s, v_s, q_s
):
    length, width = ctx_ref.shape
    heads = width // HD
    blk = min(256, length)
    span = half or length
    zero = jnp.zeros((), BF)
    head = head_of((span, width))
    for start in range(0, length, span):
        here = pl.ds(half_place(flip_ref, start, half), span)
        cos_t, low_t, high_t = tab_ref[0, here], tab_ref[1, here], tab_ref[2, here]
        proj = proj_ref[start : start + span]
        q = rotate_lanes(proj[:, :width], cos_t, low_t, high_t, 1.0).astype(BF)
        k = rotate_lanes(proj[:, width : 2 * width], cos_t, low_t, high_t, 1.0).astype(BF)
        v = proj[:, 2 * width :].astype(BF)
        rot_ref[here, :width] = q
        rot_ref[here, width : 2 * width] = k
        rot_ref[here, 2 * width :] = v
        q = q * BF(HD**-0.5)
        for h in range(heads):
            ext = (h + 1) % heads
            k_s[h, here] = jnp.where(head == h, k, jnp.where(head == ext, kx_ref[here], zero))
            v_s[h, here] = jnp.where(head == h, v, zero)
            q_s[h, here] = jnp.where(head == ext, qx_ref[here], q)
    tri = lax.broadcasted_iota(jnp.int32, (blk, blk), 0) <= lax.broadcasted_iota(
        jnp.int32, (blk, blk), 1
    )
    for i in range(length // blk):
        lo, hi = i * blk, (i + 1) * blk
        total = jnp.zeros((blk, width), F32)
        for h in range(heads):
            qb = q_s[h, lo:hi]
            diag = jnp.where(tri, dot_nt(k_s[h, lo:hi], qb), -BIG)
            top = jnp.max(diag, axis=0, keepdims=True)
            if i:
                past = dot_nt(k_s[h, :lo], qb)
                top = jnp.maximum(top, jnp.max(past, axis=0, keepdims=True))
            diag = jnp.exp(diag - top)
            mass = jnp.sum(diag, axis=0, keepdims=True)
            if i:
                past = jnp.exp(past - top)
                mass = mass + jnp.sum(past, axis=0, keepdims=True)
            lse_ref[h : h + 1, lo:hi] = top + jnp.log(mass)
            inv = 1.0 / mass
            total += dot_tn((diag * inv).astype(BF), v_s[h, lo:hi])
            if i:
                total += dot_tn((past * inv).astype(BF), v_s[h, :lo])
        ctx_ref[pl.ds(half_place(flip_ref, lo, half), blk)] = total.astype(BF)


def attend_back_kernel(
    half,
    flip_ref,
    rot_ref,
    dctx_ref,
    lse_ref,
    tab_ref,
    qx_ref,
    kx_ref,
    out_ref,
    k_s,
    v_s,
    q_s,
    dk_s,
    dv_s,
    dq_s,
):
    length, width = dctx_ref.shape
    heads = width // HD
    blk = min(256, length)
    head = head_of((length, width))
    zero = jnp.zeros((), BF)
    q = rot_ref[:, :width]
    k = rot_ref[:, width : 2 * width]
    v = rot_ref[:, 2 * width :]
    scaled = q * BF(HD**-0.5)
    for h in range(heads):
        ext = (h + 1) % heads
        k_s[h] = jnp.where(head == h, k, jnp.where(head == ext, kx_ref[...], zero))
        v_s[h] = jnp.where(head == h, v, zero)
        q_s[h] = jnp.where(head == ext, qx_ref[...], scaled)
    dk_s[...] = jnp.zeros_like(dk_s)
    dv_s[...] = jnp.zeros_like(dv_s)
    head_b = head_of((blk, width))
    tri = lax.broadcasted_iota(jnp.int32, (blk, blk), 0) <= lax.broadcasted_iota(
        jnp.int32, (blk, blk), 1
    )
    for i in range(length // blk):
        lo, hi = i * blk, (i + 1) * blk
        d_all = dctx_ref[pl.ds(half_place(flip_ref, lo, half), blk)]
        q_all = rot_ref[lo:hi, :width]
        total = jnp.zeros((blk, width), F32)
        for h in range(heads):
            qb = q_s[h, lo:hi]
            d_h = jnp.where(head_b == h, d_all, zero)
            q_h = jnp.where(head_b == h, q_all, zero)
            lse = lse_ref[h : h + 1, lo:hi]
            p_d = jnp.exp(jnp.where(tri, dot_nt(k_s[h, lo:hi], qb), -BIG) - lse)
            g_d = dot_nt(v_s[h, lo:hi], d_all)
            delta = jnp.sum(p_d * g_d, axis=0, keepdims=True)
            if i:
                p_p = jnp.exp(dot_nt(k_s[h, :lo], qb) - lse)
                g_p = dot_nt(v_s[h, :lo], d_all)
                delta = delta + jnp.sum(p_p * g_p, axis=0, keepdims=True)
            s_d = (p_d * (g_d - delta)).astype(BF)
            dv_s[lo:hi] += dot(p_d.astype(BF), d_h)
            dk_s[lo:hi] += dot(s_d, q_h)
            k_d = jnp.where(head_b == h, rot_ref[lo:hi, width : 2 * width], zero)
            total += dot_tn(s_d, k_d)
            if i:
                s_p = (p_p * (g_p - delta)).astype(BF)
                dv_s[:lo] += dot(p_p.astype(BF), d_h)
                dk_s[:lo] += dot(s_p, q_h)
                k_p = jnp.where(head_of((lo, width)) == h, rot_ref[:lo, width : 2 * width], zero)
                total += dot_tn(s_p, k_p)
        dq_s[lo:hi] = total
    scale = HD**-0.5
    cos_t, low_t, high_t = tab_ref[0], tab_ref[1], tab_ref[2]
    dq = rotate_lanes((dq_s[...] * scale).astype(BF).astype(F32), cos_t, low_t, high_t, -1.0)
    dk = rotate_lanes((dk_s[...] * scale).astype(BF).astype(F32), cos_t, low_t, high_t, -1.0)
    dv = dv_s[...]
    span = half or length
    for start in range(0, length, span):
        here = pl.ds(half_place(flip_ref, start, half), span)
        for n, grad in enumerate((dq, dk, dv)):
            out_ref[here, n * width : (n + 1) * width] = grad[start : start + span].astype(BF)


def attend(flip, half, proj, tables, q_ext, k_ext):
    length, width = proj.shape[0], proj.shape[1] // 3
    heads = width // HD
    return pl.pallas_call(
        functools.partial(attend_kernel, half),
        in_specs=[pl.BlockSpec(memory_space=pltpu.SMEM)]
        + [pl.BlockSpec(memory_space=pltpu.VMEM)] * 4,
        out_shape=(
            jax.ShapeDtypeStruct((length, width), BF),
            jax.ShapeDtypeStruct((length, 3 * width), BF),
            jax.ShapeDtypeStruct((8, length), F32),
        ),
        scratch_shapes=[pltpu.VMEM((heads, length, width), BF)] * 3,
        compiler_params=pltpu.CompilerParams(vmem_limit_bytes=50 << 20),
        cost_estimate=pl.CostEstimate(
            flops=heads * length * length * width * 2,
            bytes_accessed=length * width * 24,
            transcendentals=heads * length * length // 2,
        ),
        name="attend",
    )(flip, proj, tables, q_ext, k_ext)


def attend_back(flip, half, rot, d_context, lse, tables, q_ext, k_ext):
    length, width = d_context.shape
    heads = width // HD
    return pl.pallas_call(
        functools.partial(attend_back_kernel, half),
        in_specs=[pl.BlockSpec(memory_space=pltpu.SMEM)]
        + [pl.BlockSpec(memory_space=pltpu.VMEM)] * 6,
        out_shape=jax.ShapeDtypeStruct((length, 3 * width), BF),
        scratch_shapes=[pltpu.VMEM((heads, length, width), BF)] * 3
        + [pltpu.VMEM((length, width), F32)] * 3,
        compiler_params=pltpu.CompilerParams(vmem_limit_bytes=50 << 20),
        cost_estimate=pl.CostEstimate(
            flops=heads * length * length * width * 5,
            bytes_accessed=length * width * 24,
            transcendentals=heads * length * length // 2,
        ),
        name="attend_back",
    )(flip, rot, d_context, lse, tables, q_ext, k_ext)


def piece_row(at_ref, slot, side):
    z = (at_ref[1] + at_ref[2] * slot + 4) % 4
    g = at_ref[0] if side == 0 else 1 - at_ref[0]
    return pl.multiple_of(z * 32 + g * 16, 16)


def assemble_kernel(sources, plan, at_ref, *refs):
    n_in = 1 + max(source[0] for source in sources)
    ins, outs, flat = refs[:n_in], refs[n_in:-1], refs[-1]
    pieces = [
        (ins[ref] if index is None else ins[ref].at[index], piece_row(at_ref, slot, side))
        for ref, index, slot, side in sources
    ]
    for out_ref, (first, units, fold, parts) in zip(outs, plan):
        if fold == 1:
            rows = units // parts

            def put(u, carry):
                for part in range(parts):
                    for ref, row in pieces:
                        out_ref[pl.ds(u * 128 + row, 16), part * 256 : part * 256 + 256] = ref[
                            first + part * rows + u
                        ]
                return carry

            lax.fori_loop(0, rows, put, 0)
            continue

        def lay(u, carry):
            for ref, row in pieces:
                value = ref[first + u].astype(F32)
                for half in range(2):
                    flat[half, pl.ds(u * 128 + row, 16)] = value[:, 128 * half : 128 * (half + 1)]
            return carry

        lax.fori_loop(0, units, lay, 0)
        step = 128

        def take(n, carry):
            for p in range(fold):
                for half in range(2):
                    lane = p * 256 + half * 128
                    out_ref[pl.ds(n * step, step), lane : lane + 128] = flat[
                        half, pl.ds(n * step * fold + p, step, fold)
                    ].astype(BF)
            return carry

        lax.fori_loop(0, out_ref.shape[0] // step, take, 0)


def assemble(at, ins, sources, plan):
    vmem = pl.BlockSpec(memory_space=pltpu.VMEM)
    tall = max(units if fold > 1 else 1 for _, units, fold, _ in plan)
    total = sum(units for _, units, _, _ in plan)
    return pl.pallas_call(
        functools.partial(assemble_kernel, sources, plan),
        in_specs=[pl.BlockSpec(memory_space=pltpu.SMEM)] + [vmem] * len(ins),
        out_specs=[vmem] * len(plan),
        out_shape=[
            jax.ShapeDtypeStruct((units // parts * 128 // fold, 256 * fold * parts), BF)
            for _, units, fold, parts in plan
        ],
        scratch_shapes=[pltpu.VMEM((2, tall * 128, 128), F32)],
        compiler_params=pltpu.CompilerParams(vmem_limit_bytes=48 << 20),
        cost_estimate=pl.CostEstimate(
            flops=0, bytes_accessed=4 * total * 128 * 256, transcendentals=0
        ),
        name="assemble",
    )(at, *ins)


def disassemble_kernel(plan, at_ref, *refs):
    grads, outs, flat = refs[: len(plan)], refs[len(plan) : -1], refs[-1]
    pieces = [
        (
            outs[side].at[z] if len(outs) == 2 else outs[0].at[4 * side + z],
            piece_row(at_ref, z, side),
        )
        for side in range(2)
        for z in range(4)
    ]
    for g_ref, (first, units, fold, parts, *stride) in zip(grads, plan):
        if fold == 1:
            rows = units // parts
            (apart,) = stride or (rows,)

            def split(u, carry):
                for part in range(parts):
                    for ref, row in pieces:
                        ref[first + part * apart + u] = g_ref[
                            pl.ds(u * 128 + row, 16), part * 256 : part * 256 + 256
                        ].astype(BF)
                return carry

            lax.fori_loop(0, rows, split, 0)
            continue
        step = 128

        def lay(n, carry):
            for p in range(fold):
                for half in range(2):
                    lane = p * 256 + half * 128
                    flat[half, pl.ds(n * step * fold + p, step, fold)] = g_ref[
                        pl.ds(n * step, step), lane : lane + 128
                    ].astype(F32)
            return carry

        lax.fori_loop(0, g_ref.shape[0] // step, lay, 0)

        def give(u, carry):
            for ref, row in pieces:
                for half in range(2):
                    ref[first + u, :, 128 * half : 128 * (half + 1)] = flat[
                        half, pl.ds(u * 128 + row, 16)
                    ].astype(BF)
            return carry

        lax.fori_loop(0, units, give, 0)


def disassemble(at, grads, plan, one):
    vmem = pl.BlockSpec(memory_space=pltpu.VMEM)
    total = sum(entry[1] for entry in plan)
    tall = max(entry[1] if entry[2] > 1 else 1 for entry in plan)
    out = [jax.ShapeDtypeStruct((8 if one else 4, total, 16, 256), BF)] * (1 if one else 2)
    return pl.pallas_call(
        functools.partial(disassemble_kernel, plan),
        in_specs=[pl.BlockSpec(memory_space=pltpu.SMEM)] + [vmem] * len(grads),
        out_specs=[vmem] * len(out),
        out_shape=out,
        scratch_shapes=[pltpu.VMEM((2, tall * 128, 128), F32)],
        compiler_params=pltpu.CompilerParams(vmem_limit_bytes=48 << 20),
        cost_estimate=pl.CostEstimate(
            flops=0, bytes_accessed=6 * total * 128 * 256, transcendentals=0
        ),
        name="disassemble",
    )(at, *grads)


def adam_update(weights, grads, moment_one, moment_two, rate, decay):
    new_one = beta_first * moment_one + (1.0 - beta_first) * grads
    new_two = beta_second * moment_two + (1.0 - beta_second) * grads * grads
    corrected_one = new_one / (1.0 - beta_first**STEP)
    corrected_two = new_two / (1.0 - beta_second**STEP)
    new_weights = weights - rate * (
        corrected_one / (jnp.sqrt(corrected_two) + adam_epsilon) + decay * weights
    )
    return (new_weights, new_one, new_two)


def pack_kernel(masters_ref, out_ref, flat):
    slots = masters_ref.shape[0]
    for c in range(32):
        for part in range(8):
            place = (c // 16) * TP + part // 2
            flat[part % 2, pl.ds(place * slots * 16 + c % 16, slots, 16)] = masters_ref[
                :, c * 1024 + part * 128 : c * 1024 + part * 128 + 128
            ]
    for place in range(8):
        for side in range(2):
            out_ref[place, :, side * 128 : side * 128 + 128] = flat[
                side, place * slots * 16 : (place + 1) * slots * 16
            ].astype(BF)


def pack(masters):
    slots, piece = masters.shape
    return pl.pallas_call(
        pack_kernel,
        grid=(slots // 8,),
        in_specs=[pl.BlockSpec((8, piece), lambda i: (i, 0))],
        out_specs=pl.BlockSpec((8, 128, 256), lambda i: (0, i, 0)),
        out_shape=jax.ShapeDtypeStruct((8, slots * 16, 256), BF),
        scratch_shapes=[pltpu.VMEM((2, 1024, 128), F32)],
        compiler_params=pltpu.CompilerParams(vmem_limit_bytes=60 << 20),
        cost_estimate=pl.CostEstimate(
            flops=0, bytes_accessed=6 * slots * piece, transcendentals=0
        ),
        name="pack",
    )(masters)


def select_kernel(picks, table_ref, from_ref, *outs):
    for out_ref, blocks in zip(outs, picks):
        for n, block in enumerate(blocks):
            out_ref[n] = from_ref[pl.ds(pl.multiple_of(table_ref[block] * 16, 16), 16)]


def select(table, received, picks):
    vmem = pl.BlockSpec(memory_space=pltpu.VMEM)
    rows = received.shape[0]
    return pl.pallas_call(
        functools.partial(select_kernel, picks),
        in_specs=[pl.BlockSpec(memory_space=pltpu.SMEM), vmem],
        out_specs=[vmem] * len(picks),
        out_shape=[jax.ShapeDtypeStruct((len(p), 16, 256), BF) for p in picks],
        compiler_params=pltpu.CompilerParams(vmem_limit_bytes=60 << 20),
        cost_estimate=pl.CostEstimate(flops=0, bytes_accessed=rows * 900, transcendentals=0),
        name="select",
    )(table, received)


def place_kernel(takes, table_ref, turn_ref, extra_ref, *refs):
    ins, out_ref = refs[:-1], refs[-1]
    slots = out_ref.shape[1] // 16 - 1
    out_ref[...] = jnp.zeros_like(out_ref)
    for place in range(out_ref.shape[0]):
        out_ref[place, slots * 16 :] = extra_ref[place]
    for ref, take in zip(ins, takes):
        for n, (block, turn) in enumerate(take):
            if turn is not None:
                block = block + 2 * (turn_ref[0] ^ turn)
            slot = table_ref[block]
            out_ref[slot // slots, pl.ds(pl.multiple_of(slot % slots * 16, 16), 16)] = ref[n]


def place_blocks(table, turn, extra, ins, takes, slots):
    vmem = pl.BlockSpec(memory_space=pltpu.VMEM)
    smem = pl.BlockSpec(memory_space=pltpu.SMEM)
    return pl.pallas_call(
        functools.partial(place_kernel, takes),
        in_specs=[smem, smem, vmem] + [vmem] * len(ins),
        out_specs=vmem,
        out_shape=jax.ShapeDtypeStruct((8, slots * 16 + 16, 256), BF),
        compiler_params=pltpu.CompilerParams(vmem_limit_bytes=60 << 20),
        cost_estimate=pl.CostEstimate(flops=0, bytes_accessed=4 << 20, transcendentals=0),
        name="place",
    )(table, turn, extra, *ins)


def adam_kernel(from_ref, w_ref, one_ref, two_ref, w_out, one_out, two_out, low_out, flat):
    slots = w_ref.shape[0]
    part = pl.program_id(1)

    @pl.when(part == 0)
    def _():
        for place in range(8):
            for side in range(2):
                flat[side, place * slots * 16 : (place + 1) * slots * 16] = from_ref[
                    place, :, side * 128 : side * 128 + 128
                ].astype(F32)

    for c in range(4):
        for lane in range(8):
            at = slice(c * 1024 + lane * 128, c * 1024 + lane * 128 + 128)
            row = ((part // 4) * TP + lane // 2) * slots * 16 + (part % 4) * 4 + c
            grads = flat[lane % 2, pl.ds(row, slots, 16)]
            new, one, two = adam_update(
                w_ref[:, at], grads, one_ref[:, at], two_ref[:, at], learn_rate, decay_rate
            )
            w_out[:, at] = new
            one_out[:, at] = one
            two_out[:, at] = two
            low_out[:, at] = new.astype(BF)


def adam(received, masters, first_moment, second_moment):
    slots, piece = masters.shape
    block = pl.BlockSpec((16, piece // 8), lambda i, j: (i, j))
    whole = jax.ShapeDtypeStruct(masters.shape, F32)
    return pl.pallas_call(
        adam_kernel,
        grid=(slots // 16, 8),
        in_specs=[pl.BlockSpec((8, 256, 256), lambda i, j: (0, i, 0))] + [block] * 3,
        out_specs=[block] * 4,
        out_shape=[whole, whole, whole, jax.ShapeDtypeStruct(masters.shape, BF)],
        scratch_shapes=[pltpu.VMEM((2, 2048, 128), F32)],
        compiler_params=pltpu.CompilerParams(vmem_limit_bytes=60 << 20),
        cost_estimate=pl.CostEstimate(
            flops=20 * slots * piece, bytes_accessed=28 * slots * piece, transcendentals=0
        ),
        name="adam",
    )(received, masters, first_moment, second_moment)


@functools.lru_cache(maxsize=None)
def row_moves(n_seq, rows_here, length):
    local = length // n_seq
    per_dev = rows_here * local
    edges = {}
    for t in range(TP):
        for z in range(n_seq):
            for k in range(rows_here):
                row = rows_here * t + k
                token = (row // n_seq) * length + z * local
                target = (token // per_dev) * n_seq + row % n_seq
                edges.setdefault(t * n_seq + z, []).append((target, k, token % per_dev // local))
    steps = []
    for _ in range(rows_here):
        taken = {}

        def place(source, seen):
            for edge in edges[source]:
                if edge[0] not in seen:
                    seen.add(edge[0])
                    if edge[0] not in taken or place(taken[edge[0]][0], seen):
                        taken[edge[0]] = (source, edge)
                        return True
            return False

        for source in edges:
            assert place(source, set())
        pick = np.zeros(TP * n_seq, np.int32)
        put = np.zeros(TP * n_seq, np.int32)
        pairs = []
        for target, (source, edge) in taken.items():
            edges[source].remove(edge)
            pick[source] = edge[1]
            put[target] = edge[2]
            pairs.append((source, target))
        steps.append((sorted(pairs), pick, put))
    return steps


def body(
    tokens,
    cotangent,
    lengths,
    owners,
    masters,
    first_moment,
    second_moment,
    small_params,
    small_first,
    small_second,
):
    n_g = lax.axis_size("g")
    n_seq = lax.axis_size("seq")
    n_dp = n_g * TP
    capacity, piece = masters.shape
    n_blocks = owners.shape[0]
    rows_here, local, width = tokens.shape
    length = local * n_seq
    per_dev = rows_here * local
    group_rows = TP * per_dev // length
    cols = width // TP
    chunks = piece // width // n_g
    place_dp = lax.axis_index(DP)
    place_z = lax.axis_index("seq")
    t = place_dp % TP
    g = place_dp // TP
    core, side = t % 2, t // 2

    def swap(value, bit):
        return lax.ppermute(value, DP, [(i, i ^ bit) for i in range(n_dp)])

    pieces = n_seq == 4 and n_g == 2 and chunks == 16 and cols == 256 and capacity % 16 == 0
    at_hops = jnp.stack([g, place_z, -1]).astype(jnp.int32)
    at_near = jnp.stack([g, 0, 1]).astype(jnp.int32)
    at_all = jnp.array([0, 0, 1], jnp.int32)
    tie = lax.optimization_barrier
    n_all = n_dp * n_seq

    def to_all(value):
        return lax.all_to_all(
            value, ALL, split_axis=0, concat_axis=0, tiled=True
        )

    def order(first, second, flag):
        return jnp.concatenate(
            [jnp.where(flag == 0, first, second), jnp.where(flag == 0, second, first)], axis=0
        )

    steps = row_moves(n_seq, rows_here, length)

    def row_pairs(pairs, back):
        out = []
        for source, target in pairs:
            for a in range(n_g):
                ends = (a * TP * n_seq + source, a * TP * n_seq + target)
                out.append(ends[::-1] if back else ends)
        return out

    me = t * n_seq + place_z

    def to_rows(value):
        parts = []
        for pairs, pick, _ in steps:
            send = lax.dynamic_index_in_dim(value, jnp.asarray(pick)[me], 1, keepdims=False)
            parts.append(lax.ppermute(send, ALL, row_pairs(pairs, False)))
        puts = [jnp.asarray(put)[me] for _, _, put in steps]
        slots = []
        for s in range(rows_here):
            out = parts[0]
            for j in range(1, rows_here):
                out = jnp.where(puts[j] == s, parts[j], out)
            slots.append(out)
        return jnp.concatenate(slots, axis=1)

    def from_rows(value):
        value = value.reshape(rows_here, local, width)
        parts = []
        for pairs, _, put in steps:
            send = lax.dynamic_index_in_dim(value, jnp.asarray(put)[me], 0, keepdims=False)
            parts.append(lax.ppermute(send, ALL, row_pairs(pairs, True)))
        picks = [jnp.asarray(pick)[me] for _, pick, _ in steps]
        slots = []
        for s in range(rows_here):
            out = parts[0]
            for j in range(1, rows_here):
                out = jnp.where(picks[j] == s, parts[j], out)
            slots.append(out)
        return jnp.stack(slots, axis=0)

    block_index = jnp.arange(n_blocks, dtype=jnp.int32)
    same_owner = owners[:, None] == owners[None, :]
    earlier = block_index[None, :] < block_index[:, None]
    slot_rank = jnp.sum((same_owner & earlier).astype(jnp.int32), axis=1)
    slot_of_block = owners * capacity + slot_rank
    slot_ids = jnp.arange(n_dp * capacity, dtype=jnp.int32)
    hit = slot_of_block[None, :] == slot_ids[:, None]
    block_of_slot = jnp.sum(jnp.where(hit, block_index[None, :], 0), axis=1) + jnp.where(
        jnp.any(hit, axis=1), 0, n_blocks
    )

    if pieces:
        packed = pack(masters)
    else:
        packed = masters.astype(BF).reshape(capacity, n_g, chunks, TP, cols)
        packed = packed.transpose(1, 3, 0, 2, 4).reshape(n_dp, capacity * chunks, cols)
    small_here = small_params.shape[0]
    small_width = -(-(small_here + 2 * lengths.size) // 512) * 512
    note = jnp.concatenate(
        [
            small_params.astype(BF),
            (lengths.reshape(-1) // 32).astype(BF),
            (lengths.reshape(-1) % 32).astype(BF),
        ]
    )
    note = jnp.pad(note, (0, small_width - note.shape[0]))
    tokens, packed = tie((tokens, packed))
    token_rows = to_rows(tokens[None])[0]
    received = lax.all_to_all(packed, DP, split_axis=0, concat_axis=0, tiled=True)
    note, received, token_rows = tie((note, received, token_rows))
    notes = to_all(jnp.broadcast_to(note[None], (n_all, small_width)))

    unit_rows = n_seq * n_g * chunks
    n_qkv = 3 * width // unit_rows
    n_out = width // unit_rows
    n_in = FF // unit_rows
    per_layer = n_qkv + n_out + 2 * n_in
    my_out = n_out // TP
    fold = FF // width

    def turn(value):
        mine = [lax.dynamic_index_in_dim(value, t ^ k, 0, keepdims=False) for k in range(TP)]
        return [mine[0]] + [swap(mine[k], k) for k in range(1, TP)]

    def spread(value):
        return lax.all_gather(value, ("g", "seq"), axis=0)

    def build_hops(hops, plan):
        if not pieces:
            return build(hops, plan)
        own, along = hops
        ins = [own, *along, swap(own, TP), swap(jnp.stack(along), TP)]
        sources = [(by, None, by, 0) for by in range(n_seq)]
        sources += [(n_seq, None, 0, 1)]
        sources += [(n_seq + 1, by - 1, by, 1) for by in range(1, n_seq)]
        return assemble(at_hops, ins, sources, plan)

    def build(every, plan):
        if pieces:
            sources = [(0, a * n_seq + z, z, a) for a in range(n_g) for z in range(n_seq)]
            return assemble(at_all, [every], sources, plan)
        out = []
        for first, units, fold, parts in plan:
            rows = units // parts
            part = every[:, first : first + units]
            part = part.reshape(n_g, n_seq, parts, rows, chunks, cols).transpose(3, 1, 0, 4, 2, 5)
            out.append(part.reshape(rows * unit_rows // fold, parts * cols * fold))
        return out

    my_units = (1 + fold) * my_out
    n_both = TP * my_units

    def parts_of(layer):
        start = layer * per_layer
        qkv = list(range(start, start + n_qkv))
        inner = list(range(start + n_qkv + n_out, start + n_qkv + n_out + n_in))
        turned = []
        for a in range(TP):
            turned.append([start + n_qkv + my_out * a + e for e in range(my_out)])
            for q in range(fold):
                down = start + n_qkv + n_out + n_in + (q * TP + a) * my_out
                turned[a] += [down + e for e in range(my_out)]
        return qkv, inner, turned

    qkv0, in0, turned0 = parts_of(0)
    qkv1, in1, turned1 = parts_of(1)
    turned = [b for a in range(TP) for b in turned0[a] + turned1[a]]
    picks = [qkv0, in0, turned, qkv1 + in1]
    if pieces:
        m_qkv0, m_in0, swapped, m_rest1 = select(
            slot_of_block, received.reshape(n_dp * capacity * chunks, cols), picks
        )
    else:
        blocks = received.reshape(n_dp * capacity, chunks, cols)[slot_of_block]
        m_qkv0, m_in0, swapped, m_rest1 = [blocks[jnp.array(p)] for p in picks]
    swapped = swapped.reshape(TP, 2 * my_units, chunks, cols)
    plan_qkv = (0, n_qkv, 3, 1)
    plan_both = (0, n_both, 1, TP)
    def hop_z(value):
        return [
            lax.ppermute(value, "seq", [(i, (i + by) % n_seq) for i in range(n_seq)])
            for by in range(1, n_seq)
        ]

    m_qkv0, swapped, notes = tie((m_qkv0, swapped, notes))
    z_qkv0 = (m_qkv0, hop_z(m_qkv0)) if pieces else spread(m_qkv0)
    swapped = jnp.stack(turn(swapped))[jnp.arange(TP) ^ t]
    m_both0 = swapped[:, :my_units].reshape(n_both, chunks, cols)
    m_both1 = swapped[:, my_units:].reshape(n_both, chunks, cols)
    z_rest0 = spread(jnp.concatenate([m_in0, m_both0]))
    z_rest1 = spread(jnp.concatenate([m_rest1, m_both1]))

    small_all = notes[:, :small_here].reshape(-1)
    pairs = notes[::n_seq, small_here : small_here + 2 * lengths.size].astype(jnp.int32)
    pairs = pairs.reshape(n_dp, 2, rows_here, lengths.shape[1])
    all_lengths = (pairs[:, 0] * 32 + pairs[:, 1]).reshape(n_dp * rows_here, -1)
    vectors = []
    for layer in range(LAYERS):
        base = layer * (3 * width + FF)
        small_f = small_all[base : base + 3 * width + FF].astype(F32)
        bias_in = lax.dynamic_index_in_dim(
            small_f[2 * width : 2 * width + FF].reshape(fold, TP, cols), t, 1, keepdims=False
        ).reshape(-1)
        vectors.append(
            (small_f[:width], small_f[width : 2 * width], bias_in, small_f[2 * width + FF :])
        )

    mine_rows = jnp.arange(group_rows) * n_seq + place_z
    if group_rows == 2:
        mine_rows = jnp.where(side == 0, mine_rows, mine_rows[::-1])
    row_lengths = all_lengths[g * TP * rows_here + mine_rows]
    ends = jnp.cumsum(row_lengths, axis=1)
    starts = ends - row_lengths
    places = jnp.arange(length, dtype=jnp.int32)
    segment = jnp.sum((places[None, :, None] >= ends[:, None, :]).astype(jnp.int32), axis=2)
    which = segment[:, :, None] == jnp.arange(lengths.shape[1], dtype=jnp.int32)[None, None, :]
    within = places[None, :] - jnp.sum(jnp.where(which, starts[:, None, :], 0), axis=2)
    lane = jnp.arange(128)
    feature = lane % HD
    inverse = 1.0 / 10000.0 ** (jnp.arange(0, ROT, 2, dtype=F32) / ROT)
    angle = within.astype(F32)[..., None] * jnp.tile(inverse, 128 // (ROT // 2))
    cosine, sine = jnp.cos(angle), jnp.sin(angle)
    tables = jnp.stack(
        [
            jnp.where(feature < ROT, cosine, 1.0),
            jnp.where(feature < ROT // 2, -sine, 0.0),
            jnp.where((feature >= ROT // 2) & (feature < ROT), sine, 0.0),
        ],
        axis=1,
    )
    wide = jnp.arange(cols) % HD
    hits = segment[:, :, None] == wide[None, None, :]
    q_ext = jnp.where(hits, 1.0, 0.0).astype(BF)
    k_ext = jnp.where(hits | (wide >= lengths.shape[1])[None, None, :], 0.0, -BIG).astype(BF)

    half = 2 * per_dev // 2 if group_rows == 2 else None
    flip = jnp.full((1,), core, jnp.int32)

    def gather_group(value):
        far = swap(value, 2)
        near = swap(value, 1)
        far_near = swap(far, 1)
        if group_rows == 2:
            return [jnp.concatenate([value, near]), jnp.concatenate([far, far_near])]
        own, other = order(value, near, core), order(far, far_near, core)
        return [order(own, other, side)]

    def halve(value):
        if group_rows == 2:
            keep, send = value[:per_dev], value[per_dev:]
        else:
            value = value.reshape(2, per_dev, width)
            keep = lax.dynamic_index_in_dim(value, core, 0, keepdims=False)
            send = lax.dynamic_index_in_dim(value, 1 - core, 0, keepdims=False)
        return keep + swap(send.astype(BF), 1).astype(F32)

    def scatter_pair(parts):
        if group_rows == 2:
            return parts
        pair = parts[0].reshape(2, 2 * per_dev, width)
        own = lax.dynamic_index_in_dim(pair, side, 0, keepdims=False)
        other = lax.dynamic_index_in_dim(pair, 1 - side, 0, keepdims=False)
        return own, other

    def scatter_first(part):
        return halve(part).astype(BF) if group_rows == 2 else part

    def scatter_cross(first):
        return swap(first, 2) if group_rows == 2 else first

    def scatter_rest(far, own):
        if group_rows != 2:
            own, far = scatter_pair([own])
            far = swap(halve(far).astype(BF), 2)
        return halve(own) + far.astype(F32)

    state = token_rows.astype(F32)

    def norm(state, vector):
        gain, shift = vector[0], vector[1]
        centered = state - jnp.mean(state, axis=-1, keepdims=True)
        inv_std = lax.rsqrt(jnp.mean(centered * centered, axis=-1, keepdims=True) + norm_epsilon)
        normed = centered * inv_std
        return normed, inv_std, (normed * gain + shift).astype(BF)

    def front(hiddens, w_qkv):
        return [dot(hidden, w_qkv) for hidden in hiddens]

    def attention(projs):
        return [attend(flip, half, proj, tables[r], q_ext[r], k_ext[r]) for r, proj in enumerate(projs)]

    def gelu_pair(inner):
        tanh_part = jnp.tanh(gelu_coeff * (inner + gelu_cubic * inner * inner * inner))
        active = 0.5 * inner * (1.0 + tanh_part)
        slope = 0.5 * (1.0 + tanh_part) + 0.5 * inner * (1.0 - tanh_part * tanh_part) * (
            gelu_coeff * (1.0 + 3.0 * gelu_cubic * inner * inner)
        )
        return active.astype(BF), slope.astype(BF)

    def inside(hiddens, w_in, bias_in):
        pairs = [gelu_pair(dot(hidden, w_in) + bias_in) for hidden in hiddens]
        return [slope for _, slope in pairs], [active for active, _ in pairs]

    normed0, inv_std0, hidden = norm(state, vectors[0])
    hiddens0 = gather_group(hidden)
    (w_qkv0,) = build_hops(z_qkv0, [plan_qkv])
    attended0 = attention(front(hiddens0, w_qkv0))
    w_in0, both = build(z_rest0, [(0, n_in, fold, 1), (n_in, n_both, 1, TP)])
    inners0, actives0 = inside(hiddens0, w_in0, vectors[0][2])
    w_out0, w_down0 = both[:cols], both[cols:]
    def leave(r, attended, actives, w_out, w_down):
        return dot(attended[r][0], w_out) + dot(actives[r], w_down)

    last = group_rows - 1
    first = scatter_first(leave(last, attended0, actives0, w_out0, w_down0))
    own = first
    if last:
        first, actives0 = tie((first, actives0))
        own = leave(0, attended0, actives0, w_out0, w_down0)
    cotangent, own = tie((cotangent, own))
    cotangent_rows = to_rows(cotangent[None])[0]
    state = state + scatter_rest(scatter_cross(first), own) + vectors[0][3]
    normed1, inv_std1, hidden = norm(state, vectors[1])
    hiddens1 = gather_group(hidden)
    w_qkv1, w_in1, both = build(
        z_rest1, [plan_qkv, (n_qkv, n_in, fold, 1), (n_qkv + n_in, n_both, 1, TP)]
    )
    projs = front(hiddens1, w_qkv1)
    d_branch, projs = tie((cotangent_rows, projs))
    d_branch_rows = gather_group(d_branch)
    attended1 = attention(projs)
    inners1, actives1 = inside(hiddens1, w_in1, vectors[1][2])
    w_out1, w_down1 = both[:cols], both[cols:]
    first_out = scatter_first(leave(last, attended1, actives1, w_out1, w_down1))
    own_out = leave(0, attended1, actives1, w_out1, w_down1) if last else first_out

    def lay_out(grads, plan):
        if pieces:
            return disassemble(at_all, grads, plan, True)[0]
        every = []
        for grad, (_, units, fold, parts) in zip(grads, plan):
            rows = units // parts
            grad = grad.astype(BF).reshape(rows, n_seq, n_g, chunks, parts, cols)
            grad = grad.transpose(2, 1, 4, 0, 3, 5)
            every.append(grad.reshape(n_g * n_seq, units, chunks, cols))
        return jnp.concatenate(every, axis=1)

    def sum_all(laid):
        return lax.psum_scatter(laid, ("g", "seq"), scatter_dimension=0, tiled=False)

    def lay_near(grads, plan):
        return disassemble(at_near, grads, plan, False) if pieces else lay_out(grads, plan)

    def sum_g(laid):
        if not pieces:
            return sum_all(laid)
        keep, send = laid
        return (keep.astype(F32) + swap(send, TP).astype(F32)).astype(BF)

    def sum_z(total):
        if not pieces:
            return total
        total = lax.all_to_all(total, "seq", split_axis=0, concat_axis=0, tiled=True)
        return jnp.sum(total.astype(F32), axis=0).astype(BF)

    def both_grads(d_rows, attended, actives):
        g_out = sum(dot_tn(a[0], d) for a, d in zip(attended, d_rows))
        g_down = sum(dot_tn(a, d) for a, d in zip(actives, d_rows))
        return [g_out, g_down] if pieces else [jnp.concatenate([g_out, g_down])]

    def both_plan(start):
        if not pieces:
            return [(start, n_both, 1, TP)]
        return [
            (start, TP * my_out, 1, TP, my_units),
            (start + my_out, TP * fold * my_out, 1, TP, my_units),
        ]

    def back_inner(d_row, inner, w_down):
        return (dot_nt(d_row, w_down) * inner.astype(F32)).astype(BF)

    def back_attention(r, d_row, attended, w_out):
        d_context = dot_nt(d_row, w_out).astype(BF)
        return attend_back(flip, half, attended[1], d_context, attended[2], tables[r], q_ext[r], k_ext[r])

    def back_norm(d_state, d_hidden, normed, inv_std, vector):
        d_normed = d_hidden * vector[0]
        return d_state + inv_std * (
            d_normed
            - jnp.mean(d_normed, axis=-1, keepdims=True)
            - normed * jnp.mean(d_normed * normed, axis=-1, keepdims=True)
        )

    def sums(d_hidden, normed, d_inners, d_branch):
        g_bias_in = sum(jnp.sum(d.astype(F32), axis=0) for d in d_inners)
        wide_bias = (
            (jnp.arange(TP) == t).astype(F32)[None, :, None] * g_bias_in.reshape(fold, 1, cols)
        ).reshape(-1)
        return jnp.concatenate(
            [
                jnp.sum(d_hidden * normed, axis=0),
                jnp.sum(d_hidden, axis=0),
                wide_bias,
                jnp.sum(d_branch.astype(F32), axis=0),
            ]
        )

    turns = range(group_rows)
    d_inners1, d_projs1 = [None] * group_rows, [None] * group_rows
    d_rows = d_branch_rows
    for r in turns:
        d_inners1[r] = back_inner(d_rows[r], inners1[r], w_down1)
    g_in = sum(dot_tn(hiddens1[r], d_inners1[r]) for r in turns)
    laid = lay_out(
        [g_in, *both_grads(d_rows, attended1, actives1)],
        [(0, n_in, fold, 1), *both_plan(n_in)],
    )
    laid, d_rows, d_inners1, first_out = tie((laid, d_rows, d_inners1, first_out))
    r_early1 = sum_all(laid)

    def back_part(r, d_inners, d_projs, w_in, w_qkv):
        return dot_nt(d_inners[r], w_in) + dot_nt(d_projs[r], w_qkv)

    d_projs1[last] = back_attention(last, d_rows[last], attended1[last], w_out1)
    far_out = scatter_cross(first_out)
    d_projs1[last], far_out = tie((d_projs1[last], far_out))
    first = scatter_first(back_part(last, d_inners1, d_projs1, w_in1, w_qkv1))
    outputs = (state + scatter_rest(far_out, own_out) + vectors[1][3]).astype(BF)
    own, far = first, first
    if last:
        first, d_rows, outputs = tie((first, d_rows, outputs))
        d_projs1[0] = back_attention(0, d_rows[0], attended1[0], w_out1)
        far = scatter_cross(first)
        d_projs1[0], far = tie((d_projs1[0], far))
        own = back_part(0, d_inners1, d_projs1, w_in1, w_qkv1)
    d_state = cotangent_rows.astype(F32)
    d_hidden1 = scatter_rest(far, own)
    d_state = back_norm(d_state, d_hidden1, normed1, inv_std1, vectors[1])
    d_branch = d_state.astype(BF)
    d_branch, d_projs1, outputs = tie((d_branch, d_projs1, outputs))
    if group_rows == 2:
        d_rows = [jnp.concatenate([d_branch, swap(d_branch, 1)]), swap(d_branch, 2)]
    else:
        d_rows = gather_group(d_branch)
    g_qkv = sum(dot_tn(hiddens1[r], d_projs1[r]) for r in turns)
    laid = lay_out([g_qkv], [plan_qkv])
    d_rows[0], laid, r_early1, outputs = tie((d_rows[0], laid, r_early1, outputs))
    outputs = from_rows(outputs)
    r_qkv1 = sum_all(laid)
    d_inners0, d_projs0 = [None] * group_rows, [None] * group_rows
    d_inners0[0] = back_inner(d_rows[0], inners0[0], w_down0)
    d_projs0[0] = back_attention(0, d_rows[0], attended0[0], w_out0)
    d_rows, d_projs0[0], d_inners0[0], outputs = tie(
        (d_rows, d_projs0[0], d_inners0[0], outputs)
    )
    if group_rows == 2:
        d_rows[1] = jnp.concatenate([d_rows[1], swap(d_rows[1], 1)])
    laid = lay_near(both_grads(d_rows, attended0, actives0), both_plan(0))
    d_rows, laid = tie((d_rows, laid))
    s_both0 = sum_g(laid)
    for r in turns[1:]:
        d_inners0[r] = back_inner(d_rows[r], inners0[r], w_down0)
    g_in = sum(dot_tn(hiddens0[r], d_inners0[r]) for r in turns)
    laid = lay_near([g_in], [(0, n_in, fold, 1)])
    d_rows, laid, s_both0 = tie((d_rows, laid, s_both0))
    r_both0 = sum_z(s_both0)
    s_in0 = sum_g(laid)
    for r in turns[1:]:
        d_projs0[r] = back_attention(r, d_rows[r], attended0[r], w_out0)
    g_qkv = sum(dot_tn(hiddens0[r], d_projs0[r]) for r in turns)
    laid = lay_near([g_qkv], [plan_qkv])
    d_projs0, laid, s_in0, r_both0, r_qkv1 = tie((d_projs0, laid, s_in0, r_both0, r_qkv1))
    s_qkv0 = sum_g(laid)
    r_in0 = sum_z(s_in0)
    first = scatter_first(back_part(last, d_inners0, d_projs0, w_in0, w_qkv0))
    own = first
    if last:
        first, d_inners0, r_in0 = tie((first, d_inners0, r_in0))
        own = back_part(0, d_inners0, d_projs0, w_in0, w_qkv0)
    s_qkv0, r_in0 = tie((s_qkv0, r_in0))
    r_qkv0 = sum_z(s_qkv0)
    own, far = tie((own, scatter_cross(first)))
    d_hidden0 = scatter_rest(far, own)
    d_hidden0, r_qkv0 = tie((d_hidden0, r_qkv0))
    small_grads = [
        sums(d_hidden0, normed0, d_inners0, d_branch),
        sums(d_hidden1, normed1, d_inners1, cotangent_rows),
    ]
    d_state = back_norm(d_state, d_hidden0, normed0, inv_std0, vectors[0])
    swapped = jnp.concatenate(
        [r.reshape(TP, my_units, chunks, cols) for r in (r_both0, r_early1[n_in:])], axis=1
    )
    mine = turn(swapped)
    grad_in = from_rows(d_state.astype(BF))
    small_flat = jnp.concatenate(small_grads).reshape(n_all, small_here)
    small_flat = jnp.pad(small_flat, ((0, 0), (0, small_width - small_here)))
    if pieces:
        extra = small_flat.astype(BF).reshape(n_dp, -1, cols)
        extra = jnp.pad(extra, ((0, 0), (0, 16 - extra.shape[1]), (0, 0)))
        ins = [r_qkv0, r_in0, r_qkv1, r_early1] + mine
        takes = [[(b, None) for b in blocks] for blocks in (qkv0, in0, qkv1, in1)]
        takes += [[(b, k) for b in turned0[0] + turned1[0]] for k in range(TP)]
        slots = place_blocks(
            slot_of_block, jnp.full((1,), t, jnp.int32), extra, ins, takes, capacity
        )
        owned = lax.all_to_all(slots, DP, split_axis=0, concat_axis=0, tiled=True)
        small_part = owned[:, capacity * chunks :].astype(F32).sum(axis=0)
        small_part = small_part.reshape(-1, small_width)[:n_seq]
        small_owned = lax.all_to_all(
            small_part, "seq", split_axis=0, concat_axis=0, tiled=True
        ).sum(axis=0)[:small_here]
    else:
        swapped = jnp.stack(mine)[jnp.arange(TP) ^ t]
        ordered = [r_qkv0, r_in0, swapped.reshape(-1, chunks, cols), r_qkv1, r_early1[:n_in]]
        index = np.zeros(n_blocks + 1, np.int32)
        index[np.array(qkv0 + in0 + turned + qkv1 + in1)] = np.arange(n_blocks)
        index[n_blocks] = n_blocks
        grads = jnp.concatenate(ordered + [jnp.zeros((1, chunks, cols), BF)])
        slots = grads[jnp.asarray(index)[block_of_slot]].reshape(n_dp, capacity, chunks, cols)
        owned = lax.all_to_all(slots, DP, split_axis=0, concat_axis=0, tiled=True)
        owned = owned.reshape(n_g, TP, capacity, chunks, cols)
        owned = owned.transpose(2, 0, 3, 1, 4).reshape(capacity, piece).astype(F32)
        small_owned = jnp.sum(to_all(small_flat), axis=0)[:small_here]
    if pieces:
        new_masters, new_first, new_second, new_low = adam(
            owned, masters, first_moment, second_moment
        )
    else:
        new_masters, new_first, new_second = adam_update(
            masters, owned, first_moment, second_moment, learn_rate, decay_rate
        )
        new_low = new_masters.astype(BF)
    small_new, small_first_new, small_second_new = adam_update(
        small_params, small_owned, small_first, small_second, small_rate, 0.0
    )
    return (
        outputs,
        grad_in,
        new_masters,
        new_first,
        new_second,
        new_low,
        small_new,
        small_first_new,
        small_second_new,
    )


def solution(mesh):
    n_dp, n_seq = mesh.devices.shape
    cut = Mesh(mesh.devices.reshape(n_dp // TP, 2, 2, n_seq), ALL)
    placed = (
        P(DP, "seq", None),
        P(DP, "seq", None),
        P(DP, None),
        P(),
        P(DP, "seq"),
        P(DP, "seq"),
        P(DP, "seq"),
        P(ALL),
        P(ALL),
        P(ALL),
    )
    return jax.shard_map(
        body,
        mesh=cut,
        in_specs=placed,
        out_specs=(
            P(DP, "seq", None),
            P(DP, "seq", None),
            P(DP, "seq"),
            P(DP, "seq"),
            P(DP, "seq"),
            P(DP, "seq"),
            P(ALL),
            P(ALL),
            P(ALL),
        ),
        check_vma=False,
    )
```
